512 devices in a mesh: dp: 32 (over z_hi, y, core), mp: 16 (over z_lo, x).
Axes of the slice: x: 4, y: 8, z: 8 (z_hi: 2, z_lo: 4; z = z_hi * 4 + z_lo), core: 2. Of those that a mesh axis runs over, the one named last changes fastest.
Arguments:
- teacher_in: bfloat16 [8192, 6144], P('dp', 'mp'), may hold values from -8 to 8
- teacher_gain: float32 [6144], P('mp'), may hold values from 0.5 to 1.5
- qkv_weight: bfloat16 [6144, 3, 4096], P('dp', None, 'mp'), may hold values from -5 to 5
- qk_gain: float32 [32, 128], P('mp'), may hold values from 0.5 to 5
- student_in: bfloat16 [8192, 1024], P('dp'), may hold values from -6 to 6
- student_gain: float32 [1024], replicated, may hold values from 0.25 to 1.75
- up_weight: bfloat16 [1024, 4096], P(None, 'mp'), may hold values from -0.1875 to 0.1875
- down_weight: bfloat16 [4096, 1024], P('mp'), may hold values from -0.09375 to 0.09375
- projector: bfloat16 [1024, 4096], P(None, 'mp'), may hold values from -0.1875 to 0.1875
Outputs:
- grad_up: bfloat16 [1024, 4096], P('dp', 'mp')
- grad_down: bfloat16 [4096, 1024], P('mp', 'dp')
- grad_projector: bfloat16 [1024, 4096], P('dp', 'mp')
The draws below stay inside these ranges and needn't reach their ends.
All inputs are finite; a program needn't handle non-finite values.
Results may differ from the reference program's by a relative error of at most 0.022.
Values may be sent and summed in bfloat16 or wider, within the bound.
No kernel may reach another device: no remote copies, remote signals or barrier semaphores. Data moves between devices by JAX's collectives and lax.ppermute only.
A program may use at most 64 MiB of HBM per device.

```python
import jax
import jax.numpy as jnp
from jax import lax

D = 6144
HEAD = 128
PATCH = 256
DS = 1024
SFF = 4096
TH = 32
HD = 4096
TOK_DEV = 256
IMAGES = 32
TOKENS = 8192
N_DP = 32
N_MP = 16


def common_direction(key):
    signs = jax.random.randint(jax.random.fold_in(key, 7), (D,), 0, 2)
    return signs.astype(jnp.float32) * 2.0 - 1.0


def draw_teacher_in(key, part):
    direction = common_direction(key)
    key = jax.random.fold_in(key, 11)
    key_base = jax.random.fold_in(key, 0)
    values = jax.random.normal(key_base, (TOKENS, D), jnp.float32) + direction
    return jnp.clip(values, -8.0, 8.0).astype(jnp.bfloat16)


def draw_qkv_weight(key, part):
    direction = common_direction(key)
    key = jax.random.fold_in(key, 12)
    head_pos = (jnp.arange(HD) // HEAD).astype(jnp.float32) / max(TH - 1, 1)
    values = jnp.clip(jax.random.normal(key, (D, 3, HD), jnp.float32), -3.0, 3.0)
    head_scale = 10.0 ** head_pos
    value_part = (values[:, 2, :] + 1.5 * D ** (-0.5) * direction[:, None]) * head_scale[None, :]
    values = values.at[:, 2, :].set(value_part)
    return (values * D ** (-0.5)).astype(jnp.bfloat16)


def draw_qk_gain(key, part):
    key = jax.random.fold_in(key, 13)
    key_fine = jax.random.fold_in(key, 1)
    values = jax.random.uniform(key_fine, (TH, HEAD), jnp.float32, 0.6, 1.6)
    return values


def steps_of(rng, extent, shards, smallest, high):
    def one(dim, shards_of):
        steps = jax.random.uniform(jax.random.fold_in(jax.random.fold_in(rng, 6), dim), (shards_of,), jnp.float32, smallest / len(shards), high / len(shards))
        return jnp.repeat(jnp.exp(steps), extent[dim] // shards_of).reshape((-1,) + (1,) * (len(extent) - dim - 1))

    gain = one(*shards[0])
    for cut in shards[1:]:
        gain = gain * one(*cut)
    return gain


def scatter_about(own_key, shape, deviation, most, cuts=(), kind=jnp.bfloat16):
    values = jax.random.normal(own_key, shape, jnp.float32) * deviation
    if len(cuts) > 0:
        values = steps_of(own_key, shape, cuts, -0.22, 0.18) * values
    return jnp.clip(values, min=-most, max=most).astype(kind)


def setup_inputs(seed: int = 0) -> dict:
    splits = jax.random.split(jax.random.key(seed), 10)
    return {
        "teacher_in": draw_teacher_in(jax.random.fold_in(splits[9], 71), 0),
        "teacher_gain": jnp.clip(1.0 + 0.1 * jax.random.normal(splits[1], (D,), jnp.float32), 0.5, 1.5),
        "qkv_weight": draw_qkv_weight(jax.random.fold_in(splits[9], 71), 0),
        "qk_gain": draw_qk_gain(jax.random.fold_in(splits[9], 71), 0),
        "student_in": scatter_about(splits[4], (TOKENS, DS), 1.0, 6.0, ((0, 32),)),
        "student_gain": jnp.clip(1.0 + 0.15 * jax.random.normal(splits[5], (DS,), jnp.float32), 0.25, 1.75),
        "up_weight": scatter_about(splits[6], (DS, SFF), DS ** -0.5, 0.1875, ((1, 16),)),
        "down_weight": scatter_about(splits[7], (SFF, DS), SFF ** -0.5, 0.09375, ((0, 16),)),
        "projector": scatter_about(splits[8], (DS, HD), DS ** -0.5, 0.1875, ((1, 16),)),
    }


EPSILON = 1e-06

def normalize(values):
    row_mean = lax.optimization_barrier(jnp.mean(values, axis=-1, keepdims=True))
    centered = values - row_mean
    row_var = lax.optimization_barrier(jnp.mean(centered * centered, axis=-1, keepdims=True))
    return centered * lax.rsqrt(row_var + EPSILON)

def gelu_parts(pre_act):
    cdf_part = 0.5 * (1.0 + lax.erf(pre_act * 0.7071067811865476))
    density = jnp.exp(-0.5 * pre_act * pre_act) * 0.3989422804014327
    return (pre_act * cdf_part, cdf_part + pre_act * density)

def rounded_sum(lefts, rights, form, shape):

    def step(running, pair):
        term = jnp.einsum(form, pair[0].astype(jnp.float32), pair[1].astype(jnp.float32))
        term = lax.optimization_barrier(term.astype(jnp.bfloat16))
        return (running + term.astype(jnp.float32), None)
    running, unused = lax.scan(step, jnp.zeros(shape, jnp.float32), (lefts, rights))
    return running

def reference(teacher_in, teacher_gain, qkv_weight, qk_gain, student_in, student_gain, up_weight, down_weight, projector):
    normed = (normalize(teacher_in.astype(jnp.float32)) * teacher_gain).astype(jnp.bfloat16)
    projected = jnp.dot(normed, qkv_weight.reshape(D, 3 * HD), preferred_element_type=jnp.float32)
    projected = projected.reshape(TOKENS, 3, TH, HEAD)

    def head_norm(values):
        return (normalize(values) * qk_gain).astype(jnp.bfloat16)
    queries = head_norm(projected[:, 0]).reshape(IMAGES, PATCH, TH, HEAD)
    keys_all = head_norm(projected[:, 1]).reshape(IMAGES, PATCH, TH, HEAD)
    values_all = projected[:, 2].astype(jnp.bfloat16).reshape(IMAGES, PATCH, TH, HEAD)

    def attend(group):
        scores = jnp.einsum('qhc,khc->hqk', group[0].astype(jnp.float32), group[1].astype(jnp.float32)) * HEAD ** (-0.5)
        attn = jax.nn.softmax(scores, axis=-1).astype(jnp.bfloat16)
        return jnp.einsum('hqk,khc->qhc', attn.astype(jnp.float32), group[2].astype(jnp.float32))
    features = lax.map(attend, (queries, keys_all, values_all)).reshape(TOKENS, HD)
    target = normalize(features)
    student_normed = (normalize(student_in.astype(jnp.float32)) * student_gain).astype(jnp.bfloat16)
    pre_act = jnp.dot(student_normed, up_weight, preferred_element_type=jnp.float32)
    gated, slope = gelu_parts(pre_act)
    activ = gated.astype(jnp.bfloat16)
    hidden_blocks = SFF // N_MP
    mlp_sum = rounded_sum(activ.reshape(TOKENS, N_MP, hidden_blocks).transpose(1, 0, 2), down_weight.reshape(N_MP, hidden_blocks, DS), 'tf,fc->tc', (TOKENS, DS))
    block_out = (student_in.astype(jnp.float32) + mlp_sum).astype(jnp.bfloat16)
    predicted = jnp.dot(block_out, projector, preferred_element_type=jnp.float32)
    grad_pred = ((predicted - target) * TOKENS ** (-0.5)).astype(jnp.bfloat16)
    grad_projector = rounded_sum(block_out.reshape(N_DP, TOK_DEV, DS), grad_pred.reshape(N_DP, TOK_DEV, HD), 'tc,tf->cf', (DS, HD)).astype(jnp.bfloat16)
    feature_blocks = HD // N_MP
    grad_block = rounded_sum(grad_pred.reshape(TOKENS, N_MP, feature_blocks).transpose(1, 0, 2), projector.reshape(DS, N_MP, feature_blocks).transpose(1, 0, 2), 'tf,cf->tc', (TOKENS, DS)).astype(jnp.bfloat16)
    grad_down = rounded_sum(activ.reshape(N_DP, TOK_DEV, SFF), grad_block.reshape(N_DP, TOK_DEV, DS), 'tf,tc->fc', (SFF, DS)).astype(jnp.bfloat16)
    grad_act = jnp.dot(grad_block, down_weight.T, preferred_element_type=jnp.float32)
    grad_pre = (grad_act * slope).astype(jnp.bfloat16)
    grad_up = rounded_sum(student_normed.reshape(N_DP, TOK_DEV, DS), grad_pre.reshape(N_DP, TOK_DEV, SFF), 'tc,tf->cf', (DS, SFF)).astype(jnp.bfloat16)
    return (grad_up, grad_down, grad_projector)
```

```python
import functools
import math

import jax
import jax.numpy as jnp
from jax import lax
from jax.experimental import pallas as pl
from jax.experimental.pallas import tpu as pltpu
from jax.sharding import Mesh, PartitionSpec as P

HEAD = 128
PATCH = 256
EPSILON = 1e-06
F32 = jnp.float32
BF16 = jnp.bfloat16

SIZES = {"zh": 2, "y": 8, "c": 2, "zl": 4, "x": 4}
DP = ("zh", "y", "c")
MP = ("zl", "x")
RING_ORDER = (0, -1, 1, -2, 2, -3, 3, 4)


def normalize(values):
    row_mean = jnp.mean(values, axis=-1, keepdims=True)
    centered = values - row_mean
    row_var = jnp.mean(centered * centered, axis=-1, keepdims=True)
    return centered * lax.rsqrt(row_var + EPSILON)


def gelu_parts(pre_act):
    cdf_part = 0.5 * (1.0 + lax.erf(pre_act * 0.7071067811865476))
    density = jnp.exp(-0.5 * pre_act * pre_act) * 0.3989422804014327
    return (pre_act * cdf_part, cdf_part + pre_act * density)


def shift(values, axis, step):
    size = SIZES[axis]
    return lax.ppermute(values, axis, [(i, (i + step) % size) for i in range(size)])


def swap(values, axis):
    return lax.all_to_all(values, axis, split_axis=0, concat_axis=0)


def spread(values, axis):
    return swap(jnp.broadcast_to(values[None], (SIZES[axis],) + values.shape), axis)


def ring_gather(chunk, forward_last):
    plus = [chunk]
    minus = [chunk]
    for unused in range(3):
        plus.append(shift(plus[-1], "y", 1))
        minus.append(shift(minus[-1], "y", -1))
    last = shift(plus[3], "y", 1) if forward_last else shift(minus[3], "y", -1)
    return [chunk, plus[1], minus[1], plus[2], minus[2], plus[3], minus[3], last]


def sum_parts(parts):
    return jnp.sum(parts.astype(F32), axis=0)


def reduce_mp(term):
    rows, cols = term.shape
    part = sum_parts(swap(term.reshape(4, rows // 4, cols), "x")).astype(BF16)
    part = sum_parts(swap(part.reshape(4, rows // 16, cols), "zl")).astype(BF16)
    part = spread(part, "zl").reshape(rows // 4, cols)
    return spread(part, "x").reshape(rows, cols)


def merge_stats(stats, count, axis):
    parts = spread(stats, axis)
    size = parts.shape[0]
    means = parts[:, 0] / count
    total = jnp.sum(parts[:, 0], axis=0)
    mean = total / (count * size)
    moved = means - mean[None]
    spreads = jnp.sum(parts[:, 1], axis=0) + count * jnp.sum(moved * moved, axis=0)
    return jnp.stack([total, spreads])


def teacher_kernel(
    place, a_ref, wa_ref, wa2_ref, wb_ref, wb2_ref, qg_ref, f_ref, n_ref, acc_ref
):
    zh, y, c = place[0], place[1], place[2]
    width = 16 * 384

    def block(b):
        return a_ref[b % 4, b // 4, :256, :].astype(F32)

    def fold(values):
        return values[:, :128] + values[:, 128:256] + values[:, 256:]

    total = lax.fori_loop(
        0, 16, lambda b, t: t + fold(block(b)), jnp.zeros((256, 128), F32)
    )
    mean = jnp.sum(total, axis=1, keepdims=True) / width

    def squares(b, t):
        d = block(b) - mean
        return t + fold(d * d)

    total = lax.fori_loop(0, 16, squares, jnp.zeros((256, 128), F32))
    rstd = lax.rsqrt(jnp.sum(total, axis=1, keepdims=True) / width + EPSILON)

    def write(b, carry):
        rows = a_ref[b % 4, b // 4, 256:272, :].astype(F32)
        gain = rows[0:1] + rows[1:2] + rows[2:3]
        n_ref[b] = ((block(b) - mean) * rstd * gain).astype(BF16)
        return carry

    lax.fori_loop(0, 16, write, 0)

    acc_ref[...] = jnp.zeros_like(acc_ref)
    for own, other, hi in ((wa_ref, wa2_ref, zh), (wb_ref, wb2_ref, 1 - zh)):
        for j, off in enumerate(RING_ORDER):
            b = hi * 8 + lax.rem(y + off + 8, 8)
            left = n_ref[b]
            right = jnp.concatenate(
                [own[j, 0], own[j, 1], own[j, 2], other[j, 0], other[j, 1], other[j, 2]],
                axis=1,
            )
            acc_ref[...] += jnp.dot(left, right, preferred_element_type=F32)

    def head(base, row):
        gain = jnp.where(row == 0, qg_ref[0:1, :], qg_ref[1:2, :])
        query = (normalize(acc_ref[:, base : base + 128]) * gain).astype(BF16)
        key = (normalize(acc_ref[:, base + 128 : base + 256]) * gain).astype(BF16)
        value = acc_ref[:, base + 256 : base + 384].astype(BF16)
        scores = lax.dot_general(
            query, key, (((1,), (1,)), ((), ())), preferred_element_type=F32
        ) * (HEAD ** (-0.5))
        scores = jnp.exp(scores - jnp.max(scores, axis=1, keepdims=True))
        attn = (scores / jnp.sum(scores, axis=1, keepdims=True)).astype(BF16)
        return jnp.dot(attn, value, preferred_element_type=F32)

    mine = head(0, c)
    theirs = head(384, 1 - c)
    f_ref[:, :128] = jnp.where(c == 0, mine, theirs)
    f_ref[:, 128:] = jnp.where(c == 0, theirs, mine)


def shards(
    teacher_in,
    teacher_gain,
    qkv_weight,
    qk_gain,
    student_in,
    student_gain,
    up_weight,
    down_weight,
    projector,
):
    tok_rows = teacher_in.shape[0]

    weight = qkv_weight.transpose(1, 0, 2).reshape(3, 192, 2, 128)
    weight = lax.all_to_all(weight, "c", split_axis=2, concat_axis=1).reshape(3, 384, 128)
    weight_far = shift(weight, "zh", 1)

    hi = lax.reduce_precision(teacher_gain, 8, 7)
    mid = lax.reduce_precision(teacher_gain - hi, 8, 7)
    low = teacher_gain - hi - mid
    gain_rows = jnp.stack([hi, mid, low] + [jnp.zeros_like(hi)] * 13).astype(BF16)
    shard = jnp.concatenate([teacher_in, gain_rows], axis=0)
    gathered = lax.all_gather(lax.all_gather(shard, "zl"), "x")

    near = jnp.stack(ring_gather(weight, True))
    far = jnp.stack(ring_gather(weight_far, False))
    near_other = shift(near, "c", 1)
    far_other = shift(far, "c", 1)

    place = jnp.stack([lax.axis_index("zh"), lax.axis_index("y"), lax.axis_index("c")])
    vmem = pl.BlockSpec(memory_space=pltpu.VMEM)
    features = pl.pallas_call(
        teacher_kernel,
        out_shape=jax.ShapeDtypeStruct((256, 256), F32),
        in_specs=[pl.BlockSpec(memory_space=pltpu.SMEM)] + [vmem] * 6,
        out_specs=vmem,
        scratch_shapes=[pltpu.VMEM((16, 256, 384), BF16), pltpu.VMEM((256, 768), F32)],
        compiler_params=pltpu.CompilerParams(vmem_limit_bytes=40 * 1024 * 1024),
        cost_estimate=pl.CostEstimate(
            flops=2 * 256 * 6144 * 768, bytes_accessed=13_000_000, transcendentals=131072
        ),
        name="teacher",
    )(place, gathered, near, near_other, far, far_other, qk_gain)

    student_normed = (normalize(student_in.astype(F32)) * student_gain).astype(BF16)
    pre_act = jnp.dot(student_normed, up_weight, preferred_element_type=F32)
    gated, slope = gelu_parts(pre_act)
    activ = gated.astype(BF16)
    mlp_term = jnp.dot(activ, down_weight, preferred_element_type=F32).astype(BF16)
    mlp_sum = reduce_mp(mlp_term).astype(F32)
    block_out = (student_in.astype(F32) + mlp_sum).astype(BF16)
    predicted = jnp.dot(block_out, projector, preferred_element_type=F32)

    local_sum = jnp.sum(features, axis=1)
    local_dev = features - (local_sum / 256)[:, None]
    stats = jnp.stack([local_sum, jnp.sum(local_dev * local_dev, axis=1)])
    stats = merge_stats(merge_stats(stats, 256, "x"), 1024, "zl")
    target = (features - (stats[0] / 4096)[:, None]) * lax.rsqrt(stats[1] / 4096 + EPSILON)[:, None]

    loss_factor = 1.0 / math.sqrt(tok_rows * 32)
    grad_pred = ((predicted - target) * loss_factor).astype(BF16)
    block_term = jnp.einsum("tf,cf->tc", grad_pred, projector, preferred_element_type=F32)
    grad_block = reduce_mp(block_term.astype(BF16))
    proj_term = jnp.einsum("tc,tf->cf", block_out, grad_pred, preferred_element_type=F32)
    down_term = jnp.einsum("tc,tf->cf", grad_block, activ, preferred_element_type=F32)
    grad_act = jnp.einsum("tc,fc->tf", grad_block, down_weight, preferred_element_type=F32)
    grad_pre = (grad_act * slope).astype(BF16)
    up_term = jnp.einsum("tc,tf->cf", student_normed, grad_pre, preferred_element_type=F32)

    terms = jnp.stack([t.astype(BF16) for t in (up_term, down_term, proj_term)])
    terms = terms.reshape(3, 2, 8, 2, 32, 256)
    terms = lax.all_to_all(terms, "c", split_axis=3, concat_axis=0)
    terms = sum_parts(terms).astype(BF16)
    terms = lax.all_to_all(terms, "y", split_axis=2, concat_axis=0)
    terms = sum_parts(terms).astype(BF16)
    terms = sum_parts(lax.all_to_all(terms, "zh", split_axis=1, concat_axis=0)).astype(BF16)
    return terms[0], terms[1].T, terms[2]


def solution(mesh):
    fine = Mesh(mesh.devices.reshape(tuple(SIZES.values())), tuple(SIZES))
    in_specs = (
        P(DP, MP),
        P(MP),
        P(DP, None, MP),
        P(MP, None),
        P(DP, None),
        P(),
        P(None, MP),
        P(MP, None),
        P(None, MP),
    )
    out_specs = (P(DP, MP), P(MP, DP), P(DP, MP))
    return jax.shard_map(shards, mesh=fine, in_specs=in_specs, out_specs=out_specs, check_vma=False)
```

```python
import math

import jax
import jax.numpy as jnp
from jax import lax
from jax.experimental import pallas as pl
from jax.experimental.pallas import tpu as pltpu
from jax.sharding import Mesh, PartitionSpec as P

HEAD = 128
PATCH = 256
EPSILON = 1e-06
F32 = jnp.float32
BF16 = jnp.bfloat16

SIZES = {"zh": 2, "y": 8, "c": 2, "zl": 4, "x": 4}
DP = ("zh", "y", "c")
MP = ("zl", "x")


def normalize(values):
    row_mean = jnp.mean(values, axis=-1, keepdims=True)
    centered = values - row_mean
    row_var = jnp.mean(centered * centered, axis=-1, keepdims=True)
    return centered * lax.rsqrt(row_var + EPSILON)


def gelu_parts(pre_act):
    cdf_part = 0.5 * (1.0 + lax.erf(pre_act * 0.7071067811865476))
    density = jnp.exp(-0.5 * pre_act * pre_act) * 0.3989422804014327
    return (pre_act * cdf_part, cdf_part + pre_act * density)


def shift(values, axis, step):
    size = SIZES[axis]
    return lax.ppermute(values, axis, [(i, (i + step) % size) for i in range(size)])


def flip(values, axes, bits):
    return lax.ppermute(values, axes, [(i, i ^ bits) for i in range(4)])


def tie(values, *others):
    return lax.optimization_barrier((values, *others))[0]


def swap(values, axis):
    return lax.all_to_all(values, axis, split_axis=0, concat_axis=0)


def spread(values, axis):
    return swap(jnp.broadcast_to(values[None], (SIZES[axis],) + values.shape), axis)


def sum_parts(parts):
    return jnp.sum(parts.astype(F32), axis=0)


def mp_scatter_x(term):
    rows, cols = term.shape
    return sum_parts(swap(term.reshape(4, rows // 4, cols), "x")).astype(BF16)


def mp_scatter_zl(term):
    rows, cols = term.shape
    return sum_parts(swap(term.reshape(4, rows // 4, cols), "zl")).astype(BF16)


def mp_gather_zl(part):
    rows, cols = part.shape
    return spread(part, "zl").reshape(4 * rows, cols)


def mp_gather_x(part):
    rows, cols = part.shape
    return spread(part, "x").reshape(4 * rows, cols)


def merge_stats(stats, count):
    parts = swap(jnp.broadcast_to(stats[None], (16,) + stats.shape), MP)
    total = jnp.sum(parts[:, 0], axis=0)
    mean = total / (count * 16)
    moved = parts[:, 0] / count - mean[None]
    spreads = jnp.sum(parts[:, 1], axis=0) + count * jnp.sum(moved * moved, axis=0)
    return mean, spreads / (count * 16)


def norm_kernel(place, a0_ref, am_ref, ap_ref, lo_ref, hi_ref, n_ref):
    x, my_zl, my_zh = place[0], place[1], place[2]
    blocks = []
    for i in range(4):
        blocks.append((a0_ref, i, i, 0))
        blocks.append((am_ref, i, i, 3))
        blocks.append((ap_ref, i, i, 1))
        blocks.append((lo_ref if i < 2 else hi_ref, i % 2, i, 2))
    width = 16 * 384

    def fold(values):
        return values[:, :128] + values[:, 128:256] + values[:, 256:]

    @pl.loop(0, 8)
    def _(t):
        rows = pl.ds(pl.multiple_of(t * 32, 32), 32)
        total = jnp.zeros((32, 128), F32)
        for ref, i, dz, off in blocks:
            total += fold(ref[i, rows, :].astype(F32))
        mean = jnp.sum(total, axis=1, keepdims=True) / width
        total = jnp.zeros((32, 128), F32)
        for ref, i, dz, off in blocks:
            d = ref[i, rows, :].astype(F32) - mean
            total += fold(d * d)
        rstd = lax.rsqrt(jnp.sum(total, axis=1, keepdims=True) / width + EPSILON)
        for ref, i, dz, off in blocks:
            gains = ref[i, 256:272, :].astype(F32)
            gain = gains[0:1] + gains[1:2] + gains[2:3]
            zl = my_zl ^ dz
            xs = lax.rem(x + off, 4)
            spot = ((zl & 1) * 4 + xs) * 2 + ((zl >> 1) ^ my_zh)
            d = ref[i, rows, :].astype(F32) - mean
            n_ref[rows, pl.ds(pl.multiple_of(spot * 384, 128), 384)] = (
                d * rstd * gain
            ).astype(BF16)


def attention_kernel(place, own_ref, other_ref, w_ref, qg_ref, f_ref):
    gain = jnp.where(place[0] == 0, qg_ref[0:1, :], qg_ref[1:2, :])
    for image, ref in enumerate((own_ref, other_ref)):
        projected = jnp.dot(ref[...], w_ref[...], preferred_element_type=F32)
        query = (normalize(projected[:, :128]) * gain).astype(BF16)
        key = (normalize(projected[:, 128:256]) * gain).astype(BF16)
        value = projected[:, 256:].astype(BF16)
        scores = lax.dot_general(
            query, key, (((1,), (1,)), ((), ())), preferred_element_type=F32
        ) * (HEAD ** (-0.5))
        scores = jnp.exp(scores - jnp.max(scores, axis=1, keepdims=True))
        attn = (scores / jnp.sum(scores, axis=1, keepdims=True)).astype(BF16)
        f_ref[image] = jnp.dot(attn, value, preferred_element_type=F32)


def reduce_dp(terms):
    k = terms.shape[0]
    terms = terms.reshape(k, 16, 2, 32, 256)
    terms = lax.all_to_all(terms, "c", split_axis=2, concat_axis=0)
    terms = sum_parts(terms).astype(BF16)
    terms = lax.all_to_all(terms, ("zh", "y"), split_axis=1, concat_axis=0)
    return sum_parts(terms).astype(BF16)


def shards(
    teacher_in,
    teacher_gain,
    qkv_weight,
    qk_gain,
    student_in,
    student_gain,
    up_weight,
    down_weight,
    projector,
):
    tok_rows = teacher_in.shape[0]

    first = lax.axis_index("c") == 0
    weight = qkv_weight.reshape(192, 3, 2, 128).transpose(2, 0, 1, 3).reshape(2, 192, 384)
    kept = jnp.where(first, weight[0], weight[1])
    given = jnp.where(first, weight[1], weight[0])
    zh_kept = flip(kept, ("zh", "c"), 2)
    zh_given = flip(given, ("zh", "c"), 3)
    c_given = flip(given, ("zh", "c"), 1)

    hi = lax.reduce_precision(teacher_gain, 8, 7)
    mid = lax.reduce_precision(teacher_gain - hi, 8, 7)
    low = teacher_gain - hi - mid
    gain_rows = jnp.stack([hi, mid, low] + [jnp.zeros_like(hi)] * 13).astype(BF16)
    shard = tie(jnp.concatenate([teacher_in, gain_rows], axis=0), c_given)
    pair = jnp.stack([shard, flip(shard, "zl", 1)])

    student_normed = (normalize(student_in.astype(F32)) * student_gain).astype(BF16)
    pre_act = jnp.dot(student_normed, up_weight, preferred_element_type=F32)
    gated, slope = gelu_parts(pre_act)
    activ = gated.astype(BF16)
    mlp_term = jnp.dot(activ, down_weight, preferred_element_type=F32).astype(BF16)

    def by_core(mine, theirs):
        return jnp.where(first, jnp.stack([mine, theirs]), jnp.stack([theirs, mine]))

    zh_kept, zh_given, pair, mlp_term = lax.optimization_barrier(
        (zh_kept, zh_given, pair, mlp_term)
    )
    rows = jnp.concatenate([by_core(kept, c_given), by_core(zh_kept, zh_given)])
    weight = lax.all_gather(rows, "y").reshape(6144, 384)

    part = mp_scatter_x(tie(mlp_term, rows))
    shard = tie(jnp.concatenate([pair, flip(pair, "zl", 2)]), part)
    from_left = shift(shard, "x", 1)
    from_right = shift(shard, "x", -1)
    part = mp_gather_zl(mp_scatter_zl(tie(part, shard)))
    from_left, from_right, part = lax.optimization_barrier((from_left, from_right, part))
    far_low = shift(from_left[:2], "x", 1)
    far_high = shift(from_right[2:], "x", -1)

    place_x = jnp.stack([lax.axis_index("x"), lax.axis_index("zl"), lax.axis_index("zh")])
    place_c = lax.axis_index("c").reshape(1)
    smem = pl.BlockSpec(memory_space=pltpu.SMEM)
    vmem = pl.BlockSpec(memory_space=pltpu.VMEM)
    params = pltpu.CompilerParams(vmem_limit_bytes=40 * 1024 * 1024)
    normed = pl.pallas_call(
        norm_kernel,
        out_shape=jax.ShapeDtypeStruct((256, 6144), BF16),
        in_specs=[smem] + [vmem] * 5,
        out_specs=vmem,
        compiler_params=params,
        cost_estimate=pl.CostEstimate(
            flops=1000, bytes_accessed=1000, transcendentals=0
        ),
        name="teacher_norm",
    )(place_x, shard, from_left, from_right, far_low, far_high)
    normed_other = shift(normed, "c", 1)
    mlp_sum = mp_gather_x(tie(part, normed))
    heads = pl.pallas_call(
        attention_kernel,
        out_shape=jax.ShapeDtypeStruct((2, 256, 128), F32),
        in_specs=[smem] + [vmem] * 4,
        out_specs=vmem,
        compiler_params=params,
        cost_estimate=pl.CostEstimate(
            flops=2 * 512 * 6144 * 384, bytes_accessed=11_000_000, transcendentals=131072
        ),
        name="teacher_heads",
    )(place_c, normed, normed_other, weight, qk_gain)
    crossed = shift(heads[1], "c", 1)
    features = jnp.where(
        place_c[0] == 0,
        jnp.concatenate([heads[0], crossed], axis=1),
        jnp.concatenate([crossed, heads[0]], axis=1),
    )

    block_out = (student_in.astype(F32) + mlp_sum.astype(F32)).astype(BF16)
    predicted = jnp.dot(block_out, projector, preferred_element_type=F32)

    local_sum = jnp.sum(features, axis=1)
    local_dev = features - (local_sum / 256)[:, None]
    stats = jnp.stack([local_sum, jnp.sum(local_dev * local_dev, axis=1)])
    feat_mean, feat_var = merge_stats(stats, 256)
    target = (features - feat_mean[:, None]) * lax.rsqrt(feat_var + EPSILON)[:, None]

    loss_factor = 1.0 / math.sqrt(tok_rows * 32)
    grad_pred = ((predicted - target) * loss_factor).astype(BF16)
    block_term = jnp.einsum("tf,cf->tc", grad_pred, projector, preferred_element_type=F32)
    proj_term = jnp.einsum("tc,tf->cf", block_out, grad_pred, preferred_element_type=F32)
    grad_block = mp_scatter_zl(mp_scatter_x(block_term.astype(BF16)))
    grad_block = mp_gather_x(mp_gather_zl(grad_block))
    down_term = jnp.einsum("tc,tf->cf", grad_block, activ, preferred_element_type=F32)
    grad_act = jnp.einsum("tc,fc->tf", grad_block, down_weight, preferred_element_type=F32)
    grad_pre = (grad_act * slope).astype(BF16)
    up_term = jnp.einsum("tc,tf->cf", student_normed, grad_pre, preferred_element_type=F32)
    terms = jnp.stack([t.astype(BF16) for t in (up_term, down_term, proj_term)])
    grad_up, grad_down, grad_projector = reduce_dp(terms)
    return grad_up, grad_down.T, grad_projector


def solution(mesh):
    fine = Mesh(mesh.devices.reshape(tuple(SIZES.values())), tuple(SIZES))
    in_specs = (
        P(DP, MP),
        P(MP),
        P(DP, None, MP),
        P(MP, None),
        P(DP, None),
        P(),
        P(None, MP),
        P(MP, None),
        P(None, MP),
    )
    out_specs = (P(DP, MP), P(MP, DP), P(DP, MP))
    return jax.shard_map(shards, mesh=fine, in_specs=in_specs, out_specs=out_specs, check_vma=False)
```

```python
import math

import jax
import jax.numpy as jnp
from jax import lax
from jax.experimental import pallas as pl
from jax.experimental.pallas import tpu as pltpu
from jax.sharding import Mesh, PartitionSpec as P

HEAD = 128
PATCH = 256
EPSILON = 1e-06
F32 = jnp.float32
BF16 = jnp.bfloat16

SIZES = {"zh": 2, "y": 8, "c": 2, "zl": 4, "x": 4}
DP = ("zh", "y", "c")
MP = ("zl", "x")


def normalize(values):
    row_mean = jnp.mean(values, axis=-1, keepdims=True)
    centered = values - row_mean
    row_var = jnp.mean(centered * centered, axis=-1, keepdims=True)
    return centered * lax.rsqrt(row_var + EPSILON)


def gelu_parts(pre_act):
    cdf_part = 0.5 * (1.0 + lax.erf(pre_act * 0.7071067811865476))
    density = jnp.exp(-0.5 * pre_act * pre_act) * 0.3989422804014327
    return (pre_act * cdf_part, cdf_part + pre_act * density)


def shift(values, axis, step):
    size = SIZES[axis]
    return lax.ppermute(values, axis, [(i, (i + step) % size) for i in range(size)])


def flip(values, axes, bits=1):
    return lax.ppermute(values, axes, [(i, i ^ bits) for i in range(SIZES[axes])])


def tie(values, *others):
    return lax.optimization_barrier((values, *others))[0]


def swap(values, axis):
    return lax.all_to_all(values, axis, split_axis=0, concat_axis=0)


def spread(values, axis):
    return swap(jnp.broadcast_to(values[None], (SIZES[axis],) + values.shape), axis)


def sum_parts(parts):
    return jnp.sum(parts.astype(F32), axis=0)


def mp_scatter_x(term):
    rows, cols = term.shape
    return sum_parts(swap(term.reshape(4, rows // 4, cols), "x")).astype(BF16)


def mp_scatter_zl(term):
    rows, cols = term.shape
    return sum_parts(swap(term.reshape(4, rows // 4, cols), "zl")).astype(BF16)


def mp_gather_zl(part):
    rows, cols = part.shape
    return spread(part, "zl").reshape(4 * rows, cols)


def mp_gather_x(part):
    rows, cols = part.shape
    return spread(part, "x").reshape(4 * rows, cols)


def merge_stats(stats, count):
    parts = swap(jnp.broadcast_to(stats[None], (16,) + stats.shape), MP)
    total = jnp.sum(parts[:, 0], axis=0)
    mean = total / (count * 16)
    moved = parts[:, 0] / count - mean[None]
    spreads = jnp.sum(parts[:, 1], axis=0) + count * jnp.sum(moved * moved, axis=0)
    return mean, spreads / (count * 16)


def norm_kernel(place, *refs):
    n_ref = refs[-1]
    x, my_zl, my_zh = place[0], place[1], place[2]
    blocks = []
    for half in range(2):
        own, left, right, low, high = refs[5 * half : 5 * half + 5]
        for i in range(2):
            blocks.append((own, i, 2 * half + i, 0))
            blocks.append((left, i, 2 * half + i, 3))
            blocks.append((right, i, 2 * half + i, 1))
        blocks.append((low, 0, 2 * half, 2))
        blocks.append((high, 0, 2 * half + 1, 2))
    width = 16 * 384

    def fold(values):
        return values[:, :128] + values[:, 128:256] + values[:, 256:]

    @pl.loop(0, 8)
    def _(t):
        rows = pl.ds(pl.multiple_of(t * 32, 32), 32)
        total = jnp.zeros((32, 128), F32)
        for ref, i, dz, off in blocks:
            total += fold(ref[i, rows, :].astype(F32))
        mean = jnp.sum(total, axis=1, keepdims=True) / width
        total = jnp.zeros((32, 128), F32)
        for ref, i, dz, off in blocks:
            d = ref[i, rows, :].astype(F32) - mean
            total += fold(d * d)
        rstd = lax.rsqrt(jnp.sum(total, axis=1, keepdims=True) / width + EPSILON)
        for ref, i, dz, off in blocks:
            gains = ref[i, 256:272, :].astype(F32)
            gain = gains[0:1] + gains[1:2] + gains[2:3]
            zl = my_zl ^ dz
            xs = lax.rem(x + off, 4)
            spot = ((zl & 1) * 4 + xs) * 2 + ((zl >> 1) ^ my_zh)
            d = ref[i, rows, :].astype(F32) - mean
            n_ref[rows, pl.ds(pl.multiple_of(spot * 384, 128), 384)] = (
                d * rstd * gain
            ).astype(BF16)


def attention_kernel(place, own_ref, other_ref, w_ref, qg_ref, f_ref):
    gain = jnp.where(place[0] == 0, qg_ref[0:1, :], qg_ref[1:2, :])
    for image, ref in enumerate((own_ref, other_ref)):
        projected = jnp.dot(ref[...], w_ref[...], preferred_element_type=F32)
        query = (normalize(projected[:, :128]) * gain).astype(BF16)
        key = (normalize(projected[:, 128:256]) * gain).astype(BF16)
        value = projected[:, 256:].astype(BF16)
        scores = lax.dot_general(
            query, key, (((1,), (1,)), ((), ())), preferred_element_type=F32
        ) * (HEAD ** (-0.5))
        scores = jnp.exp(scores - jnp.max(scores, axis=1, keepdims=True))
        attn = (scores / jnp.sum(scores, axis=1, keepdims=True)).astype(BF16)
        f_ref[image] = jnp.dot(attn, value, preferred_element_type=F32)


def reduce_dp(terms):
    k = terms.shape[0]
    terms = terms.reshape(k, 16, 2, 32, 256)
    terms = lax.all_to_all(terms, "c", split_axis=2, concat_axis=0)
    terms = sum_parts(terms).astype(BF16)
    terms = lax.all_to_all(terms, ("zh", "y"), split_axis=1, concat_axis=0)
    return sum_parts(terms).astype(BF16)


def reduce_projector(term, first):
    term = term.reshape(2, 8, 2, 32, 256)
    mine = jnp.where(first, term[:, :, 0], term[:, :, 1])
    theirs = flip(jnp.where(first, term[:, :, 1], term[:, :, 0]), "c")
    term = (mine.astype(F32) + theirs.astype(F32)).astype(BF16)
    term = term.transpose(1, 0, 2, 3).reshape(8 * 64, 256)
    term = lax.psum_scatter(term, "y", scatter_dimension=0, tiled=True).reshape(2, 32, 256)
    low = lax.axis_index("zh") == 0
    theirs = flip(jnp.where(low, term[1], term[0]), "zh")
    mine = jnp.where(low, term[0], term[1])
    return (mine.astype(F32) + theirs.astype(F32)).astype(BF16)


def shards(
    teacher_in,
    teacher_gain,
    qkv_weight,
    qk_gain,
    student_in,
    student_gain,
    up_weight,
    down_weight,
    projector,
):
    tok_rows = teacher_in.shape[0]

    first = lax.axis_index("c") == 0
    weight = qkv_weight.reshape(192, 3, 2, 128).transpose(2, 0, 1, 3).reshape(2, 192, 384)
    near = jnp.where(first, weight, weight[::-1])
    far = flip(near, "zh")
    given = flip(jnp.stack([near[1], far[1]]), "c")

    hi = lax.reduce_precision(teacher_gain, 8, 7)
    mid = lax.reduce_precision(teacher_gain - hi, 8, 7)
    low = teacher_gain - hi - mid
    gain_rows = jnp.stack([hi, mid, low] + [jnp.zeros_like(hi)] * 13).astype(BF16)
    shard = tie(jnp.concatenate([teacher_in, gain_rows], axis=0), near)
    pair = jnp.stack([shard, flip(shard, "zl", 1)])

    student_normed = (normalize(student_in.astype(F32)) * student_gain).astype(BF16)
    pre_act = jnp.dot(student_normed, up_weight, preferred_element_type=F32)
    gated, slope = gelu_parts(pre_act)
    activ = gated.astype(BF16)
    mlp_term = jnp.dot(activ, down_weight, preferred_element_type=F32).astype(BF16)

    def by_core(mine, theirs):
        return jnp.where(first, jnp.stack([mine, theirs]), jnp.stack([theirs, mine]))

    given, pair, mlp_term = lax.optimization_barrier((given, pair, mlp_term))
    rows = jnp.concatenate([by_core(near[0], given[0]), by_core(far[0], given[1])])
    weight = lax.all_gather(rows, "y").reshape(6144, 384)

    late = flip(pair, "zl", 2)
    left, right = shift(pair, "x", 1), shift(pair, "x", -1)
    part = mp_scatter_x(tie(mlp_term, rows))
    late = tie(late, part)
    late_left, late_right = shift(late, "x", 1), shift(late, "x", -1)
    low, high = shift(left[:1], "x", 1), shift(right[1:], "x", -1)
    part = mp_scatter_zl(tie(part, left, right))
    late_left, late_right, part, low, high = lax.optimization_barrier(
        (late_left, late_right, part, low, high)
    )
    late_low, late_high = shift(late_left[:1], "x", 1), shift(late_right[1:], "x", -1)
    part = mp_gather_zl(part)
    late_low, part = lax.optimization_barrier((late_low, part))
    blocks = (pair, left, right, low, high, late, late_left, late_right, late_low, late_high)

    place_x = jnp.stack([lax.axis_index("x"), lax.axis_index("zl"), lax.axis_index("zh")])
    place_c = lax.axis_index("c").reshape(1)
    smem = pl.BlockSpec(memory_space=pltpu.SMEM)
    vmem = pl.BlockSpec(memory_space=pltpu.VMEM)
    params = pltpu.CompilerParams(vmem_limit_bytes=40 * 1024 * 1024)
    normed = pl.pallas_call(
        norm_kernel,
        out_shape=jax.ShapeDtypeStruct((256, 6144), BF16),
        in_specs=[smem] + [vmem] * 10,
        out_specs=vmem,
        compiler_params=params,
        cost_estimate=pl.CostEstimate(
            flops=1000, bytes_accessed=1000, transcendentals=0
        ),
        name="teacher_norm",
    )(place_x, *blocks)
    normed_other = shift(normed, "c", 1)
    mlp_sum = mp_gather_x(tie(part, normed))
    heads = pl.pallas_call(
        attention_kernel,
        out_shape=jax.ShapeDtypeStruct((2, 256, 128), F32),
        in_specs=[smem] + [vmem] * 4,
        out_specs=vmem,
        compiler_params=params,
        cost_estimate=pl.CostEstimate(
            flops=2 * 512 * 6144 * 384, bytes_accessed=11_000_000, transcendentals=131072
        ),
        name="teacher_heads",
    )(place_c, normed, normed_other, weight, qk_gain)
    crossed = shift(heads[1], "c", 1)
    features = jnp.where(
        place_c[0] == 0,
        jnp.concatenate([heads[0], crossed], axis=1),
        jnp.concatenate([crossed, heads[0]], axis=1),
    )

    block_out = (student_in.astype(F32) + mlp_sum.astype(F32)).astype(BF16)
    predicted = jnp.dot(block_out, projector, preferred_element_type=F32)

    local_sum = jnp.sum(features, axis=1)
    local_dev = features - (local_sum / 256)[:, None]
    stats = jnp.stack([local_sum, jnp.sum(local_dev * local_dev, axis=1)])
    feat_mean, feat_var = merge_stats(stats, 256)
    target = (features - feat_mean[:, None]) * lax.rsqrt(feat_var + EPSILON)[:, None]

    loss_factor = 1.0 / math.sqrt(tok_rows * 32)
    grad_pred = ((predicted - target) * loss_factor).astype(BF16)
    block_term = jnp.einsum("tf,cf->tc", grad_pred, projector, preferred_element_type=F32)
    proj_term = jnp.einsum("tc,tf->cf", block_out, grad_pred, preferred_element_type=F32)
    grad_projector = reduce_projector(proj_term.astype(BF16), first)
    grad_block = mp_scatter_zl(mp_scatter_x(block_term.astype(BF16)))
    grad_block = mp_gather_x(mp_gather_zl(grad_block))
    down_term = jnp.einsum("tc,tf->cf", grad_block, activ, preferred_element_type=F32)
    grad_act = jnp.einsum("tc,fc->tf", grad_block, down_weight, preferred_element_type=F32)
    grad_pre = (grad_act * slope).astype(BF16)
    up_term = jnp.einsum("tc,tf->cf", student_normed, grad_pre, preferred_element_type=F32)
    grad_up, grad_down = reduce_dp(jnp.stack([up_term.astype(BF16), down_term.astype(BF16)]))
    return grad_up, grad_down.T, grad_projector


def solution(mesh):
    fine = Mesh(mesh.devices.reshape(tuple(SIZES.values())), tuple(SIZES))
    in_specs = (
        P(DP, MP),
        P(MP),
        P(DP, None, MP),
        P(MP, None),
        P(DP, None),
        P(),
        P(None, MP),
        P(MP, None),
        P(None, MP),
    )
    out_specs = (P(DP, MP), P(MP, DP), P(DP, MP))
    return jax.shard_map(shards, mesh=fine, in_specs=in_specs, out_specs=out_specs, check_vma=False)
```

```python
import math

import jax
import jax.numpy as jnp
from jax import lax
from jax.experimental import pallas as pl
from jax.experimental.pallas import tpu as pltpu
from jax.sharding import Mesh, PartitionSpec as P

HEAD = 128
PATCH = 256
EPSILON = 1e-06
F32 = jnp.float32
BF16 = jnp.bfloat16

SIZES = {"zh": 2, "y": 8, "c": 2, "zl": 4, "x": 4}
DP = ("zh", "y", "c")
MP = ("zl", "x")


def normalize(values):
    row_mean = jnp.mean(values, axis=-1, keepdims=True)
    centered = values - row_mean
    row_var = jnp.mean(centered * centered, axis=-1, keepdims=True)
    return centered * lax.rsqrt(row_var + EPSILON)


def gelu_parts(pre_act):
    cdf_part = 0.5 * (1.0 + lax.erf(pre_act * 0.7071067811865476))
    density = jnp.exp(-0.5 * pre_act * pre_act) * 0.3989422804014327
    return (pre_act * cdf_part, cdf_part + pre_act * density)


def shift(values, axis, step):
    size = SIZES[axis]
    return lax.ppermute(values, axis, [(i, (i + step) % size) for i in range(size)])


def flip(values, axes, bits=1):
    return lax.ppermute(values, axes, [(i, i ^ bits) for i in range(SIZES[axes])])


def tie(values, *others):
    return lax.optimization_barrier((values, *others))[0]


def swap(values, axis):
    return lax.all_to_all(values, axis, split_axis=0, concat_axis=0)


def spread(values, axis):
    return swap(jnp.broadcast_to(values[None], (SIZES[axis],) + values.shape), axis)


def sum_parts(parts):
    return jnp.sum(parts.astype(F32), axis=0)


def mp_scatter_x(term):
    rows, cols = term.shape
    return sum_parts(swap(term.reshape(4, rows // 4, cols), "x")).astype(BF16)


def mp_scatter_zl(term):
    rows, cols = term.shape
    return sum_parts(swap(term.reshape(4, rows // 4, cols), "zl")).astype(BF16)


def mp_gather_zl(part):
    rows, cols = part.shape
    return spread(part, "zl").reshape(4 * rows, cols)


def mp_gather_x(part):
    rows, cols = part.shape
    return spread(part, "x").reshape(4 * rows, cols)


def merge_stats(stats, count):
    parts = swap(jnp.broadcast_to(stats[None], (16,) + stats.shape), MP)
    total = jnp.sum(parts[:, 0], axis=0)
    mean = total / (count * 16)
    moved = parts[:, 0] / count - mean[None]
    spreads = jnp.sum(parts[:, 1], axis=0) + count * jnp.sum(moved * moved, axis=0)
    return mean, spreads / (count * 16)


def norm_kernel(place, a0_ref, am_ref, ap_ref, lo_ref, hi_ref, n_ref):
    x, my_zl, my_zh = place[0], place[1], place[2]
    blocks = []
    for i in range(4):
        blocks.append((a0_ref, i, i, 0))
        blocks.append((am_ref, i, i, 3))
        blocks.append((ap_ref, i, i, 1))
        blocks.append((lo_ref if i < 2 else hi_ref, i % 2, i, 2))
    width = 16 * 384

    def fold(values):
        return values[:, :128] + values[:, 128:256] + values[:, 256:]

    @pl.loop(0, 8)
    def _(t):
        rows = pl.ds(pl.multiple_of(t * 32, 32), 32)
        total = jnp.zeros((32, 128), F32)
        for ref, i, dz, off in blocks:
            total += fold(ref[i, rows, :].astype(F32))
        mean = jnp.sum(total, axis=1, keepdims=True) / width
        total = jnp.zeros((32, 128), F32)
        for ref, i, dz, off in blocks:
            d = ref[i, rows, :].astype(F32) - mean
            total += fold(d * d)
        rstd = lax.rsqrt(jnp.sum(total, axis=1, keepdims=True) / width + EPSILON)
        for ref, i, dz, off in blocks:
            gains = ref[i, 256:272, :].astype(F32)
            gain = gains[0:1] + gains[1:2] + gains[2:3]
            zl = my_zl ^ dz
            xs = lax.rem(x + off, 4)
            spot = ((zl >> 1) ^ my_zh) * 8 + (zl & 1) * 4 + xs
            d = ref[i, rows, :].astype(F32) - mean
            n_ref[rows, pl.ds(pl.multiple_of(spot * 384, 128), 384)] = (
                d * rstd * gain
            ).astype(BF16)


def near_kernel(own_ref, other_ref, w_ref, p_ref):
    for image, ref in enumerate((own_ref, other_ref)):
        p_ref[image] = jnp.dot(ref[:, :3072], w_ref[...], preferred_element_type=F32)


def attention_kernel(place, own_ref, other_ref, w_ref, p_ref, qg_ref, f_ref):
    gain = jnp.where(place[0] == 0, qg_ref[0:1, :], qg_ref[1:2, :])
    for image, ref in enumerate((own_ref, other_ref)):
        projected = p_ref[image] + jnp.dot(
            ref[:, 3072:], w_ref[...], preferred_element_type=F32
        )
        query = (normalize(projected[:, :128]) * gain).astype(BF16)
        key = (normalize(projected[:, 128:256]) * gain).astype(BF16)
        value = projected[:, 256:].astype(BF16)
        scores = lax.dot_general(
            query, key, (((1,), (1,)), ((), ())), preferred_element_type=F32
        ) * (HEAD ** (-0.5))
        scores = jnp.exp(scores - jnp.max(scores, axis=1, keepdims=True))
        attn = (scores / jnp.sum(scores, axis=1, keepdims=True)).astype(BF16)
        f_ref[image] = jnp.dot(attn, value, preferred_element_type=F32)


def reduce_dp(terms):
    k = terms.shape[0]
    terms = terms.reshape(k, 16, 2, 32, 256)
    terms = lax.all_to_all(terms, "c", split_axis=2, concat_axis=0)
    terms = sum_parts(terms).astype(BF16)
    terms = lax.all_to_all(terms, ("zh", "y"), split_axis=1, concat_axis=0)
    return sum_parts(terms).astype(BF16)


def reduce_projector(term, first):
    term = term.reshape(2, 8, 2 * 32, 256).transpose(1, 0, 2, 3).reshape(8 * 128, 256)
    term = lax.psum_scatter(term, "y", scatter_dimension=0, tiled=True).reshape(2, 2, 32, 256)
    theirs = flip(jnp.where(first, term[:, 1], term[:, 0]), "c")
    mine = jnp.where(first, term[:, 0], term[:, 1])
    term = (mine.astype(F32) + theirs.astype(F32)).astype(BF16)
    low = lax.axis_index("zh") == 0
    theirs = flip(jnp.where(low, term[1], term[0]), "zh")
    mine = jnp.where(low, term[0], term[1])
    return (mine.astype(F32) + theirs.astype(F32)).astype(BF16)


def shards(
    teacher_in,
    teacher_gain,
    qkv_weight,
    qk_gain,
    student_in,
    student_gain,
    up_weight,
    down_weight,
    projector,
):
    tok_rows = teacher_in.shape[0]

    first = lax.axis_index("c") == 0
    weight = qkv_weight.reshape(192, 3, 2, 128).transpose(2, 0, 1, 3).reshape(2, 192, 384)
    near = jnp.where(first, weight, weight[::-1])

    def by_core(pair):
        given = flip(pair[1], "c")
        return jnp.where(first, jnp.stack([pair[0], given]), jnp.stack([given, pair[0]]))

    near_rows = by_core(near)
    near_weight = lax.all_gather(near_rows, "y").reshape(3072, 384)

    hi = lax.reduce_precision(teacher_gain, 8, 7)
    mid = lax.reduce_precision(teacher_gain - hi, 8, 7)
    low = teacher_gain - hi - mid
    gain_rows = jnp.stack([hi, mid, low] + [jnp.zeros_like(hi)] * 13).astype(BF16)
    shard = jnp.concatenate([teacher_in, gain_rows], axis=0)
    pair = jnp.stack([shard, flip(shard, "zl", 1)])

    student_normed = (normalize(student_in.astype(F32)) * student_gain).astype(BF16)
    pre_act = jnp.dot(student_normed, up_weight, preferred_element_type=F32)
    gated, slope = gelu_parts(pre_act)
    activ = gated.astype(BF16)
    mlp_term = jnp.dot(activ, down_weight, preferred_element_type=F32).astype(BF16)

    pair, near_rows = lax.optimization_barrier((pair, near_rows))
    late = flip(pair, "zl", 2)
    part = mp_scatter_x(tie(mlp_term, pair))
    far = flip(tie(near, part), "zh")
    shard = jnp.concatenate([pair, late])
    left, right = shift(shard, "x", 1), shift(shard, "x", -1)
    far_weight = lax.all_gather(by_core(far), "y").reshape(3072, 384)
    part = mp_gather_zl(mp_scatter_zl(part))
    left, right, part = lax.optimization_barrier((left, right, part))
    low, high = shift(left[:2], "x", 1), shift(right[2:], "x", -1)
    blocks = (shard, left, right, low, high)

    place_x = jnp.stack([lax.axis_index("x"), lax.axis_index("zl"), lax.axis_index("zh")])
    place_c = lax.axis_index("c").reshape(1)
    smem = pl.BlockSpec(memory_space=pltpu.SMEM)
    vmem = pl.BlockSpec(memory_space=pltpu.VMEM)
    params = pltpu.CompilerParams(vmem_limit_bytes=40 * 1024 * 1024)
    normed = pl.pallas_call(
        norm_kernel,
        out_shape=jax.ShapeDtypeStruct((256, 6144), BF16),
        in_specs=[smem] + [vmem] * 5,
        out_specs=vmem,
        compiler_params=params,
        cost_estimate=pl.CostEstimate(
            flops=1000, bytes_accessed=1000, transcendentals=0
        ),
        name="teacher_norm",
    )(place_x, *blocks)
    normed_other = shift(normed, "c", 1)
    mlp_sum = mp_gather_x(tie(part, normed))
    partial = pl.pallas_call(
        near_kernel,
        out_shape=jax.ShapeDtypeStruct((2, 256, 384), F32),
        in_specs=[vmem] * 3,
        out_specs=vmem,
        compiler_params=params,
        cost_estimate=pl.CostEstimate(
            flops=512 * 6144 * 384, bytes_accessed=6_000_000, transcendentals=0
        ),
        name="teacher_near",
    )(normed, normed_other, near_weight)
    heads = pl.pallas_call(
        attention_kernel,
        out_shape=jax.ShapeDtypeStruct((2, 256, 128), F32),
        in_specs=[smem] + [vmem] * 5,
        out_specs=vmem,
        compiler_params=params,
        cost_estimate=pl.CostEstimate(
            flops=512 * 6144 * 384, bytes_accessed=6_000_000, transcendentals=131072
        ),
        name="teacher_heads",
    )(place_c, normed, normed_other, far_weight, partial, qk_gain)
    crossed = shift(heads[1], "c", 1)
    features = jnp.where(
        place_c[0] == 0,
        jnp.concatenate([heads[0], crossed], axis=1),
        jnp.concatenate([crossed, heads[0]], axis=1),
    )

    block_out = (student_in.astype(F32) + mlp_sum.astype(F32)).astype(BF16)
    predicted = jnp.dot(block_out, projector, preferred_element_type=F32)

    local_sum = jnp.sum(features, axis=1)
    local_dev = features - (local_sum / 256)[:, None]
    stats = jnp.stack([local_sum, jnp.sum(local_dev * local_dev, axis=1)])
    feat_mean, feat_var = merge_stats(stats, 256)
    target = (features - feat_mean[:, None]) * lax.rsqrt(feat_var + EPSILON)[:, None]

    loss_factor = 1.0 / math.sqrt(tok_rows * 32)
    grad_pred = ((predicted - target) * loss_factor).astype(BF16)
    block_term = jnp.einsum("tf,cf->tc", grad_pred, projector, preferred_element_type=F32)
    proj_term = jnp.einsum("tc,tf->cf", block_out, grad_pred, preferred_element_type=F32)
    proj_term, block_term = lax.optimization_barrier(
        (proj_term.astype(BF16), block_term.astype(BF16))
    )
    grad_projector = reduce_projector(proj_term.astype(F32), first)
    grad_block = mp_scatter_zl(mp_scatter_x(block_term))
    grad_block = mp_gather_x(mp_gather_zl(grad_block))
    down_term = jnp.einsum("tc,tf->cf", grad_block, activ, preferred_element_type=F32)
    grad_act = jnp.einsum("tc,fc->tf", grad_block, down_weight, preferred_element_type=F32)
    grad_pre = (grad_act * slope).astype(BF16)
    up_term = jnp.einsum("tc,tf->cf", student_normed, grad_pre, preferred_element_type=F32)
    grad_up, grad_down = reduce_dp(jnp.stack([up_term.astype(BF16), down_term.astype(BF16)]))
    return grad_up, grad_down.T, grad_projector


def solution(mesh):
    fine = Mesh(mesh.devices.reshape(tuple(SIZES.values())), tuple(SIZES))
    in_specs = (
        P(DP, MP),
        P(MP),
        P(DP, None, MP),
        P(MP, None),
        P(DP, None),
        P(),
        P(None, MP),
        P(MP, None),
        P(None, MP),
    )
    out_specs = (P(DP, MP), P(MP, DP), P(DP, MP))
    return jax.shard_map(shards, mesh=fine, in_specs=in_specs, out_specs=out_specs, check_vma=False)
```

```python
import math

import jax
import jax.numpy as jnp
from jax import lax
from jax.experimental import pallas as pl
from jax.experimental.pallas import tpu as pltpu
from jax.sharding import Mesh, PartitionSpec as P

HEAD = 128
PATCH = 256
EPSILON = 1e-06
F32 = jnp.float32
BF16 = jnp.bfloat16

SIZES = {"zh": 2, "y": 8, "c": 2, "zl": 4, "x": 4}
DP = ("zh", "y", "c")
MP = ("zl", "x")


def normalize(values):
    row_mean = jnp.mean(values, axis=-1, keepdims=True)
    centered = values - row_mean
    row_var = jnp.mean(centered * centered, axis=-1, keepdims=True)
    return centered * lax.rsqrt(row_var + EPSILON)


def gelu_parts(pre_act):
    cdf_part = 0.5 * (1.0 + lax.erf(pre_act * 0.7071067811865476))
    density = jnp.exp(-0.5 * pre_act * pre_act) * 0.3989422804014327
    return (pre_act * cdf_part, cdf_part + pre_act * density)


def shift(values, axis, step):
    size = SIZES[axis]
    return lax.ppermute(values, axis, [(i, (i + step) % size) for i in range(size)])


def flip(values, axes, bits=1):
    return lax.ppermute(values, axes, [(i, i ^ bits) for i in range(SIZES[axes])])


def tie(values, *others):
    return lax.optimization_barrier((values, *others))[0]


def swap(values, axis):
    return lax.all_to_all(values, axis, split_axis=0, concat_axis=0)


def spread(values, axis):
    return swap(jnp.broadcast_to(values[None], (SIZES[axis],) + values.shape), axis)


def sum_parts(parts):
    return jnp.sum(parts.astype(F32), axis=0)


def mp_scatter_x(term):
    rows, cols = term.shape
    return sum_parts(swap(term.reshape(4, rows // 4, cols), "x")).astype(BF16)


def mp_scatter_zl(term):
    rows, cols = term.shape
    return sum_parts(swap(term.reshape(4, rows // 4, cols), "zl")).astype(BF16)


def mp_gather_zl(part):
    rows, cols = part.shape
    return spread(part, "zl").reshape(4 * rows, cols)


def mp_gather_x(part):
    rows, cols = part.shape
    return spread(part, "x").reshape(4 * rows, cols)


def merge_stats(stats, count):
    parts = swap(jnp.broadcast_to(stats[None], (16,) + stats.shape), MP)
    total = jnp.sum(parts[:, 0], axis=0)
    mean = total / (count * 16)
    moved = parts[:, 0] / count - mean[None]
    spreads = jnp.sum(parts[:, 1], axis=0) + count * jnp.sum(moved * moved, axis=0)
    return mean, spreads / (count * 16)


def block_list(refs):
    blocks = []
    for half in range(len(refs) // 5):
        own, left, right, low, high = refs[5 * half : 5 * half + 5]
        for i in range(2):
            blocks.append((own, i, 2 * half + i, 0))
            blocks.append((left, i, 2 * half + i, 3))
            blocks.append((right, i, 2 * half + i, 1))
        blocks.append((low, 0, 2 * half, 2))
        blocks.append((high, 0, 2 * half + 1, 2))
    return blocks


def block_stats(blocks, rows):
    def fold(values):
        return values[:, :128] + values[:, 128:256] + values[:, 256:]

    total = jnp.zeros((32, 128), F32)
    for ref, i, dz, off in blocks:
        total += fold(ref[i, rows, :].astype(F32))
    total = jnp.sum(total, axis=1, keepdims=True)
    mean = total / (len(blocks) * 384)
    square = jnp.zeros((32, 128), F32)
    for ref, i, dz, off in blocks:
        d = ref[i, rows, :].astype(F32) - mean
        square += fold(d * d)
    return total, jnp.sum(square, axis=1, keepdims=True)


def stats_kernel(*refs):
    out_ref = refs[-1]
    blocks = block_list(list(refs[:8]) + [None, None])[:14]

    @pl.loop(0, 8)
    def _(t):
        rows = pl.ds(pl.multiple_of(t * 32, 32), 32)
        total, square = block_stats(blocks, rows)
        out_ref[0, rows, :] = jnp.broadcast_to(total, (32, 128))
        out_ref[1, rows, :] = jnp.broadcast_to(square, (32, 128))


def norm_kernel(place, stats_ref, *refs):
    n_ref = refs[-1]
    x, my_zl, my_zh = place[0], place[1], place[2]
    blocks = block_list(refs[:10])
    width, early, last = 16 * 384, 14 * 384, 2 * 384

    @pl.loop(0, 8)
    def _(t):
        rows = pl.ds(pl.multiple_of(t * 32, 32), 32)
        total, square = block_stats(blocks[14:], rows)
        first_total = stats_ref[0, rows, :][:, :1]
        mean = (first_total + total) / width
        apart = first_total / early - total / last
        square += stats_ref[1, rows, :][:, :1] + apart * apart * (early * last / width)
        rstd = lax.rsqrt(square / width + EPSILON)
        for ref, i, dz, off in blocks:
            gains = ref[i, 256:272, :].astype(F32)
            gain = gains[0:1] + gains[1:2] + gains[2:3]
            zl = my_zl ^ dz
            xs = lax.rem(x + off, 4)
            spot = ((zl >> 1) ^ my_zh) * 8 + (zl & 1) * 4 + xs
            d = ref[i, rows, :].astype(F32) - mean
            n_ref[rows, pl.ds(pl.multiple_of(spot * 384, 128), 384)] = (
                d * rstd * gain
            ).astype(BF16)


def near_kernel(own_ref, other_ref, w_ref, p_ref):
    for image, ref in enumerate((own_ref, other_ref)):
        p_ref[image] = jnp.dot(ref[:, :3072], w_ref[...], preferred_element_type=F32)


def attention_kernel(place, own_ref, other_ref, w_ref, p_ref, qg_ref, f_ref):
    gain = jnp.where(place[0] == 0, qg_ref[0:1, :], qg_ref[1:2, :])
    for image, ref in enumerate((own_ref, other_ref)):
        projected = p_ref[image] + jnp.dot(
            ref[:, 3072:], w_ref[...], preferred_element_type=F32
        )
        query = (normalize(projected[:, :128]) * gain).astype(BF16)
        key = (normalize(projected[:, 128:256]) * gain).astype(BF16)
        value = projected[:, 256:].astype(BF16)
        scores = lax.dot_general(
            query, key, (((1,), (1,)), ((), ())), preferred_element_type=F32
        ) * (HEAD ** (-0.5))
        scores = jnp.exp(scores - jnp.max(scores, axis=1, keepdims=True))
        attn = (scores / jnp.sum(scores, axis=1, keepdims=True)).astype(BF16)
        f_ref[image] = jnp.dot(attn, value, preferred_element_type=F32)


def reduce_dp(terms):
    k = terms.shape[0]
    terms = terms.reshape(k, 16, 2, 32, 256)
    terms = lax.all_to_all(terms, "c", split_axis=2, concat_axis=0)
    terms = sum_parts(terms).astype(BF16)
    terms = lax.all_to_all(terms, ("zh", "y"), split_axis=1, concat_axis=0)
    return sum_parts(terms).astype(BF16)


def shards(
    teacher_in,
    teacher_gain,
    qkv_weight,
    qk_gain,
    student_in,
    student_gain,
    up_weight,
    down_weight,
    projector,
):
    tok_rows = teacher_in.shape[0]

    first = lax.axis_index("c") == 0
    weight = qkv_weight.reshape(192, 3, 2, 128).transpose(2, 0, 1, 3).reshape(2, 192, 384)
    near = jnp.where(first, weight, weight[::-1])

    def by_core(pair):
        given = flip(pair[1], "c")
        return jnp.where(first, jnp.stack([pair[0], given]), jnp.stack([given, pair[0]]))

    near_rows = by_core(near)
    far_rows = by_core(flip(near, "zh"))
    near_weight = lax.all_gather(near_rows, "y").reshape(3072, 384)

    hi = lax.reduce_precision(teacher_gain, 8, 7)
    mid = lax.reduce_precision(teacher_gain - hi, 8, 7)
    low = teacher_gain - hi - mid
    gain_rows = jnp.stack([hi, mid, low] + [jnp.zeros_like(hi)] * 13).astype(BF16)
    shard = jnp.concatenate([teacher_in, gain_rows], axis=0)
    pair = jnp.stack([shard, flip(shard, "zl", 1)])

    student_normed = (normalize(student_in.astype(F32)) * student_gain).astype(BF16)
    pre_act = jnp.dot(student_normed, up_weight, preferred_element_type=F32)
    gated, slope = gelu_parts(pre_act)
    activ = gated.astype(BF16)
    mlp_term = jnp.dot(activ, down_weight, preferred_element_type=F32).astype(BF16)

    pair, near_rows = lax.optimization_barrier((pair, near_rows))
    late = flip(pair, "zl", 2)
    left, right = shift(pair, "x", 1), shift(pair, "x", -1)
    part = mp_scatter_x(tie(mlp_term, pair))
    part, far_rows = lax.optimization_barrier((part, far_rows))
    part = mp_scatter_zl(part)
    far_weight = lax.all_gather(far_rows, "y").reshape(3072, 384)
    late = tie(late, part)
    late_left, late_right = shift(late, "x", 1), shift(late, "x", -1)
    low, high = shift(left[:1], "x", 1), shift(right[1:], "x", -1)
    late_left, late_right, part, low, high = lax.optimization_barrier(
        (late_left, late_right, part, low, high)
    )
    late_low, late_high = shift(late_left[:1], "x", 1), shift(late_right[1:], "x", -1)
    part = mp_gather_zl(part)
    late_low, part = lax.optimization_barrier((late_low, part))
    blocks = (pair, left, right, low, high, late, late_left, late_right, late_low, late_high)

    place_x = jnp.stack([lax.axis_index("x"), lax.axis_index("zl"), lax.axis_index("zh")])
    place_c = lax.axis_index("c").reshape(1)
    smem = pl.BlockSpec(memory_space=pltpu.SMEM)
    vmem = pl.BlockSpec(memory_space=pltpu.VMEM)
    params = pltpu.CompilerParams(vmem_limit_bytes=40 * 1024 * 1024)
    early_stats = pl.pallas_call(
        stats_kernel,
        out_shape=jax.ShapeDtypeStruct((2, 256, 128), F32),
        in_specs=[vmem] * 8,
        out_specs=vmem,
        compiler_params=params,
        cost_estimate=pl.CostEstimate(
            flops=8_000_000, bytes_accessed=3_000_000, transcendentals=0
        ),
        name="teacher_stats",
    )(*blocks[:8])
    normed = pl.pallas_call(
        norm_kernel,
        out_shape=jax.ShapeDtypeStruct((256, 6144), BF16),
        in_specs=[smem] + [vmem] * 11,
        out_specs=vmem,
        compiler_params=params,
        cost_estimate=pl.CostEstimate(
            flops=1000, bytes_accessed=1000, transcendentals=0
        ),
        name="teacher_norm",
    )(place_x, early_stats, *blocks)
    normed_other = shift(normed, "c", 1)
    mlp_sum = mp_gather_x(tie(part, normed))
    partial = pl.pallas_call(
        near_kernel,
        out_shape=jax.ShapeDtypeStruct((2, 256, 384), F32),
        in_specs=[vmem] * 3,
        out_specs=vmem,
        compiler_params=params,
        cost_estimate=pl.CostEstimate(
            flops=512 * 6144 * 384, bytes_accessed=6_000_000, transcendentals=0
        ),
        name="teacher_near",
    )(normed, normed_other, near_weight)
    heads = pl.pallas_call(
        attention_kernel,
        out_shape=jax.ShapeDtypeStruct((2, 256, 128), F32),
        in_specs=[smem] + [vmem] * 5,
        out_specs=vmem,
        compiler_params=params,
        cost_estimate=pl.CostEstimate(
            flops=512 * 6144 * 384, bytes_accessed=6_000_000, transcendentals=131072
        ),
        name="teacher_heads",
    )(place_c, normed, normed_other, far_weight, partial, qk_gain)
    crossed = shift(heads[1], "c", 1)
    features = jnp.where(
        place_c[0] == 0,
        jnp.concatenate([heads[0], crossed], axis=1),
        jnp.concatenate([crossed, heads[0]], axis=1),
    )

    block_out = (student_in.astype(F32) + mlp_sum.astype(F32)).astype(BF16)
    predicted = jnp.dot(block_out, projector, preferred_element_type=F32)

    local_sum = jnp.sum(features, axis=1)
    local_dev = features - (local_sum / 256)[:, None]
    stats = jnp.stack([local_sum, jnp.sum(local_dev * local_dev, axis=1)])
    feat_mean, feat_var = merge_stats(stats, 256)
    target = (features - feat_mean[:, None]) * lax.rsqrt(feat_var + EPSILON)[:, None]

    loss_factor = 1.0 / math.sqrt(tok_rows * 32)
    grad_pred = ((predicted - target) * loss_factor).astype(BF16)
    block_term = jnp.einsum("tf,cf->tc", grad_pred, projector, preferred_element_type=F32)
    proj_term = jnp.einsum("tc,tf->cf", block_out, grad_pred, preferred_element_type=F32)
    grad_block = mp_scatter_zl(mp_scatter_x(block_term.astype(BF16)))
    grad_block = mp_gather_x(mp_gather_zl(grad_block))
    down_term = jnp.einsum("tc,tf->cf", grad_block, activ, preferred_element_type=F32)
    grad_act = jnp.einsum("tc,fc->tf", grad_block, down_weight, preferred_element_type=F32)
    grad_pre = (grad_act * slope).astype(BF16)
    up_term = jnp.einsum("tc,tf->cf", student_normed, grad_pre, preferred_element_type=F32)
    terms = jnp.stack([t.astype(BF16) for t in (up_term, down_term, proj_term)])
    grad_up, grad_down, grad_projector = reduce_dp(terms)
    return grad_up, grad_down.T, grad_projector


def solution(mesh):
    fine = Mesh(mesh.devices.reshape(tuple(SIZES.values())), tuple(SIZES))
    in_specs = (
        P(DP, MP),
        P(MP),
        P(DP, None, MP),
        P(MP, None),
        P(DP, None),
        P(),
        P(None, MP),
        P(MP, None),
        P(None, MP),
    )
    out_specs = (P(DP, MP), P(MP, DP), P(DP, MP))
    return jax.shard_map(shards, mesh=fine, in_specs=in_specs, out_specs=out_specs, check_vma=False)
```

```python
import math

import jax
import jax.numpy as jnp
from jax import lax
from jax.experimental import pallas as pl
from jax.experimental.pallas import tpu as pltpu
from jax.sharding import Mesh, PartitionSpec as P

HEAD = 128
PATCH = 256
EPSILON = 1e-06
F32 = jnp.float32
BF16 = jnp.bfloat16

SIZES = {"zh": 2, "y": 8, "c": 2, "zl": 4, "x": 4}
DP = ("zh", "y", "c")
MP = ("zl", "x")


def normalize(values):
    row_mean = jnp.mean(values, axis=-1, keepdims=True)
    centered = values - row_mean
    row_var = jnp.mean(centered * centered, axis=-1, keepdims=True)
    return centered * lax.rsqrt(row_var + EPSILON)


def gelu_parts(pre_act):
    cdf_part = 0.5 * (1.0 + lax.erf(pre_act * 0.7071067811865476))
    density = jnp.exp(-0.5 * pre_act * pre_act) * 0.3989422804014327
    return (pre_act * cdf_part, cdf_part + pre_act * density)


def shift(values, axis, step):
    size = SIZES[axis]
    return lax.ppermute(values, axis, [(i, (i + step) % size) for i in range(size)])


def flip(values, axes, bits=1):
    return lax.ppermute(values, axes, [(i, i ^ bits) for i in range(SIZES[axes])])


def tie(values, *others):
    return lax.optimization_barrier((values, *others))[0]


def swap(values, axis):
    return lax.all_to_all(values, axis, split_axis=0, concat_axis=0)


def spread(values, axis):
    return swap(jnp.broadcast_to(values[None], (SIZES[axis],) + values.shape), axis)


def sum_parts(parts):
    return jnp.sum(parts.astype(F32), axis=0)


def mp_scatter_x(term):
    rows, cols = term.shape
    return sum_parts(swap(term.reshape(4, rows // 4, cols), "x")).astype(BF16)


def mp_scatter_zl(term):
    rows, cols = term.shape
    return sum_parts(swap(term.reshape(4, rows // 4, cols), "zl")).astype(BF16)


def mp_gather_zl(part):
    rows, cols = part.shape
    return spread(part, "zl").reshape(4 * rows, cols)


def mp_gather_x(part):
    rows, cols = part.shape
    return spread(part, "x").reshape(4 * rows, cols)


def merge_stats(stats, count):
    parts = swap(jnp.broadcast_to(stats[None], (16,) + stats.shape), MP)
    total = jnp.sum(parts[:, 0], axis=0)
    mean = total / (count * 16)
    moved = parts[:, 0] / count - mean[None]
    spreads = jnp.sum(parts[:, 1], axis=0) + count * jnp.sum(moved * moved, axis=0)
    return mean, spreads / (count * 16)


def norm_kernel(place, *refs):
    n_ref = refs[-1]
    x, my_zl, my_zh = place[0], place[1], place[2]
    blocks = []
    for half in range(2):
        own, left, right, low, high = refs[5 * half : 5 * half + 5]
        for i in range(2):
            blocks.append((own, i, 2 * half + i, 0))
            blocks.append((left, i, 2 * half + i, 3))
            blocks.append((right, i, 2 * half + i, 1))
        blocks.append((low, 0, 2 * half, 2))
        blocks.append((high, 0, 2 * half + 1, 2))
    width = 16 * 384

    def fold(values):
        return values[:, :128] + values[:, 128:256] + values[:, 256:]

    @pl.loop(0, 8)
    def _(t):
        rows = pl.ds(pl.multiple_of(t * 32, 32), 32)
        total = jnp.zeros((32, 128), F32)
        for ref, i, dz, off in blocks:
            total += fold(ref[i, rows, :].astype(F32))
        mean = jnp.sum(total, axis=1, keepdims=True) / width
        total = jnp.zeros((32, 128), F32)
        for ref, i, dz, off in blocks:
            d = ref[i, rows, :].astype(F32) - mean
            total += fold(d * d)
        rstd = lax.rsqrt(jnp.sum(total, axis=1, keepdims=True) / width + EPSILON)
        for ref, i, dz, off in blocks:
            gains = ref[i, 256:272, :].astype(F32)
            gain = gains[0:1] + gains[1:2] + gains[2:3]
            zl = my_zl ^ dz
            xs = lax.rem(x + off, 4)
            spot = ((zl & 1) * 4 + xs) * 2 + ((zl >> 1) ^ my_zh)
            d = ref[i, rows, :].astype(F32) - mean
            n_ref[rows, pl.ds(pl.multiple_of(spot * 384, 128), 384)] = (
                d * rstd * gain
            ).astype(BF16)


def attention_kernel(place, own_ref, other_ref, w_ref, qg_ref, f_ref):
    gain = jnp.where(place[0] == 0, qg_ref[0:1, :], qg_ref[1:2, :])
    for image, ref in enumerate((own_ref, other_ref)):
        projected = jnp.dot(ref[...], w_ref[...], preferred_element_type=F32)
        query = (normalize(projected[:, :128]) * gain).astype(BF16)
        key = (normalize(projected[:, 128:256]) * gain).astype(BF16)
        value = projected[:, 256:].astype(BF16)
        scores = lax.dot_general(
            query, key, (((1,), (1,)), ((), ())), preferred_element_type=F32
        ) * (HEAD ** (-0.5))
        scores = jnp.exp(scores - jnp.max(scores, axis=1, keepdims=True))
        attn = (scores / jnp.sum(scores, axis=1, keepdims=True)).astype(BF16)
        f_ref[image] = jnp.dot(attn, value, preferred_element_type=F32)


def reduce_dp(terms):
    k = terms.shape[0]
    terms = terms.reshape(k, 16, 2, 32, 256)
    terms = lax.all_to_all(terms, "c", split_axis=2, concat_axis=0)
    terms = sum_parts(terms).astype(BF16)
    terms = lax.all_to_all(terms, ("zh", "y"), split_axis=1, concat_axis=0)
    return sum_parts(terms).astype(BF16)


def shards(
    teacher_in,
    teacher_gain,
    qkv_weight,
    qk_gain,
    student_in,
    student_gain,
    up_weight,
    down_weight,
    projector,
):
    tok_rows = teacher_in.shape[0]

    first = lax.axis_index("c") == 0
    weight = qkv_weight.reshape(192, 3, 2, 128).transpose(2, 0, 1, 3).reshape(2, 192, 384)
    near = jnp.where(first, weight, weight[::-1])
    far = flip(near, "zh")
    hi = lax.reduce_precision(teacher_gain, 8, 7)
    mid = lax.reduce_precision(teacher_gain - hi, 8, 7)
    low = teacher_gain - hi - mid
    gain_rows = jnp.stack([hi, mid, low] + [jnp.zeros_like(hi)] * 13).astype(BF16)
    shard = tie(jnp.concatenate([teacher_in, gain_rows], axis=0), near)
    pair = jnp.stack([shard, flip(shard, "zl", 1)])

    student_normed = (normalize(student_in.astype(F32)) * student_gain).astype(BF16)
    pre_act = jnp.dot(student_normed, up_weight, preferred_element_type=F32)
    gated, slope = gelu_parts(pre_act)
    activ = gated.astype(BF16)
    mlp_term = jnp.dot(activ, down_weight, preferred_element_type=F32).astype(BF16)

    def by_core(mine, theirs):
        return jnp.where(first, jnp.stack([mine, theirs]), jnp.stack([theirs, mine]))

    part = mp_scatter_x(mlp_term)
    given = flip(jnp.stack([near[1], far[1]]), "c")
    given, part, pair = lax.optimization_barrier((given, part, pair))
    rows = jnp.concatenate([by_core(near[0], given[0]), by_core(far[0], given[1])])
    weight = lax.all_gather(rows, "y").reshape(6144, 384)

    late = flip(pair, "zl", 2)
    left, right = shift(pair, "x", 1), shift(pair, "x", -1)
    part = mp_scatter_zl(tie(part, rows))
    late = tie(late, part)
    late_left, late_right = shift(late, "x", 1), shift(late, "x", -1)
    low, high = shift(left[:1], "x", 1), shift(right[1:], "x", -1)
    late_left, late_right, part, low, high = lax.optimization_barrier(
        (late_left, late_right, part, low, high)
    )
    late_low, late_high = shift(late_left[:1], "x", 1), shift(late_right[1:], "x", -1)
    part = mp_gather_zl(part)
    late_low, part = lax.optimization_barrier((late_low, part))
    blocks = (pair, left, right, low, high, late, late_left, late_right, late_low, late_high)

    place_x = jnp.stack([lax.axis_index("x"), lax.axis_index("zl"), lax.axis_index("zh")])
    place_c = lax.axis_index("c").reshape(1)
    smem = pl.BlockSpec(memory_space=pltpu.SMEM)
    vmem = pl.BlockSpec(memory_space=pltpu.VMEM)
    params = pltpu.CompilerParams(vmem_limit_bytes=40 * 1024 * 1024)
    normed = pl.pallas_call(
        norm_kernel,
        out_shape=jax.ShapeDtypeStruct((256, 6144), BF16),
        in_specs=[smem] + [vmem] * 10,
        out_specs=vmem,
        compiler_params=params,
        cost_estimate=pl.CostEstimate(
            flops=1000, bytes_accessed=1000, transcendentals=0
        ),
        name="teacher_norm",
    )(place_x, *blocks)
    normed_other = shift(normed, "c", 1)
    mlp_sum = mp_gather_x(tie(part, normed))
    heads = pl.pallas_call(
        attention_kernel,
        out_shape=jax.ShapeDtypeStruct((2, 256, 128), F32),
        in_specs=[smem] + [vmem] * 4,
        out_specs=vmem,
        compiler_params=params,
        cost_estimate=pl.CostEstimate(
            flops=2 * 512 * 6144 * 384, bytes_accessed=11_000_000, transcendentals=131072
        ),
        name="teacher_heads",
    )(place_c, normed, normed_other, weight, qk_gain)
    crossed = shift(heads[1], "c", 1)
    features = jnp.where(
        place_c[0] == 0,
        jnp.concatenate([heads[0], crossed], axis=1),
        jnp.concatenate([crossed, heads[0]], axis=1),
    )

    block_out = (student_in.astype(F32) + mlp_sum.astype(F32)).astype(BF16)
    predicted = jnp.dot(block_out, projector, preferred_element_type=F32)

    local_sum = jnp.sum(features, axis=1)
    local_dev = features - (local_sum / 256)[:, None]
    stats = jnp.stack([local_sum, jnp.sum(local_dev * local_dev, axis=1)])
    feat_mean, feat_var = merge_stats(stats, 256)
    target = (features - feat_mean[:, None]) * lax.rsqrt(feat_var + EPSILON)[:, None]

    loss_factor = 1.0 / math.sqrt(tok_rows * 32)
    grad_pred = ((predicted - target) * loss_factor).astype(BF16)
    block_term = jnp.einsum("tf,cf->tc", grad_pred, projector, preferred_element_type=F32)
    proj_term = jnp.einsum("tc,tf->cf", block_out, grad_pred, preferred_element_type=F32)
    grad_block = mp_scatter_zl(mp_scatter_x(block_term.astype(BF16)))
    grad_block = mp_gather_x(mp_gather_zl(grad_block))
    down_term = jnp.einsum("tc,tf->cf", grad_block, activ, preferred_element_type=F32)
    grad_act = jnp.einsum("tc,fc->tf", grad_block, down_weight, preferred_element_type=F32)
    grad_pre = (grad_act * slope).astype(BF16)
    up_term = jnp.einsum("tc,tf->cf", student_normed, grad_pre, preferred_element_type=F32)
    terms = jnp.stack([t.astype(BF16) for t in (up_term, down_term, proj_term)])
    grad_up, grad_down, grad_projector = reduce_dp(terms)
    return grad_up, grad_down.T, grad_projector


def solution(mesh):
    fine = Mesh(mesh.devices.reshape(tuple(SIZES.values())), tuple(SIZES))
    in_specs = (
        P(DP, MP),
        P(MP),
        P(DP, None, MP),
        P(MP, None),
        P(DP, None),
        P(),
        P(None, MP),
        P(MP, None),
        P(None, MP),
    )
    out_specs = (P(DP, MP), P(MP, DP), P(DP, MP))
    return jax.shard_map(shards, mesh=fine, in_specs=in_specs, out_specs=out_specs, check_vma=False)
```

```python
import math

import jax
import jax.numpy as jnp
from jax import lax
from jax.experimental import pallas as pl
from jax.experimental.pallas import tpu as pltpu
from jax.sharding import Mesh, PartitionSpec as P

HEAD = 128
PATCH = 256
EPSILON = 1e-06
F32 = jnp.float32
BF16 = jnp.bfloat16

SIZES = {"zh": 2, "y": 8, "c": 2, "zl": 4, "x": 4}
DP = ("zh", "y", "c")
MP = ("zl", "x")


def normalize(values):
    row_mean = jnp.mean(values, axis=-1, keepdims=True)
    centered = values - row_mean
    row_var = jnp.mean(centered * centered, axis=-1, keepdims=True)
    return centered * lax.rsqrt(row_var + EPSILON)


def gelu_parts(pre_act):
    cdf_part = 0.5 * (1.0 + lax.erf(pre_act * 0.7071067811865476))
    density = jnp.exp(-0.5 * pre_act * pre_act) * 0.3989422804014327
    return (pre_act * cdf_part, cdf_part + pre_act * density)


def shift(values, axis, step):
    size = SIZES[axis]
    return lax.ppermute(values, axis, [(i, (i + step) % size) for i in range(size)])


def flip(values, axes, bits=1):
    return lax.ppermute(values, axes, [(i, i ^ bits) for i in range(SIZES[axes])])


def tie(values, *others):
    return lax.optimization_barrier((values, *others))[0]


def swap(values, axis):
    return lax.all_to_all(values, axis, split_axis=0, concat_axis=0)


def spread(values, axis):
    return swap(jnp.broadcast_to(values[None], (SIZES[axis],) + values.shape), axis)


def sum_parts(parts):
    return jnp.sum(parts.astype(F32), axis=0)


def mp_scatter_x(term):
    rows, cols = term.shape
    return sum_parts(swap(term.reshape(4, rows // 4, cols), "x")).astype(BF16)


def mp_scatter_zl(term):
    rows, cols = term.shape
    return sum_parts(swap(term.reshape(4, rows // 4, cols), "zl")).astype(BF16)


def mp_sum_zl(part):
    for bits in (1, 2):
        part = (part.astype(F32) + flip(part, "zl", bits).astype(F32)).astype(BF16)
    return part


def mp_gather_zl(part):
    rows, cols = part.shape
    return spread(part, "zl").reshape(4 * rows, cols)


def mp_gather_x(part):
    rows, cols = part.shape
    return spread(part, "x").reshape(4 * rows, cols)


def merge_stats(stats, count):
    parts = swap(jnp.broadcast_to(stats[None], (16,) + stats.shape), MP)
    total = jnp.sum(parts[:, 0], axis=0)
    mean = total / (count * 16)
    moved = parts[:, 0] / count - mean[None]
    spreads = jnp.sum(parts[:, 1], axis=0) + count * jnp.sum(moved * moved, axis=0)
    return mean, spreads / (count * 16)


def norm_kernel(place, pair_ref, late_ref, n_ref):
    my_zl, my_zh = place[0], place[1]
    blocks = []
    for dz in range(4):
        for x in range(4):
            blocks.append(((pair_ref, late_ref)[dz // 2], (x, dz % 2), dz, x))
    width = 16 * 384

    def fold(values):
        return values[:, :128] + values[:, 128:256] + values[:, 256:]

    @pl.loop(0, 8)
    def _(t):
        rows = pl.ds(pl.multiple_of(t * 32, 32), 32)
        total = jnp.zeros((32, 128), F32)
        for ref, (i, j), dz, x in blocks:
            total += fold(ref[i, j, rows, :].astype(F32))
        mean = jnp.sum(total, axis=1, keepdims=True) / width
        total = jnp.zeros((32, 128), F32)
        for ref, (i, j), dz, x in blocks:
            d = ref[i, j, rows, :].astype(F32) - mean
            total += fold(d * d)
        rstd = lax.rsqrt(jnp.sum(total, axis=1, keepdims=True) / width + EPSILON)
        for ref, (i, j), dz, x in blocks:
            gains = ref[i, j, 256:272, :].astype(F32)
            gain = gains[0:1] + gains[1:2] + gains[2:3]
            zl = my_zl ^ dz
            spot = ((zl & 1) * 4 + x) * 2 + ((zl >> 1) ^ my_zh)
            d = ref[i, j, rows, :].astype(F32) - mean
            n_ref[rows, pl.ds(pl.multiple_of(spot * 384, 128), 384)] = (
                d * rstd * gain
            ).astype(BF16)


def attention_kernel(place, own_ref, other_ref, w_ref, qg_ref, f_ref):
    gain = jnp.where(place[0] == 0, qg_ref[0:1, :], qg_ref[1:2, :])
    for image, ref in enumerate((own_ref, other_ref)):
        projected = jnp.dot(ref[...], w_ref[...], preferred_element_type=F32)
        query = (normalize(projected[:, :128]) * gain).astype(BF16)
        key = (normalize(projected[:, 128:256]) * gain).astype(BF16)
        value = projected[:, 256:].astype(BF16)
        scores = lax.dot_general(
            query, key, (((1,), (1,)), ((), ())), preferred_element_type=F32
        ) * (HEAD ** (-0.5))
        scores = jnp.exp(scores - jnp.max(scores, axis=1, keepdims=True))
        attn = (scores / jnp.sum(scores, axis=1, keepdims=True)).astype(BF16)
        f_ref[image] = jnp.dot(attn, value, preferred_element_type=F32)


def reduce_dp(terms):
    k = terms.shape[0]
    terms = terms.reshape(k, 16, 2, 32, 256)
    terms = lax.all_to_all(terms, "c", split_axis=2, concat_axis=0)
    terms = sum_parts(terms).astype(BF16)
    terms = lax.all_to_all(terms, ("zh", "y"), split_axis=1, concat_axis=0)
    return sum_parts(terms).astype(BF16)


def shards(
    teacher_in,
    teacher_gain,
    qkv_weight,
    qk_gain,
    student_in,
    student_gain,
    up_weight,
    down_weight,
    projector,
):
    tok_rows = teacher_in.shape[0]

    first = lax.axis_index("c") == 0
    weight = qkv_weight.reshape(192, 3, 2, 128).transpose(2, 0, 1, 3).reshape(2, 192, 384)
    near = jnp.where(first, weight, weight[::-1])
    far = flip(near, "zh")
    hi = lax.reduce_precision(teacher_gain, 8, 7)
    mid = lax.reduce_precision(teacher_gain - hi, 8, 7)
    low = teacher_gain - hi - mid
    gain_rows = jnp.stack([hi, mid, low] + [jnp.zeros_like(hi)] * 13).astype(BF16)
    shard = tie(jnp.concatenate([teacher_in, gain_rows], axis=0), near)
    pair = jnp.stack([shard, flip(shard, "zl", 1)])

    student_normed = (normalize(student_in.astype(F32)) * student_gain).astype(BF16)
    pre_act = jnp.dot(student_normed, up_weight, preferred_element_type=F32)
    gated, slope = gelu_parts(pre_act)
    activ = gated.astype(BF16)
    mlp_term = jnp.dot(activ, down_weight, preferred_element_type=F32).astype(BF16)

    def by_core(mine, theirs):
        return jnp.where(first, jnp.stack([mine, theirs]), jnp.stack([theirs, mine]))

    part = mp_scatter_x(mlp_term)
    given = flip(jnp.stack([near[1], far[1]]), "c")
    given, part, pair = lax.optimization_barrier((given, part, pair))
    rows = jnp.concatenate([by_core(near[0], given[0]), by_core(far[0], given[1])])
    weight = lax.all_gather(rows, "y").reshape(6144, 384)

    late = flip(pair, "zl", 2)
    pair = spread(pair, "x")
    part = mp_sum_zl(tie(part, rows))
    late, part = lax.optimization_barrier((spread(tie(late, pair), "x"), part))

    place_z = jnp.stack([lax.axis_index("zl"), lax.axis_index("zh")])
    place_c = lax.axis_index("c").reshape(1)
    smem = pl.BlockSpec(memory_space=pltpu.SMEM)
    vmem = pl.BlockSpec(memory_space=pltpu.VMEM)
    params = pltpu.CompilerParams(vmem_limit_bytes=40 * 1024 * 1024)
    normed = pl.pallas_call(
        norm_kernel,
        out_shape=jax.ShapeDtypeStruct((256, 6144), BF16),
        in_specs=[smem] + [vmem] * 2,
        out_specs=vmem,
        compiler_params=params,
        cost_estimate=pl.CostEstimate(
            flops=1000, bytes_accessed=1000, transcendentals=0
        ),
        name="teacher_norm",
    )(place_z, pair, late)
    normed_other = shift(normed, "c", 1)
    mlp_sum = mp_gather_x(tie(part, normed))
    heads = pl.pallas_call(
        attention_kernel,
        out_shape=jax.ShapeDtypeStruct((2, 256, 128), F32),
        in_specs=[smem] + [vmem] * 4,
        out_specs=vmem,
        compiler_params=params,
        cost_estimate=pl.CostEstimate(
            flops=2 * 512 * 6144 * 384, bytes_accessed=11_000_000, transcendentals=131072
        ),
        name="teacher_heads",
    )(place_c, normed, normed_other, weight, qk_gain)
    crossed = shift(heads[1], "c", 1)
    features = jnp.where(
        place_c[0] == 0,
        jnp.concatenate([heads[0], crossed], axis=1),
        jnp.concatenate([crossed, heads[0]], axis=1),
    )

    block_out = (student_in.astype(F32) + mlp_sum.astype(F32)).astype(BF16)
    predicted = jnp.dot(block_out, projector, preferred_element_type=F32)

    local_sum = jnp.sum(features, axis=1)
    local_dev = features - (local_sum / 256)[:, None]
    stats = jnp.stack([local_sum, jnp.sum(local_dev * local_dev, axis=1)])
    feat_mean, feat_var = merge_stats(stats, 256)
    target = (features - feat_mean[:, None]) * lax.rsqrt(feat_var + EPSILON)[:, None]

    loss_factor = 1.0 / math.sqrt(tok_rows * 32)
    grad_pred = ((predicted - target) * loss_factor).astype(BF16)
    block_term = jnp.einsum("tf,cf->tc", grad_pred, projector, preferred_element_type=F32)
    proj_term = jnp.einsum("tc,tf->cf", block_out, grad_pred, preferred_element_type=F32)
    grad_block = mp_scatter_zl(mp_scatter_x(block_term.astype(BF16)))
    grad_block = mp_gather_x(mp_gather_zl(grad_block))
    down_term = jnp.einsum("tc,tf->cf", grad_block, activ, preferred_element_type=F32)
    grad_act = jnp.einsum("tc,fc->tf", grad_block, down_weight, preferred_element_type=F32)
    grad_pre = (grad_act * slope).astype(BF16)
    up_term = jnp.einsum("tc,tf->cf", student_normed, grad_pre, preferred_element_type=F32)
    terms = jnp.stack([t.astype(BF16) for t in (up_term, down_term, proj_term)])
    grad_up, grad_down, grad_projector = reduce_dp(terms)
    return grad_up, grad_down.T, grad_projector


def solution(mesh):
    fine = Mesh(mesh.devices.reshape(tuple(SIZES.values())), tuple(SIZES))
    in_specs = (
        P(DP, MP),
        P(MP),
        P(DP, None, MP),
        P(MP, None),
        P(DP, None),
        P(),
        P(None, MP),
        P(MP, None),
        P(None, MP),
    )
    out_specs = (P(DP, MP), P(MP, DP), P(DP, MP))
    return jax.shard_map(shards, mesh=fine, in_specs=in_specs, out_specs=out_specs, check_vma=False)
```

```python
import math

import jax
import jax.numpy as jnp
from jax import lax
from jax.experimental import pallas as pl
from jax.experimental.pallas import tpu as pltpu
from jax.sharding import Mesh, PartitionSpec as P

HEAD = 128
PATCH = 256
EPSILON = 1e-06
F32 = jnp.float32
BF16 = jnp.bfloat16

SIZES = {"zh": 2, "y": 8, "c": 2, "zl": 4, "x": 4}
DP = ("zh", "y", "c")
MP = ("zl", "x")


def normalize(values):
    row_mean = jnp.mean(values, axis=-1, keepdims=True)
    centered = values - row_mean
    row_var = jnp.mean(centered * centered, axis=-1, keepdims=True)
    return centered * lax.rsqrt(row_var + EPSILON)


def gelu_parts(pre_act):
    cdf_part = 0.5 * (1.0 + lax.erf(pre_act * 0.7071067811865476))
    density = jnp.exp(-0.5 * pre_act * pre_act) * 0.3989422804014327
    return (pre_act * cdf_part, cdf_part + pre_act * density)


def shift(values, axis, step):
    size = SIZES[axis]
    return lax.ppermute(values, axis, [(i, (i + step) % size) for i in range(size)])


def flip(values, axes, bits=1):
    return lax.ppermute(values, axes, [(i, i ^ bits) for i in range(SIZES[axes])])


def tie(values, *others):
    return lax.optimization_barrier((values, *others))[0]


def swap(values, axis):
    return lax.all_to_all(values, axis, split_axis=0, concat_axis=0)


def spread(values, axis):
    return swap(jnp.broadcast_to(values[None], (SIZES[axis],) + values.shape), axis)


def sum_parts(parts):
    return jnp.sum(parts.astype(F32), axis=0)


def mp_scatter_x(term):
    rows, cols = term.shape
    return sum_parts(swap(term.reshape(4, rows // 4, cols), "x")).astype(BF16)


def mp_sum_zl(part):
    for bits in (1, 2):
        part = (part.astype(F32) + flip(part, "zl", bits).astype(F32)).astype(BF16)
    return part


def mp_gather_x(part):
    rows, cols = part.shape
    return spread(part, "x").reshape(4 * rows, cols)


def merge_stats(stats, count):
    parts = swap(jnp.broadcast_to(stats[None], (16,) + stats.shape), MP)
    total = jnp.sum(parts[:, 0], axis=0)
    mean = total / (count * 16)
    moved = parts[:, 0] / count - mean[None]
    spreads = jnp.sum(parts[:, 1], axis=0) + count * jnp.sum(moved * moved, axis=0)
    return mean, spreads / (count * 16)


def norm_kernel(place, pair_ref, late_ref, n_ref):
    my_zl, my_zh = place[0], place[1]
    blocks = []
    for dz in range(4):
        for x in range(4):
            blocks.append(((pair_ref, late_ref)[dz % 2], (x, dz // 2), dz, x))
    width = 16 * 384

    def fold(values):
        return values[:, :128] + values[:, 128:256] + values[:, 256:]

    @pl.loop(0, 8)
    def _(t):
        rows = pl.ds(pl.multiple_of(t * 32, 32), 32)
        total = jnp.zeros((32, 128), F32)
        for ref, (i, j), dz, x in blocks:
            total += fold(ref[i, j, rows, :].astype(F32))
        mean = jnp.sum(total, axis=1, keepdims=True) / width
        total = jnp.zeros((32, 128), F32)
        for ref, (i, j), dz, x in blocks:
            d = ref[i, j, rows, :].astype(F32) - mean
            total += fold(d * d)
        rstd = lax.rsqrt(jnp.sum(total, axis=1, keepdims=True) / width + EPSILON)
        for ref, (i, j), dz, x in blocks:
            gains = ref[i, j, 256:272, :].astype(F32)
            gain = gains[0:1] + gains[1:2] + gains[2:3]
            zl = my_zl ^ dz
            spot = ((zl & 1) * 4 + x) * 2 + ((zl >> 1) ^ my_zh)
            d = ref[i, j, rows, :].astype(F32) - mean
            n_ref[rows, pl.ds(pl.multiple_of(spot * 384, 128), 384)] = (
                d * rstd * gain
            ).astype(BF16)


def attention_kernel(place, own_ref, other_ref, w_ref, qg_ref, f_ref):
    gain = jnp.where(place[0] == 0, qg_ref[0:1, :], qg_ref[1:2, :])
    for image, ref in enumerate((own_ref, other_ref)):
        projected = jnp.dot(ref[...], w_ref[...], preferred_element_type=F32)
        query = (normalize(projected[:, :128]) * gain).astype(BF16)
        key = (normalize(projected[:, 128:256]) * gain).astype(BF16)
        value = projected[:, 256:].astype(BF16)
        scores = lax.dot_general(
            query, key, (((1,), (1,)), ((), ())), preferred_element_type=F32
        ) * (HEAD ** (-0.5))
        scores = jnp.exp(scores - jnp.max(scores, axis=1, keepdims=True))
        attn = (scores / jnp.sum(scores, axis=1, keepdims=True)).astype(BF16)
        f_ref[image] = jnp.dot(attn, value, preferred_element_type=F32)


def reduce_dp(terms):
    k = terms.shape[0]
    terms = terms.reshape(k, 16, 2, 32, 256)
    terms = lax.all_to_all(terms, "c", split_axis=2, concat_axis=0)
    terms = sum_parts(terms).astype(BF16)
    terms = lax.all_to_all(terms, ("zh", "y"), split_axis=1, concat_axis=0)
    return sum_parts(terms).astype(BF16)


def shards(
    teacher_in,
    teacher_gain,
    qkv_weight,
    qk_gain,
    student_in,
    student_gain,
    up_weight,
    down_weight,
    projector,
):
    tok_rows = teacher_in.shape[0]

    first = lax.axis_index("c") == 0
    weight = qkv_weight.reshape(192, 3, 2, 128).transpose(2, 0, 1, 3).reshape(2, 192, 384)
    near = jnp.where(first, weight, weight[::-1])
    far = flip(near, "zh")
    hi = lax.reduce_precision(teacher_gain, 8, 7)
    mid = lax.reduce_precision(teacher_gain - hi, 8, 7)
    low = teacher_gain - hi - mid
    gain_rows = jnp.stack([hi, mid, low] + [jnp.zeros_like(hi)] * 13).astype(BF16)
    shard = tie(jnp.concatenate([teacher_in, gain_rows], axis=0), near)
    pair = jnp.stack([shard, flip(shard, "zl", 2)])

    student_normed = (normalize(student_in.astype(F32)) * student_gain).astype(BF16)
    pre_act = jnp.dot(student_normed, up_weight, preferred_element_type=F32)
    gated, slope = gelu_parts(pre_act)
    activ = gated.astype(BF16)
    mlp_term = jnp.dot(activ, down_weight, preferred_element_type=F32).astype(BF16)

    def by_core(mine, theirs):
        return jnp.where(first, jnp.stack([mine, theirs]), jnp.stack([theirs, mine]))

    part = mp_scatter_x(mlp_term)
    given = flip(jnp.stack([near[1], far[1]]), "c")
    given, part, pair = lax.optimization_barrier((given, part, pair))
    rows = jnp.concatenate([by_core(near[0], given[0]), by_core(far[0], given[1])])
    weight = lax.all_gather(rows, "y").reshape(6144, 384)

    late = flip(pair, "zl", 1)
    pair = spread(pair, "x")
    part = mp_sum_zl(tie(part, rows))
    late, part = lax.optimization_barrier((spread(tie(late, pair), "x"), part))

    place_z = jnp.stack([lax.axis_index("zl"), lax.axis_index("zh")])
    place_c = lax.axis_index("c").reshape(1)
    smem = pl.BlockSpec(memory_space=pltpu.SMEM)
    vmem = pl.BlockSpec(memory_space=pltpu.VMEM)
    params = pltpu.CompilerParams(vmem_limit_bytes=40 * 1024 * 1024)
    normed = pl.pallas_call(
        norm_kernel,
        out_shape=jax.ShapeDtypeStruct((256, 6144), BF16),
        in_specs=[smem] + [vmem] * 2,
        out_specs=vmem,
        compiler_params=params,
        cost_estimate=pl.CostEstimate(
            flops=1000, bytes_accessed=1000, transcendentals=0
        ),
        name="teacher_norm",
    )(place_z, pair, late)
    normed_other = shift(normed, "c", 1)
    mlp_sum = mp_gather_x(tie(part, normed))
    heads = pl.pallas_call(
        attention_kernel,
        out_shape=jax.ShapeDtypeStruct((2, 256, 128), F32),
        in_specs=[smem] + [vmem] * 4,
        out_specs=vmem,
        compiler_params=params,
        cost_estimate=pl.CostEstimate(
            flops=2 * 512 * 6144 * 384, bytes_accessed=11_000_000, transcendentals=131072
        ),
        name="teacher_heads",
    )(place_c, normed, normed_other, weight, qk_gain)
    crossed = shift(heads[1], "c", 1)
    features = jnp.where(
        place_c[0] == 0,
        jnp.concatenate([heads[0], crossed], axis=1),
        jnp.concatenate([crossed, heads[0]], axis=1),
    )

    block_out = (student_in.astype(F32) + mlp_sum.astype(F32)).astype(BF16)
    predicted = jnp.dot(block_out, projector, preferred_element_type=F32)

    local_sum = jnp.sum(features, axis=1)
    local_dev = features - (local_sum / 256)[:, None]
    stats = jnp.stack([local_sum, jnp.sum(local_dev * local_dev, axis=1)])
    feat_mean, feat_var = merge_stats(stats, 256)
    target = (features - feat_mean[:, None]) * lax.rsqrt(feat_var + EPSILON)[:, None]

    loss_factor = 1.0 / math.sqrt(tok_rows * 32)
    grad_pred = ((predicted - target) * loss_factor).astype(BF16)
    block_term = jnp.einsum("tf,cf->tc", grad_pred, projector, preferred_element_type=F32)
    proj_term = jnp.einsum("tc,tf->cf", block_out, grad_pred, preferred_element_type=F32)
    grad_block = mp_gather_x(mp_sum_zl(mp_scatter_x(block_term.astype(BF16))))
    down_term = jnp.einsum("tc,tf->cf", grad_block, activ, preferred_element_type=F32)
    grad_act = jnp.einsum("tc,fc->tf", grad_block, down_weight, preferred_element_type=F32)
    grad_pre = (grad_act * slope).astype(BF16)
    up_term = jnp.einsum("tc,tf->cf", student_normed, grad_pre, preferred_element_type=F32)
    terms = jnp.stack([t.astype(BF16) for t in (up_term, down_term, proj_term)])
    grad_up, grad_down, grad_projector = reduce_dp(terms)
    return grad_up, grad_down.T, grad_projector


def solution(mesh):
    fine = Mesh(mesh.devices.reshape(tuple(SIZES.values())), tuple(SIZES))
    in_specs = (
        P(DP, MP),
        P(MP),
        P(DP, None, MP),
        P(MP, None),
        P(DP, None),
        P(),
        P(None, MP),
        P(MP, None),
        P(None, MP),
    )
    out_specs = (P(DP, MP), P(MP, DP), P(DP, MP))
    return jax.shard_map(shards, mesh=fine, in_specs=in_specs, out_specs=out_specs, check_vma=False)
```

```python
import math

import jax
import jax.numpy as jnp
from jax import lax
from jax.experimental import pallas as pl
from jax.experimental.pallas import tpu as pltpu
from jax.sharding import Mesh, PartitionSpec as P

HEAD = 128
PATCH = 256
EPSILON = 1e-06
F32 = jnp.float32
BF16 = jnp.bfloat16

SIZES = {"zh": 2, "y": 8, "c": 2, "zl": 4, "x": 4}
DP = ("zh", "y", "c")
MP = ("zl", "x")


def normalize(values):
    row_mean = jnp.mean(values, axis=-1, keepdims=True)
    centered = values - row_mean
    row_var = jnp.mean(centered * centered, axis=-1, keepdims=True)
    return centered * lax.rsqrt(row_var + EPSILON)


def gelu_parts(pre_act):
    cdf_part = 0.5 * (1.0 + lax.erf(pre_act * 0.7071067811865476))
    density = jnp.exp(-0.5 * pre_act * pre_act) * 0.3989422804014327
    return (pre_act * cdf_part, cdf_part + pre_act * density)


def shift(values, axis, step):
    size = SIZES[axis]
    return lax.ppermute(values, axis, [(i, (i + step) % size) for i in range(size)])


def flip(values, axes, bits=1):
    return lax.ppermute(values, axes, [(i, i ^ bits) for i in range(SIZES[axes])])


def tie(values, *others):
    return lax.optimization_barrier((values, *others))[0]


def swap(values, axis):
    return lax.all_to_all(values, axis, split_axis=0, concat_axis=0)


def spread(values, axis):
    return swap(jnp.broadcast_to(values[None], (SIZES[axis],) + values.shape), axis)


def sum_parts(parts):
    return jnp.sum(parts.astype(F32), axis=0)


def mp_scatter_x(term):
    rows, cols = term.shape
    return sum_parts(swap(term.reshape(4, rows // 4, cols), "x")).astype(BF16)


def mp_scatter_x_beside(term):
    rows, cols = term.shape
    term = term.reshape(4, rows // 4, cols)
    x = lax.axis_index("x")
    total = lax.dynamic_index_in_dim(term, x, 0, False).astype(F32)
    for bits in (1, 2, 3):
        given = lax.dynamic_index_in_dim(term, x ^ bits, 0, False)
        total += flip(given, "x", bits).astype(F32)
    return total.astype(BF16)


def mp_sum_zl(part):
    for bits in (1, 2):
        part = (part.astype(F32) + flip(part, "zl", bits).astype(F32)).astype(BF16)
    return part


def mp_gather_x(part):
    rows, cols = part.shape
    return spread(part, "x").reshape(4 * rows, cols)


def merge_stats(stats, count):
    parts = swap(jnp.broadcast_to(stats[None], (16,) + stats.shape), MP)
    total = jnp.sum(parts[:, 0], axis=0)
    mean = total / (count * 16)
    moved = parts[:, 0] / count - mean[None]
    spreads = jnp.sum(parts[:, 1], axis=0) + count * jnp.sum(moved * moved, axis=0)
    return mean, spreads / (count * 16)


def norm_kernel(place, own_ref, near_ref, late_ref, n_ref, gain_ref):
    my_zl, my_zh = place[0], place[1]
    blocks = []
    for x in range(4):
        blocks.append((own_ref, (x,), 0, x))
        blocks.append((near_ref, (x,), 1, x))
        blocks.append((late_ref, (x, 0), 2, x))
        blocks.append((late_ref, (x, 1), 3, x))
    for k, (ref, at, dz, x) in enumerate(blocks):
        gains = ref[(*at, slice(256, 272), slice(None))].astype(F32)
        gain_ref[k : k + 1, :] = gains[0:1] + gains[1:2] + gains[2:3]
    width = 16 * 384

    def fold(values):
        return values[:, :128] + values[:, 128:256] + values[:, 256:]

    @pl.loop(0, 8)
    def _(t):
        rows = pl.ds(pl.multiple_of(t * 32, 32), 32)

        def read(ref, at):
            return ref[(*at, rows, slice(None))].astype(F32)

        total = jnp.zeros((32, 128), F32)
        for ref, at, dz, x in blocks:
            total += fold(read(ref, at))
        mean = jnp.sum(total, axis=1, keepdims=True) / width
        total = jnp.zeros((32, 128), F32)
        for ref, at, dz, x in blocks:
            d = read(ref, at) - mean
            total += fold(d * d)
        rstd = lax.rsqrt(jnp.sum(total, axis=1, keepdims=True) / width + EPSILON)
        for k, (ref, at, dz, x) in enumerate(blocks):
            zl = my_zl ^ dz
            spot = ((zl & 1) * 4 + x) * 2 + ((zl >> 1) ^ my_zh)
            n_ref[rows, pl.ds(pl.multiple_of(spot * 384, 128), 384)] = (
                (read(ref, at) - mean) * rstd * gain_ref[k : k + 1, :]
            ).astype(BF16)


def attention_kernel(place, n_ref, w_ref, qg_ref, f_ref):
    gain = jnp.where(place[0] == 0, qg_ref[0:1, :], qg_ref[1:2, :])
    projected = jnp.dot(n_ref[...], w_ref[...], preferred_element_type=F32)
    query = (normalize(projected[:, :128]) * gain).astype(BF16)
    key = (normalize(projected[:, 128:256]) * gain).astype(BF16)
    value = projected[:, 256:].astype(BF16)
    scores = lax.dot_general(
        query, key, (((1,), (1,)), ((), ())), preferred_element_type=F32
    ) * (HEAD ** (-0.5))
    scores = jnp.exp(scores - jnp.max(scores, axis=1, keepdims=True))
    attn = (scores / jnp.sum(scores, axis=1, keepdims=True)).astype(BF16)
    f_ref[...] = jnp.dot(attn, value, preferred_element_type=F32)


def reduce_dp(terms):
    k = terms.shape[0]
    terms = terms.reshape(k, 16, 2, 32, 256)
    terms = lax.all_to_all(terms, "c", split_axis=2, concat_axis=0)
    terms = sum_parts(terms).astype(BF16)
    terms = lax.all_to_all(terms, ("zh", "y"), split_axis=1, concat_axis=0)
    return sum_parts(terms).astype(BF16)


def shards(
    teacher_in,
    teacher_gain,
    qkv_weight,
    qk_gain,
    student_in,
    student_gain,
    up_weight,
    down_weight,
    projector,
):
    tok_rows = teacher_in.shape[0]

    first = lax.axis_index("c") == 0
    weight = qkv_weight.reshape(192, 3, 2, 128).transpose(2, 0, 1, 3).reshape(2, 192, 384)
    near = jnp.where(first, weight, weight[::-1])
    far = flip(near, "zh")
    hi = lax.reduce_precision(teacher_gain, 8, 7)
    mid = lax.reduce_precision(teacher_gain - hi, 8, 7)
    low = teacher_gain - hi - mid
    gain_rows = jnp.stack([hi, mid, low] + [jnp.zeros_like(hi)] * 13).astype(BF16)
    shard = tie(jnp.concatenate([teacher_in, gain_rows], axis=0), near)
    own = spread(shard, "x")
    near_block = flip(shard, "zl", 1)

    student_normed = (normalize(student_in.astype(F32)) * student_gain).astype(BF16)
    pre_act = jnp.dot(student_normed, up_weight, preferred_element_type=F32)
    gated, slope = gelu_parts(pre_act)
    activ = gated.astype(BF16)
    mlp_term = jnp.dot(activ, down_weight, preferred_element_type=F32).astype(BF16)

    def by_core(mine, theirs):
        return jnp.where(first, jnp.stack([mine, theirs]), jnp.stack([theirs, mine]))

    given = flip(jnp.stack([near[1], far[1]]), "c")
    given, own, near_block, mlp_term = lax.optimization_barrier(
        (given, own, near_block, mlp_term)
    )
    rows = jnp.concatenate([by_core(near[0], given[0]), by_core(far[0], given[1])])
    weight = lax.all_gather(rows, "y").reshape(6144, 384)

    late = flip(jnp.stack([shard, near_block]), "zl", 2)
    near_block = spread(near_block, "x")
    part = mp_scatter_x_beside(tie(mlp_term, rows))
    late, part = lax.optimization_barrier((late, part))
    part = mp_sum_zl(part)
    late, part = lax.optimization_barrier((spread(tie(late, near_block), "x"), part))

    place_z = jnp.stack([lax.axis_index("zl"), lax.axis_index("zh")])
    place_c = lax.axis_index("c").reshape(1)
    smem = pl.BlockSpec(memory_space=pltpu.SMEM)
    vmem = pl.BlockSpec(memory_space=pltpu.VMEM)
    params = pltpu.CompilerParams(vmem_limit_bytes=40 * 1024 * 1024)
    normed = pl.pallas_call(
        norm_kernel,
        out_shape=jax.ShapeDtypeStruct((256, 6144), BF16),
        scratch_shapes=[pltpu.VMEM((16, 384), F32)],
        in_specs=[smem] + [vmem] * 3,
        out_specs=vmem,
        compiler_params=params,
        cost_estimate=pl.CostEstimate(
            flops=1000, bytes_accessed=1000, transcendentals=0
        ),
        name="teacher_norm",
    )(place_z, own, near_block, late)
    normed_other = shift(normed, "c", 1)
    mlp_sum = mp_gather_x(tie(part, normed))
    heads = pl.pallas_call(
        attention_kernel,
        out_shape=jax.ShapeDtypeStruct((256, 128), F32),
        in_specs=[smem] + [vmem] * 3,
        out_specs=vmem,
        compiler_params=params,
        cost_estimate=pl.CostEstimate(
            flops=2 * 256 * 6144 * 384, bytes_accessed=8_000_000, transcendentals=65536
        ),
        name="teacher_heads",
    )
    crossed = shift(heads(place_c, normed_other, weight, qk_gain), "c", 1)
    kept = heads(place_c, normed, weight, qk_gain)
    features = jnp.where(
        place_c[0] == 0,
        jnp.concatenate([kept, crossed], axis=1),
        jnp.concatenate([crossed, kept], axis=1),
    )

    block_out = (student_in.astype(F32) + mlp_sum.astype(F32)).astype(BF16)
    predicted = jnp.dot(block_out, projector, preferred_element_type=F32)

    local_sum = jnp.sum(features, axis=1)
    local_dev = features - (local_sum / 256)[:, None]
    stats = jnp.stack([local_sum, jnp.sum(local_dev * local_dev, axis=1)])
    feat_mean, feat_var = merge_stats(stats, 256)
    target = (features - feat_mean[:, None]) * lax.rsqrt(feat_var + EPSILON)[:, None]

    loss_factor = 1.0 / math.sqrt(tok_rows * 32)
    grad_pred = ((predicted - target) * loss_factor).astype(BF16)
    block_term = jnp.einsum("tf,cf->tc", grad_pred, projector, preferred_element_type=F32)
    proj_term = jnp.einsum("tc,tf->cf", block_out, grad_pred, preferred_element_type=F32)
    grad_block = mp_gather_x(mp_sum_zl(mp_scatter_x(block_term.astype(BF16))))
    down_term = jnp.einsum("tc,tf->cf", grad_block, activ, preferred_element_type=F32)
    grad_act = jnp.einsum("tc,fc->tf", grad_block, down_weight, preferred_element_type=F32)
    grad_pre = (grad_act * slope).astype(BF16)
    up_term = jnp.einsum("tc,tf->cf", student_normed, grad_pre, preferred_element_type=F32)
    terms = jnp.stack([t.astype(BF16) for t in (up_term, down_term, proj_term)])
    grad_up, grad_down, grad_projector = reduce_dp(terms)
    return grad_up, grad_down.T, grad_projector


def solution(mesh):
    fine = Mesh(mesh.devices.reshape(tuple(SIZES.values())), tuple(SIZES))
    in_specs = (
        P(DP, MP),
        P(MP),
        P(DP, None, MP),
        P(MP, None),
        P(DP, None),
        P(),
        P(None, MP),
        P(MP, None),
        P(None, MP),
    )
    out_specs = (P(DP, MP), P(MP, DP), P(DP, MP))
    return jax.shard_map(shards, mesh=fine, in_specs=in_specs, out_specs=out_specs, check_vma=False)
```

```python
import math

import jax
import jax.numpy as jnp
from jax import lax
from jax.experimental import pallas as pl
from jax.experimental.pallas import tpu as pltpu
from jax.sharding import Mesh, PartitionSpec as P

HEAD = 128
PATCH = 256
EPSILON = 1e-06
F32 = jnp.float32
BF16 = jnp.bfloat16

SIZES = {"zh": 2, "y": 8, "c": 2, "zl": 4, "x": 4}
DP = ("zh", "y", "c")
MP = ("zl", "x")


def normalize(values):
    row_mean = jnp.mean(values, axis=-1, keepdims=True)
    centered = values - row_mean
    row_var = jnp.mean(centered * centered, axis=-1, keepdims=True)
    return centered * lax.rsqrt(row_var + EPSILON)


def gelu_parts(pre_act):
    cdf_part = 0.5 * (1.0 + lax.erf(pre_act * 0.7071067811865476))
    density = jnp.exp(-0.5 * pre_act * pre_act) * 0.3989422804014327
    return (pre_act * cdf_part, cdf_part + pre_act * density)


def shift(values, axis, step):
    size = SIZES[axis]
    return lax.ppermute(values, axis, [(i, (i + step) % size) for i in range(size)])


def flip(values, axes, bits=1):
    return lax.ppermute(values, axes, [(i, i ^ bits) for i in range(SIZES[axes])])


def tie(values, *others):
    return lax.optimization_barrier((values, *others))[0]


def swap(values, axis):
    return lax.all_to_all(values, axis, split_axis=0, concat_axis=0)


def spread(values, axis):
    return swap(jnp.broadcast_to(values[None], (SIZES[axis],) + values.shape), axis)


def sum_parts(parts):
    return jnp.sum(parts.astype(F32), axis=0)


def mp_scatter_x(term):
    rows, cols = term.shape
    return sum_parts(swap(term.reshape(4, rows // 4, cols), "x")).astype(BF16)


def mp_scatter_x_beside(term):
    rows, cols = term.shape
    term = term.reshape(4, rows // 4, cols)
    x = lax.axis_index("x")
    total = lax.dynamic_index_in_dim(term, x, 0, False).astype(F32)
    for bits in (1, 2, 3):
        given = lax.dynamic_index_in_dim(term, x ^ bits, 0, False)
        total += flip(given, "x", bits).astype(F32)
    return total.astype(BF16)


def mp_sum_zl(part):
    for bits in (1, 2):
        part = (part.astype(F32) + flip(part, "zl", bits).astype(F32)).astype(BF16)
    return part


def mp_gather_x(part):
    rows, cols = part.shape
    return spread(part, "x").reshape(4 * rows, cols)


def merge_stats(stats, count):
    parts = swap(jnp.broadcast_to(stats[None], (16,) + stats.shape), MP)
    total = jnp.sum(parts[:, 0], axis=0)
    mean = total / (count * 16)
    moved = parts[:, 0] / count - mean[None]
    spreads = jnp.sum(parts[:, 1], axis=0) + count * jnp.sum(moved * moved, axis=0)
    return mean, spreads / (count * 16)


def norm_kernel(place, own_ref, far_ref, late_ref, n_ref, gain_ref):
    my_zl, my_zh = place[0], place[1]
    blocks = []
    for x in range(4):
        blocks.append((own_ref, (x,), 0, x))
        blocks.append((far_ref, (x,), 2, x))
        blocks.append((late_ref, (x, 0), 1, x))
        blocks.append((late_ref, (x, 1), 3, x))
    for k, (ref, at, dz, x) in enumerate(blocks):
        gains = ref[(*at, slice(256, 272), slice(None))].astype(F32)
        gain_ref[k : k + 1, :] = gains[0:1] + gains[1:2] + gains[2:3]
    width = 16 * 384

    def fold(values):
        return values[:, :128] + values[:, 128:256] + values[:, 256:]

    @pl.loop(0, 8)
    def _(t):
        rows = pl.ds(pl.multiple_of(t * 32, 32), 32)

        def read(ref, at):
            return ref[(*at, rows, slice(None))].astype(F32)

        total = jnp.zeros((32, 128), F32)
        for ref, at, dz, x in blocks:
            total += fold(read(ref, at))
        mean = jnp.sum(total, axis=1, keepdims=True) / width
        total = jnp.zeros((32, 128), F32)
        for ref, at, dz, x in blocks:
            d = read(ref, at) - mean
            total += fold(d * d)
        rstd = lax.rsqrt(jnp.sum(total, axis=1, keepdims=True) / width + EPSILON)
        for k, (ref, at, dz, x) in enumerate(blocks):
            zl = my_zl ^ dz
            spot = ((zl & 1) * 4 + x) * 2 + ((zl >> 1) ^ my_zh)
            n_ref[rows, pl.ds(pl.multiple_of(spot * 384, 128), 384)] = (
                (read(ref, at) - mean) * rstd * gain_ref[k : k + 1, :]
            ).astype(BF16)


def attention_kernel(place, own_ref, other_ref, w_ref, qg_ref, f_ref):
    gain = jnp.where(place[0] == 0, qg_ref[0:1, :], qg_ref[1:2, :])
    for image, ref in enumerate((own_ref, other_ref)):
        projected = jnp.dot(ref[...], w_ref[...], preferred_element_type=F32)
        query = (normalize(projected[:, :128]) * gain).astype(BF16)
        key = (normalize(projected[:, 128:256]) * gain).astype(BF16)
        value = projected[:, 256:].astype(BF16)
        scores = lax.dot_general(
            query, key, (((1,), (1,)), ((), ())), preferred_element_type=F32
        ) * (HEAD ** (-0.5))
        scores = jnp.exp(scores - jnp.max(scores, axis=1, keepdims=True))
        attn = (scores / jnp.sum(scores, axis=1, keepdims=True)).astype(BF16)
        f_ref[image] = jnp.dot(attn, value, preferred_element_type=F32)


def reduce_dp(terms):
    k = terms.shape[0]
    terms = terms.reshape(k, 16, 2, 32, 256)
    terms = lax.all_to_all(terms, "c", split_axis=2, concat_axis=0)
    terms = sum_parts(terms).astype(BF16)
    terms = lax.all_to_all(terms, ("zh", "y"), split_axis=1, concat_axis=0)
    return sum_parts(terms).astype(BF16)


def shards(
    teacher_in,
    teacher_gain,
    qkv_weight,
    qk_gain,
    student_in,
    student_gain,
    up_weight,
    down_weight,
    projector,
):
    tok_rows = teacher_in.shape[0]

    first = lax.axis_index("c") == 0
    weight = qkv_weight.reshape(192, 3, 2, 128).transpose(2, 0, 1, 3).reshape(2, 192, 384)
    near = jnp.where(first, weight, weight[::-1])
    far = flip(near, "zh")
    hi = lax.reduce_precision(teacher_gain, 8, 7)
    mid = lax.reduce_precision(teacher_gain - hi, 8, 7)
    low = teacher_gain - hi - mid
    gain_rows = jnp.stack([hi, mid, low] + [jnp.zeros_like(hi)] * 13).astype(BF16)
    shard = tie(jnp.concatenate([teacher_in, gain_rows], axis=0), near)
    own = spread(shard, "x")
    far_block = flip(shard, "zl", 2)

    student_normed = (normalize(student_in.astype(F32)) * student_gain).astype(BF16)
    pre_act = jnp.dot(student_normed, up_weight, preferred_element_type=F32)
    gated, slope = gelu_parts(pre_act)
    activ = gated.astype(BF16)
    mlp_term = jnp.dot(activ, down_weight, preferred_element_type=F32).astype(BF16)

    def by_core(mine, theirs):
        return jnp.where(first, jnp.stack([mine, theirs]), jnp.stack([theirs, mine]))

    given = flip(jnp.stack([near[1], far[1]]), "c")
    given, own, far_block, mlp_term = lax.optimization_barrier(
        (given, own, far_block, mlp_term)
    )
    rows = jnp.concatenate([by_core(near[0], given[0]), by_core(far[0], given[1])])
    weight = lax.all_gather(rows, "y").reshape(6144, 384)

    late = flip(jnp.stack([shard, far_block]), "zl", 1)
    far_block = spread(far_block, "x")
    part = mp_scatter_x_beside(tie(mlp_term, rows))
    late, part = lax.optimization_barrier((spread(tie(late, far_block), "x"), part))

    place_z = jnp.stack([lax.axis_index("zl"), lax.axis_index("zh")])
    place_c = lax.axis_index("c").reshape(1)
    smem = pl.BlockSpec(memory_space=pltpu.SMEM)
    vmem = pl.BlockSpec(memory_space=pltpu.VMEM)
    params = pltpu.CompilerParams(vmem_limit_bytes=40 * 1024 * 1024)
    normed = pl.pallas_call(
        norm_kernel,
        out_shape=jax.ShapeDtypeStruct((256, 6144), BF16),
        scratch_shapes=[pltpu.VMEM((16, 384), F32)],
        in_specs=[smem] + [vmem] * 3,
        out_specs=vmem,
        compiler_params=params,
        cost_estimate=pl.CostEstimate(
            flops=1000, bytes_accessed=1000, transcendentals=0
        ),
        name="teacher_norm",
    )(place_z, own, far_block, late)
    normed_other = shift(normed, "c", 1)
    mlp_sum = mp_gather_x(mp_sum_zl(tie(part, normed)))
    heads = pl.pallas_call(
        attention_kernel,
        out_shape=jax.ShapeDtypeStruct((2, 256, 128), F32),
        in_specs=[smem] + [vmem] * 4,
        out_specs=vmem,
        compiler_params=params,
        cost_estimate=pl.CostEstimate(
            flops=2 * 512 * 6144 * 384, bytes_accessed=11_000_000, transcendentals=131072
        ),
        name="teacher_heads",
    )(place_c, normed, normed_other, weight, qk_gain)
    crossed = shift(heads[1], "c", 1)
    features = jnp.where(
        place_c[0] == 0,
        jnp.concatenate([heads[0], crossed], axis=1),
        jnp.concatenate([crossed, heads[0]], axis=1),
    )

    block_out = (student_in.astype(F32) + mlp_sum.astype(F32)).astype(BF16)
    predicted = jnp.dot(block_out, projector, preferred_element_type=F32)

    local_sum = jnp.sum(features, axis=1)
    local_dev = features - (local_sum / 256)[:, None]
    stats = jnp.stack([local_sum, jnp.sum(local_dev * local_dev, axis=1)])
    feat_mean, feat_var = merge_stats(stats, 256)
    target = (features - feat_mean[:, None]) * lax.rsqrt(feat_var + EPSILON)[:, None]

    loss_factor = 1.0 / math.sqrt(tok_rows * 32)
    grad_pred = ((predicted - target) * loss_factor).astype(BF16)
    block_term = jnp.einsum("tf,cf->tc", grad_pred, projector, preferred_element_type=F32)
    proj_term = jnp.einsum("tc,tf->cf", block_out, grad_pred, preferred_element_type=F32)
    grad_block = mp_gather_x(mp_sum_zl(mp_scatter_x(block_term.astype(BF16))))
    down_term = jnp.einsum("tc,tf->cf", grad_block, activ, preferred_element_type=F32)
    grad_act = jnp.einsum("tc,fc->tf", grad_block, down_weight, preferred_element_type=F32)
    grad_pre = (grad_act * slope).astype(BF16)
    up_term = jnp.einsum("tc,tf->cf", student_normed, grad_pre, preferred_element_type=F32)
    terms = jnp.stack([t.astype(BF16) for t in (up_term, down_term, proj_term)])
    grad_up, grad_down, grad_projector = reduce_dp(terms)
    return grad_up, grad_down.T, grad_projector


def solution(mesh):
    fine = Mesh(mesh.devices.reshape(tuple(SIZES.values())), tuple(SIZES))
    in_specs = (
        P(DP, MP),
        P(MP),
        P(DP, None, MP),
        P(MP, None),
        P(DP, None),
        P(),
        P(None, MP),
        P(MP, None),
        P(None, MP),
    )
    out_specs = (P(DP, MP), P(MP, DP), P(DP, MP))
    return jax.shard_map(shards, mesh=fine, in_specs=in_specs, out_specs=out_specs, check_vma=False)
```

```python
import math

import jax
import jax.numpy as jnp
from jax import lax
from jax.experimental import pallas as pl
from jax.experimental.pallas import tpu as pltpu
from jax.sharding import Mesh, PartitionSpec as P

HEAD = 128
PATCH = 256
EPSILON = 1e-06
F32 = jnp.float32
BF16 = jnp.bfloat16

SIZES = {"zh": 2, "y": 8, "c": 2, "zl": 4, "x": 4}
DP = ("zh", "y", "c")
MP = ("zl", "x")


def normalize(values):
    row_mean = jnp.mean(values, axis=-1, keepdims=True)
    centered = values - row_mean
    row_var = jnp.mean(centered * centered, axis=-1, keepdims=True)
    return centered * lax.rsqrt(row_var + EPSILON)


def gelu_parts(pre_act):
    cdf_part = 0.5 * (1.0 + lax.erf(pre_act * 0.7071067811865476))
    density = jnp.exp(-0.5 * pre_act * pre_act) * 0.3989422804014327
    return (pre_act * cdf_part, cdf_part + pre_act * density)


def shift(values, axis, step):
    size = SIZES[axis]
    return lax.ppermute(values, axis, [(i, (i + step) % size) for i in range(size)])


def flip(values, axes, bits=1):
    return lax.ppermute(values, axes, [(i, i ^ bits) for i in range(SIZES[axes])])


def tie(values, *others):
    return lax.optimization_barrier((values, *others))[0]


def swap(values, axis):
    return lax.all_to_all(values, axis, split_axis=0, concat_axis=0)


def spread(values, axis):
    return swap(jnp.broadcast_to(values[None], (SIZES[axis],) + values.shape), axis)


def sum_parts(parts):
    return jnp.sum(parts.astype(F32), axis=0)


def mp_scatter_x(term):
    rows, cols = term.shape
    return sum_parts(swap(term.reshape(4, rows // 4, cols), "x")).astype(BF16)


def mp_sum_zl(part):
    for bits in (1, 2):
        part = (part.astype(F32) + flip(part, "zl", bits).astype(F32)).astype(BF16)
    return part


def mp_gather_x(part):
    rows, cols = part.shape
    return spread(part, "x").reshape(4 * rows, cols)


def merge_stats(stats, count):
    parts = swap(jnp.broadcast_to(stats[None], (16,) + stats.shape), MP)
    total = jnp.sum(parts[:, 0], axis=0)
    mean = total / (count * 16)
    moved = parts[:, 0] / count - mean[None]
    spreads = jnp.sum(parts[:, 1], axis=0) + count * jnp.sum(moved * moved, axis=0)
    return mean, spreads / (count * 16)


def norm_kernel(place, pair_ref, late_ref, n_ref, gain_ref):
    my_zl, my_zh = place[0], place[1]
    blocks = []
    for x in range(4):
        blocks.append((pair_ref, (x, 0), 0, x))
        blocks.append((pair_ref, (x, 1), 1, x))
        blocks.append((late_ref, (x, 0), 2, x))
        blocks.append((late_ref, (x, 1), 3, x))
    for k, (ref, at, dz, x) in enumerate(blocks):
        gains = ref[(*at, slice(256, 272), slice(None))].astype(F32)
        gain_ref[k : k + 1, :] = gains[0:1] + gains[1:2] + gains[2:3]
    width = 16 * 384

    def fold(values):
        return values[:, :128] + values[:, 128:256] + values[:, 256:]

    @pl.loop(0, 8)
    def _(t):
        rows = pl.ds(pl.multiple_of(t * 32, 32), 32)

        def read(ref, at):
            return ref[(*at, rows, slice(None))].astype(F32)

        total = jnp.zeros((32, 128), F32)
        for ref, at, dz, x in blocks:
            total += fold(read(ref, at))
        mean = jnp.sum(total, axis=1, keepdims=True) / width
        total = jnp.zeros((32, 128), F32)
        for ref, at, dz, x in blocks:
            d = read(ref, at) - mean
            total += fold(d * d)
        rstd = lax.rsqrt(jnp.sum(total, axis=1, keepdims=True) / width + EPSILON)
        for k, (ref, at, dz, x) in enumerate(blocks):
            zl = my_zl ^ dz
            spot = ((zl & 1) * 4 + x) * 2 + ((zl >> 1) ^ my_zh)
            n_ref[rows, pl.ds(pl.multiple_of(spot * 384, 128), 384)] = (
                (read(ref, at) - mean) * rstd * gain_ref[k : k + 1, :]
            ).astype(BF16)


def attention_kernel(place, own_ref, other_ref, w_ref, qg_ref, f_ref):
    gain = jnp.where(place[0] == 0, qg_ref[0:1, :], qg_ref[1:2, :])
    for image, ref in enumerate((own_ref, other_ref)):
        projected = jnp.dot(ref[...], w_ref[...], preferred_element_type=F32)
        query = (normalize(projected[:, :128]) * gain).astype(BF16)
        key = (normalize(projected[:, 128:256]) * gain).astype(BF16)
        value = projected[:, 256:].astype(BF16)
        scores = lax.dot_general(
            query, key, (((1,), (1,)), ((), ())), preferred_element_type=F32
        ) * (HEAD ** (-0.5))
        scores = jnp.exp(scores - jnp.max(scores, axis=1, keepdims=True))
        attn = (scores / jnp.sum(scores, axis=1, keepdims=True)).astype(BF16)
        f_ref[image] = jnp.dot(attn, value, preferred_element_type=F32)


def reduce_zh(term):
    low = lax.axis_index("zh") == 0
    theirs = flip(jnp.where(low, term[1], term[0]), "zh")
    mine = jnp.where(low, term[0], term[1])
    return (mine.astype(F32) + theirs.astype(F32)).astype(BF16)


def reduce_dp(terms):
    k = terms.shape[0]
    terms = terms.reshape(k, 2, 8, 2, 32, 256)
    terms = lax.all_to_all(terms, "c", split_axis=3, concat_axis=0)
    terms = sum_parts(terms).astype(BF16)
    upper = reduce_zh(terms[:, :, :, :16].transpose(1, 2, 0, 3, 4))
    lower = swap(terms[:, :, :, 16:].transpose(2, 1, 0, 3, 4), "y")
    upper = sum_parts(swap(upper, "y")).astype(BF16)
    lower = reduce_zh(sum_parts(lower).astype(BF16))
    return jnp.concatenate([upper, lower], axis=1)


def shards(
    teacher_in,
    teacher_gain,
    qkv_weight,
    qk_gain,
    student_in,
    student_gain,
    up_weight,
    down_weight,
    projector,
):
    tok_rows = teacher_in.shape[0]

    first = lax.axis_index("c") == 0
    weight = qkv_weight.reshape(192, 3, 2, 128).transpose(2, 0, 1, 3).reshape(2, 192, 384)
    near = jnp.where(first, weight, weight[::-1])
    far = flip(near, "zh")
    hi = lax.reduce_precision(teacher_gain, 8, 7)
    mid = lax.reduce_precision(teacher_gain - hi, 8, 7)
    low = teacher_gain - hi - mid
    gain_rows = jnp.stack([hi, mid, low] + [jnp.zeros_like(hi)] * 13).astype(BF16)
    shard = tie(jnp.concatenate([teacher_in, gain_rows], axis=0), near)
    pair = jnp.stack([shard, flip(shard, "zl", 1)])

    student_normed = (normalize(student_in.astype(F32)) * student_gain).astype(BF16)
    pre_act = jnp.dot(student_normed, up_weight, preferred_element_type=F32)
    gated, slope = gelu_parts(pre_act)
    activ = gated.astype(BF16)
    mlp_term = jnp.dot(activ, down_weight, preferred_element_type=F32).astype(BF16)

    def by_core(mine, theirs):
        return jnp.where(first, jnp.stack([mine, theirs]), jnp.stack([theirs, mine]))

    part = mp_scatter_x(mlp_term)
    given = flip(jnp.stack([near[1], far[1]]), "c")
    given, part, pair = lax.optimization_barrier((given, part, pair))
    rows = jnp.concatenate([by_core(near[0], given[0]), by_core(far[0], given[1])])
    weight = lax.all_gather(rows, "y").reshape(6144, 384)

    late = flip(pair, "zl", 2)
    pair = spread(pair, "x")
    part = mp_sum_zl(tie(part, rows))
    late, part = lax.optimization_barrier((spread(tie(late, pair), "x"), part))

    place_z = jnp.stack([lax.axis_index("zl"), lax.axis_index("zh")])
    place_c = lax.axis_index("c").reshape(1)
    smem = pl.BlockSpec(memory_space=pltpu.SMEM)
    vmem = pl.BlockSpec(memory_space=pltpu.VMEM)
    params = pltpu.CompilerParams(vmem_limit_bytes=40 * 1024 * 1024)
    normed = pl.pallas_call(
        norm_kernel,
        out_shape=jax.ShapeDtypeStruct((256, 6144), BF16),
        scratch_shapes=[pltpu.VMEM((16, 384), F32)],
        in_specs=[smem] + [vmem] * 2,
        out_specs=vmem,
        compiler_params=params,
        cost_estimate=pl.CostEstimate(
            flops=1000, bytes_accessed=1000, transcendentals=0
        ),
        name="teacher_norm",
    )(place_z, pair, late)
    normed_other = shift(normed, "c", 1)
    mlp_sum = mp_gather_x(tie(part, normed))
    heads = pl.pallas_call(
        attention_kernel,
        out_shape=jax.ShapeDtypeStruct((2, 256, 128), F32),
        in_specs=[smem] + [vmem] * 4,
        out_specs=vmem,
        compiler_params=params,
        cost_estimate=pl.CostEstimate(
            flops=2 * 512 * 6144 * 384, bytes_accessed=11_000_000, transcendentals=131072
        ),
        name="teacher_heads",
    )(place_c, normed, normed_other, weight, qk_gain)
    crossed = shift(heads[1], "c", 1)
    features = jnp.where(
        place_c[0] == 0,
        jnp.concatenate([heads[0], crossed], axis=1),
        jnp.concatenate([crossed, heads[0]], axis=1),
    )

    block_out = (student_in.astype(F32) + mlp_sum.astype(F32)).astype(BF16)
    predicted = jnp.dot(block_out, projector, preferred_element_type=F32)

    local_sum = jnp.sum(features, axis=1)
    local_dev = features - (local_sum / 256)[:, None]
    stats = jnp.stack([local_sum, jnp.sum(local_dev * local_dev, axis=1)])
    feat_mean, feat_var = merge_stats(stats, 256)
    target = (features - feat_mean[:, None]) * lax.rsqrt(feat_var + EPSILON)[:, None]

    loss_factor = 1.0 / math.sqrt(tok_rows * 32)
    grad_pred = ((predicted - target) * loss_factor).astype(BF16)
    block_term = jnp.einsum("tf,cf->tc", grad_pred, projector, preferred_element_type=F32)
    proj_term = jnp.einsum("tc,tf->cf", block_out, grad_pred, preferred_element_type=F32)
    grad_block = mp_gather_x(mp_sum_zl(mp_scatter_x(block_term.astype(BF16))))
    down_term = jnp.einsum("tc,tf->cf", grad_block, activ, preferred_element_type=F32)
    grad_act = jnp.einsum("tc,fc->tf", grad_block, down_weight, preferred_element_type=F32)
    grad_pre = (grad_act * slope).astype(BF16)
    up_term = jnp.einsum("tc,tf->cf", student_normed, grad_pre, preferred_element_type=F32)
    terms = jnp.stack([t.astype(BF16) for t in (up_term, down_term, proj_term)])
    grad_up, grad_down, grad_projector = reduce_dp(terms)
    return grad_up, grad_down.T, grad_projector


def solution(mesh):
    fine = Mesh(mesh.devices.reshape(tuple(SIZES.values())), tuple(SIZES))
    in_specs = (
        P(DP, MP),
        P(MP),
        P(DP, None, MP),
        P(MP, None),
        P(DP, None),
        P(),
        P(None, MP),
        P(MP, None),
        P(None, MP),
    )
    out_specs = (P(DP, MP), P(MP, DP), P(DP, MP))
    return jax.shard_map(shards, mesh=fine, in_specs=in_specs, out_specs=out_specs, check_vma=False)
```

```python
import math

import jax
import jax.numpy as jnp
from jax import lax
from jax.experimental import pallas as pl
from jax.experimental.pallas import tpu as pltpu
from jax.sharding import Mesh, PartitionSpec as P

HEAD = 128
PATCH = 256
EPSILON = 1e-06
F32 = jnp.float32
BF16 = jnp.bfloat16

SIZES = {"zh": 2, "y": 8, "c": 2, "zl": 4, "x": 4}
DP = ("zh", "y", "c")
MP = ("zl", "x")


def normalize(values):
    row_mean = jnp.mean(values, axis=-1, keepdims=True)
    centered = values - row_mean
    row_var = jnp.mean(centered * centered, axis=-1, keepdims=True)
    return centered * lax.rsqrt(row_var + EPSILON)


def gelu_parts(pre_act):
    cdf_part = 0.5 * (1.0 + lax.erf(pre_act * 0.7071067811865476))
    density = jnp.exp(-0.5 * pre_act * pre_act) * 0.3989422804014327
    return (pre_act * cdf_part, cdf_part + pre_act * density)


def shift(values, axis, step):
    size = SIZES[axis]
    return lax.ppermute(values, axis, [(i, (i + step) % size) for i in range(size)])


def flip(values, axes, bits=1):
    return lax.ppermute(values, axes, [(i, i ^ bits) for i in range(SIZES[axes])])


def tie(values, *others):
    return lax.optimization_barrier((values, *others))[0]


def swap(values, axis):
    return lax.all_to_all(values, axis, split_axis=0, concat_axis=0)


def spread(values, axis):
    return swap(jnp.broadcast_to(values[None], (SIZES[axis],) + values.shape), axis)


def sum_parts(parts):
    return jnp.sum(parts.astype(F32), axis=0)


def mp_scatter_x(term):
    rows, cols = term.shape
    return sum_parts(swap(term.reshape(4, rows // 4, cols), "x")).astype(BF16)


def spread_and_scatter_x(block, term):
    rows, cols = term.shape
    term = term.reshape(4, rows // 4, 4, cols // 4).transpose(0, 2, 1, 3)
    term = jnp.pad(term.reshape(4, rows, cols // 4), ((0, 0), (0, 16), (0, 0)))
    block = jnp.broadcast_to(block[None], (4,) + block.shape)
    block = swap(jnp.concatenate([block, term], axis=2), "x")
    part = sum_parts(block[:, :rows, 384:]).astype(BF16)
    part = part.reshape(4, rows // 4, cols // 4).transpose(1, 0, 2)
    return block, part.reshape(rows // 4, cols)


def mp_sum_zl(part):
    for bits in (1, 2):
        part = (part.astype(F32) + flip(part, "zl", bits).astype(F32)).astype(BF16)
    return part


def mp_gather_x(part):
    rows, cols = part.shape
    return spread(part, "x").reshape(4 * rows, cols)


def merge_stats(stats, count):
    parts = swap(jnp.broadcast_to(stats[None], (16,) + stats.shape), MP)
    total = jnp.sum(parts[:, 0], axis=0)
    mean = total / (count * 16)
    moved = parts[:, 0] / count - mean[None]
    spreads = jnp.sum(parts[:, 1], axis=0) + count * jnp.sum(moved * moved, axis=0)
    return mean, spreads / (count * 16)


def norm_kernel(place, own_ref, far_ref, late_ref, n_ref, gain_ref):
    my_zl, my_zh = place[0], place[1]
    blocks = []
    for x in range(4):
        blocks.append((own_ref, (x,), 0, x))
        blocks.append((far_ref, (x,), 2, x))
        blocks.append((late_ref, (x, 0), 1, x))
        blocks.append((late_ref, (x, 1), 3, x))
    for k, (ref, at, dz, x) in enumerate(blocks):
        gains = ref[(*at, slice(256, 272), slice(0, 384))].astype(F32)
        gain_ref[k : k + 1, :] = gains[0:1] + gains[1:2] + gains[2:3]
    width = 16 * 384

    def fold(values):
        return values[:, :128] + values[:, 128:256] + values[:, 256:]

    @pl.loop(0, 8)
    def _(t):
        rows = pl.ds(pl.multiple_of(t * 32, 32), 32)

        def read(ref, at):
            return ref[(*at, rows, slice(0, 384))].astype(F32)

        total = jnp.zeros((32, 128), F32)
        for ref, at, dz, x in blocks:
            total += fold(read(ref, at))
        mean = jnp.sum(total, axis=1, keepdims=True) / width
        total = jnp.zeros((32, 128), F32)
        for ref, at, dz, x in blocks:
            d = read(ref, at) - mean
            total += fold(d * d)
        rstd = lax.rsqrt(jnp.sum(total, axis=1, keepdims=True) / width + EPSILON)
        for k, (ref, at, dz, x) in enumerate(blocks):
            zl = my_zl ^ dz
            spot = ((zl & 1) * 4 + x) * 2 + ((zl >> 1) ^ my_zh)
            n_ref[rows, pl.ds(pl.multiple_of(spot * 384, 128), 384)] = (
                (read(ref, at) - mean) * rstd * gain_ref[k : k + 1, :]
            ).astype(BF16)


def attention_kernel(place, own_ref, other_ref, w_ref, qg_ref, f_ref):
    gain = jnp.where(place[0] == 0, qg_ref[0:1, :], qg_ref[1:2, :])
    for image, ref in enumerate((own_ref, other_ref)):
        projected = jnp.dot(ref[...], w_ref[...], preferred_element_type=F32)
        query = (normalize(projected[:, :128]) * gain).astype(BF16)
        key = (normalize(projected[:, 128:256]) * gain).astype(BF16)
        value = projected[:, 256:].astype(BF16)
        scores = lax.dot_general(
            query, key, (((1,), (1,)), ((), ())), preferred_element_type=F32
        ) * (HEAD ** (-0.5))
        scores = jnp.exp(scores - jnp.max(scores, axis=1, keepdims=True))
        attn = (scores / jnp.sum(scores, axis=1, keepdims=True)).astype(BF16)
        f_ref[image] = jnp.dot(attn, value, preferred_element_type=F32)


def reduce_dp(terms):
    k = terms.shape[0]
    terms = terms.reshape(k, 16, 2, 32, 256)
    terms = lax.all_to_all(terms, "c", split_axis=2, concat_axis=0)
    terms = sum_parts(terms).astype(BF16)
    terms = lax.all_to_all(terms, ("zh", "y"), split_axis=1, concat_axis=0)
    return sum_parts(terms).astype(BF16)


def shards(
    teacher_in,
    teacher_gain,
    qkv_weight,
    qk_gain,
    student_in,
    student_gain,
    up_weight,
    down_weight,
    projector,
):
    tok_rows = teacher_in.shape[0]

    first = lax.axis_index("c") == 0
    weight = qkv_weight.reshape(192, 3, 2, 128).transpose(2, 0, 1, 3).reshape(2, 192, 384)
    near = jnp.where(first, weight, weight[::-1])
    far = flip(near, "zh")
    hi = lax.reduce_precision(teacher_gain, 8, 7)
    mid = lax.reduce_precision(teacher_gain - hi, 8, 7)
    low = teacher_gain - hi - mid
    gain_rows = jnp.stack([hi, mid, low] + [jnp.zeros_like(hi)] * 13).astype(BF16)
    shard = tie(jnp.concatenate([teacher_in, gain_rows], axis=0), near)
    own = spread(shard, "x")
    far_block = flip(shard, "zl", 2)

    student_normed = (normalize(student_in.astype(F32)) * student_gain).astype(BF16)
    pre_act = jnp.dot(student_normed, up_weight, preferred_element_type=F32)
    gated, slope = gelu_parts(pre_act)
    activ = gated.astype(BF16)
    mlp_term = jnp.dot(activ, down_weight, preferred_element_type=F32).astype(BF16)

    def by_core(mine, theirs):
        return jnp.where(first, jnp.stack([mine, theirs]), jnp.stack([theirs, mine]))

    given = flip(jnp.stack([near[1], far[1]]), "c")
    given, own, far_block, mlp_term = lax.optimization_barrier(
        (given, own, far_block, mlp_term)
    )
    rows = jnp.concatenate([by_core(near[0], given[0]), by_core(far[0], given[1])])
    weight = lax.all_gather(rows, "y").reshape(6144, 384)

    late = flip(jnp.stack([shard, far_block]), "zl", 1)
    far_block, part = spread_and_scatter_x(far_block, mlp_term)
    late = spread(tie(late, far_block), "x")
    late, part = lax.optimization_barrier((late, mp_sum_zl(part)))

    place_z = jnp.stack([lax.axis_index("zl"), lax.axis_index("zh")])
    place_c = lax.axis_index("c").reshape(1)
    smem = pl.BlockSpec(memory_space=pltpu.SMEM)
    vmem = pl.BlockSpec(memory_space=pltpu.VMEM)
    params = pltpu.CompilerParams(vmem_limit_bytes=40 * 1024 * 1024)
    normed = pl.pallas_call(
        norm_kernel,
        out_shape=jax.ShapeDtypeStruct((256, 6144), BF16),
        scratch_shapes=[pltpu.VMEM((16, 384), F32)],
        in_specs=[smem] + [vmem] * 3,
        out_specs=vmem,
        compiler_params=params,
        cost_estimate=pl.CostEstimate(
            flops=1000, bytes_accessed=1000, transcendentals=0
        ),
        name="teacher_norm",
    )(place_z, own, far_block, late)
    normed_other = shift(normed, "c", 1)
    mlp_sum = mp_gather_x(tie(part, normed))
    heads = pl.pallas_call(
        attention_kernel,
        out_shape=jax.ShapeDtypeStruct((2, 256, 128), F32),
        in_specs=[smem] + [vmem] * 4,
        out_specs=vmem,
        compiler_params=params,
        cost_estimate=pl.CostEstimate(
            flops=2 * 512 * 6144 * 384, bytes_accessed=11_000_000, transcendentals=131072
        ),
        name="teacher_heads",
    )(place_c, normed, normed_other, weight, qk_gain)
    crossed = shift(heads[1], "c", 1)
    features = jnp.where(
        place_c[0] == 0,
        jnp.concatenate([heads[0], crossed], axis=1),
        jnp.concatenate([crossed, heads[0]], axis=1),
    )

    block_out = (student_in.astype(F32) + mlp_sum.astype(F32)).astype(BF16)
    predicted = jnp.dot(block_out, projector, preferred_element_type=F32)

    local_sum = jnp.sum(features, axis=1)
    local_dev = features - (local_sum / 256)[:, None]
    stats = jnp.stack([local_sum, jnp.sum(local_dev * local_dev, axis=1)])
    feat_mean, feat_var = merge_stats(stats, 256)
    target = (features - feat_mean[:, None]) * lax.rsqrt(feat_var + EPSILON)[:, None]

    loss_factor = 1.0 / math.sqrt(tok_rows * 32)
    grad_pred = ((predicted - target) * loss_factor).astype(BF16)
    block_term = jnp.einsum("tf,cf->tc", grad_pred, projector, preferred_element_type=F32)
    proj_term = jnp.einsum("tc,tf->cf", block_out, grad_pred, preferred_element_type=F32)
    grad_block = mp_gather_x(mp_sum_zl(mp_scatter_x(block_term.astype(BF16))))
    down_term = jnp.einsum("tc,tf->cf", grad_block, activ, preferred_element_type=F32)
    grad_act = jnp.einsum("tc,fc->tf", grad_block, down_weight, preferred_element_type=F32)
    grad_pre = (grad_act * slope).astype(BF16)
    up_term = jnp.einsum("tc,tf->cf", student_normed, grad_pre, preferred_element_type=F32)
    terms = jnp.stack([t.astype(BF16) for t in (up_term, down_term, proj_term)])
    grad_up, grad_down, grad_projector = reduce_dp(terms)
    return grad_up, grad_down.T, grad_projector


def solution(mesh):
    fine = Mesh(mesh.devices.reshape(tuple(SIZES.values())), tuple(SIZES))
    in_specs = (
        P(DP, MP),
        P(MP),
        P(DP, None, MP),
        P(MP, None),
        P(DP, None),
        P(),
        P(None, MP),
        P(MP, None),
        P(None, MP),
    )
    out_specs = (P(DP, MP), P(MP, DP), P(DP, MP))
    return jax.shard_map(shards, mesh=fine, in_specs=in_specs, out_specs=out_specs, check_vma=False)
```

```python
import math

import jax
import jax.numpy as jnp
from jax import lax
from jax.experimental import pallas as pl
from jax.experimental.pallas import tpu as pltpu
from jax.sharding import Mesh, PartitionSpec as P

HEAD = 128
PATCH = 256
EPSILON = 1e-06
F32 = jnp.float32
BF16 = jnp.bfloat16

SIZES = {"zh": 2, "y": 8, "c": 2, "zl": 4, "x": 4}
DP = ("zh", "y", "c")
MP = ("zl", "x")


def normalize(values):
    row_mean = jnp.mean(values, axis=-1, keepdims=True)
    centered = values - row_mean
    row_var = jnp.mean(centered * centered, axis=-1, keepdims=True)
    return centered * lax.rsqrt(row_var + EPSILON)


def gelu_parts(pre_act):
    cdf_part = 0.5 * (1.0 + lax.erf(pre_act * 0.7071067811865476))
    density = jnp.exp(-0.5 * pre_act * pre_act) * 0.3989422804014327
    return (pre_act * cdf_part, cdf_part + pre_act * density)


def shift(values, axis, step):
    size = SIZES[axis]
    return lax.ppermute(values, axis, [(i, (i + step) % size) for i in range(size)])


def flip(values, axes, bits=1):
    return lax.ppermute(values, axes, [(i, i ^ bits) for i in range(SIZES[axes])])


def tie(values, *others):
    return lax.optimization_barrier((values, *others))[0]


def swap(values, axis):
    return lax.all_to_all(values, axis, split_axis=0, concat_axis=0)


def spread(values, axis):
    return swap(jnp.broadcast_to(values[None], (SIZES[axis],) + values.shape), axis)


def sum_parts(parts):
    return jnp.sum(parts.astype(F32), axis=0)


def mp_scatter_x(term):
    rows, cols = term.shape
    return sum_parts(swap(term.reshape(4, rows // 4, cols), "x")).astype(BF16)


def spread_and_scatter_x(block, term):
    rows, cols = term.shape
    term = term.reshape(4, rows // 4, 4, cols // 4).transpose(0, 2, 1, 3)
    term = jnp.pad(term.reshape(4, rows, cols // 4), ((0, 0), (0, 16), (0, 0)))
    block = jnp.broadcast_to(block[None], (4,) + block.shape)
    block = swap(jnp.concatenate([block, term], axis=2), "x")
    part = sum_parts(block[:, :rows, 384:]).astype(BF16)
    part = part.reshape(4, rows // 4, cols // 4).transpose(1, 0, 2)
    return block, part.reshape(rows // 4, cols)


def mp_sum_zl(part):
    for bits in (1, 2):
        part = (part.astype(F32) + flip(part, "zl", bits).astype(F32)).astype(BF16)
    return part


def mp_gather_x(part):
    rows, cols = part.shape
    return spread(part, "x").reshape(4 * rows, cols)


def merge_stats(stats, count):
    parts = swap(jnp.broadcast_to(stats[None], (16,) + stats.shape), MP)
    total = jnp.sum(parts[:, 0], axis=0)
    mean = total / (count * 16)
    moved = parts[:, 0] / count - mean[None]
    spreads = jnp.sum(parts[:, 1], axis=0) + count * jnp.sum(moved * moved, axis=0)
    return mean, spreads / (count * 16)


def norm_kernel(place, own_ref, far_ref, late_ref, n_ref, gain_ref):
    my_zl, my_zh = place[0], place[1]
    blocks = []
    for x in range(4):
        blocks.append((own_ref, (x,), 0, x))
        blocks.append((far_ref, (x,), 2, x))
        blocks.append((late_ref, (x, 0), 1, x))
        blocks.append((late_ref, (x, 1), 3, x))
    for k, (ref, at, dz, x) in enumerate(blocks):
        gains = ref[(*at, slice(256, 272), slice(0, 384))].astype(F32)
        gain_ref[k : k + 1, :] = gains[0:1] + gains[1:2] + gains[2:3]
    width = 16 * 384

    def fold(values):
        return values[:, :128] + values[:, 128:256] + values[:, 256:]

    @pl.loop(0, 8)
    def _(t):
        rows = pl.ds(pl.multiple_of(t * 32, 32), 32)

        def read(ref, at):
            return ref[(*at, rows, slice(0, 384))].astype(F32)

        total = jnp.zeros((32, 128), F32)
        for ref, at, dz, x in blocks:
            total += fold(read(ref, at))
        mean = jnp.sum(total, axis=1, keepdims=True) / width
        total = jnp.zeros((32, 128), F32)
        for ref, at, dz, x in blocks:
            d = read(ref, at) - mean
            total += fold(d * d)
        rstd = lax.rsqrt(jnp.sum(total, axis=1, keepdims=True) / width + EPSILON)
        for k, (ref, at, dz, x) in enumerate(blocks):
            zl = my_zl ^ dz
            spot = ((zl & 1) * 4 + x) * 2 + ((zl >> 1) ^ my_zh)
            n_ref[rows, pl.ds(pl.multiple_of(spot * 384, 128), 384)] = (
                (read(ref, at) - mean) * rstd * gain_ref[k : k + 1, :]
            ).astype(BF16)


def attention_kernel(place, n_ref, w_ref, qg_ref, f_ref):
    gain = jnp.where(place[0] == 0, qg_ref[0:1, :], qg_ref[1:2, :])
    projected = jnp.dot(n_ref[...], w_ref[...], preferred_element_type=F32)
    query = (normalize(projected[:, :128]) * gain).astype(BF16)
    key = (normalize(projected[:, 128:256]) * gain).astype(BF16)
    value = projected[:, 256:].astype(BF16)
    scores = lax.dot_general(
        query, key, (((1,), (1,)), ((), ())), preferred_element_type=F32
    ) * (HEAD ** (-0.5))
    scores = jnp.exp(scores - jnp.max(scores, axis=1, keepdims=True))
    attn = (scores / jnp.sum(scores, axis=1, keepdims=True)).astype(BF16)
    f_ref[...] = jnp.dot(attn, value, preferred_element_type=F32)


def reduce_dp(terms):
    k = terms.shape[0]
    terms = terms.reshape(k, 16, 2, 32, 256)
    terms = lax.all_to_all(terms, "c", split_axis=2, concat_axis=0)
    terms = sum_parts(terms).astype(BF16)
    terms = lax.all_to_all(terms, ("zh", "y"), split_axis=1, concat_axis=0)
    return sum_parts(terms).astype(BF16)


def shards(
    teacher_in,
    teacher_gain,
    qkv_weight,
    qk_gain,
    student_in,
    student_gain,
    up_weight,
    down_weight,
    projector,
):
    tok_rows = teacher_in.shape[0]

    first = lax.axis_index("c") == 0
    weight = qkv_weight.reshape(192, 3, 2, 128).transpose(2, 0, 1, 3).reshape(2, 192, 384)
    near = jnp.where(first, weight, weight[::-1])
    far = flip(near, "zh")
    hi = lax.reduce_precision(teacher_gain, 8, 7)
    mid = lax.reduce_precision(teacher_gain - hi, 8, 7)
    low = teacher_gain - hi - mid
    gain_rows = jnp.stack([hi, mid, low] + [jnp.zeros_like(hi)] * 13).astype(BF16)
    shard = tie(jnp.concatenate([teacher_in, gain_rows], axis=0), near)
    own = spread(shard, "x")
    far_block = flip(shard, "zl", 2)

    student_normed = (normalize(student_in.astype(F32)) * student_gain).astype(BF16)
    pre_act = jnp.dot(student_normed, up_weight, preferred_element_type=F32)
    gated, slope = gelu_parts(pre_act)
    activ = gated.astype(BF16)
    mlp_term = jnp.dot(activ, down_weight, preferred_element_type=F32).astype(BF16)

    def by_core(mine, theirs):
        return jnp.where(first, jnp.stack([mine, theirs]), jnp.stack([theirs, mine]))

    given = flip(jnp.stack([near[1], far[1]]), "c")
    given, own, far_block, mlp_term = lax.optimization_barrier(
        (given, own, far_block, mlp_term)
    )
    rows = jnp.concatenate([by_core(near[0], given[0]), by_core(far[0], given[1])])
    weight = lax.all_gather(rows, "y").reshape(6144, 384)

    late = flip(jnp.stack([shard, far_block]), "zl", 1)
    far_block, part = spread_and_scatter_x(far_block, mlp_term)
    late = jnp.broadcast_to(late[None], (4,) + late.shape)
    late = swap(tie(late, far_block), "x")
    late, part = lax.optimization_barrier((late, mp_sum_zl(part)))

    place_z = jnp.stack([lax.axis_index("zl"), lax.axis_index("zh")])
    place_c = lax.axis_index("c").reshape(1)
    smem = pl.BlockSpec(memory_space=pltpu.SMEM)
    vmem = pl.BlockSpec(memory_space=pltpu.VMEM)
    params = pltpu.CompilerParams(vmem_limit_bytes=24 * 1024 * 1024)
    normed = pl.pallas_call(
        norm_kernel,
        out_shape=jax.ShapeDtypeStruct((256, 6144), BF16),
        scratch_shapes=[pltpu.VMEM((16, 384), F32)],
        in_specs=[smem] + [vmem] * 3,
        out_specs=vmem,
        compiler_params=params,
        cost_estimate=pl.CostEstimate(
            flops=1000, bytes_accessed=1000, transcendentals=0
        ),
        name="teacher_norm",
    )(place_z, own, far_block, late)
    normed_other = shift(normed, "c", 1)
    mlp_sum = mp_gather_x(tie(part, normed))
    heads = pl.pallas_call(
        attention_kernel,
        out_shape=jax.ShapeDtypeStruct((256, 128), F32),
        in_specs=[smem] + [vmem] * 3,
        out_specs=vmem,
        compiler_params=params,
        cost_estimate=pl.CostEstimate(
            flops=2 * 256 * 6144 * 384, bytes_accessed=8_000_000, transcendentals=65536
        ),
        name="teacher_heads",
    )
    kept = heads(place_c, normed, weight, qk_gain)
    crossed = shift(heads(place_c, tie(normed_other, kept), weight, qk_gain), "c", 1)
    features = jnp.where(
        place_c[0] == 0,
        jnp.concatenate([kept, crossed], axis=1),
        jnp.concatenate([crossed, kept], axis=1),
    )

    block_out = (student_in.astype(F32) + mlp_sum.astype(F32)).astype(BF16)
    predicted = jnp.dot(block_out, projector, preferred_element_type=F32)

    local_sum = jnp.sum(features, axis=1)
    local_dev = features - (local_sum / 256)[:, None]
    stats = jnp.stack([local_sum, jnp.sum(local_dev * local_dev, axis=1)])
    feat_mean, feat_var = merge_stats(stats, 256)
    target = (features - feat_mean[:, None]) * lax.rsqrt(feat_var + EPSILON)[:, None]

    loss_factor = 1.0 / math.sqrt(tok_rows * 32)
    grad_pred = ((predicted - target) * loss_factor).astype(BF16)
    block_term = jnp.einsum("tf,cf->tc", grad_pred, projector, preferred_element_type=F32)
    proj_term = jnp.einsum("tc,tf->cf", block_out, grad_pred, preferred_element_type=F32)
    grad_block = mp_gather_x(mp_sum_zl(mp_scatter_x(block_term.astype(BF16))))
    down_term = jnp.einsum("tc,tf->cf", grad_block, activ, preferred_element_type=F32)
    grad_act = jnp.einsum("tc,fc->tf", grad_block, down_weight, preferred_element_type=F32)
    grad_pre = (grad_act * slope).astype(BF16)
    up_term = jnp.einsum("tc,tf->cf", student_normed, grad_pre, preferred_element_type=F32)
    terms = jnp.stack([t.astype(BF16) for t in (up_term, down_term, proj_term)])
    grad_up, grad_down, grad_projector = reduce_dp(terms)
    return grad_up, grad_down.T, grad_projector


def solution(mesh):
    fine = Mesh(mesh.devices.reshape(tuple(SIZES.values())), tuple(SIZES))
    in_specs = (
        P(DP, MP),
        P(MP),
        P(DP, None, MP),
        P(MP, None),
        P(DP, None),
        P(),
        P(None, MP),
        P(MP, None),
        P(None, MP),
    )
    out_specs = (P(DP, MP), P(MP, DP), P(DP, MP))
    return jax.shard_map(shards, mesh=fine, in_specs=in_specs, out_specs=out_specs, check_vma=False)
```

```python
import math

import jax
import jax.numpy as jnp
from jax import lax
from jax.experimental import pallas as pl
from jax.experimental.pallas import tpu as pltpu
from jax.sharding import Mesh, PartitionSpec as P

HEAD = 128
PATCH = 256
EPSILON = 1e-06
F32 = jnp.float32
BF16 = jnp.bfloat16

SIZES = {"zh": 2, "y": 8, "c": 2, "zl": 4, "x": 4}
DP = ("zh", "y", "c")
MP = ("zl", "x")


def normalize(values):
    row_mean = jnp.mean(values, axis=-1, keepdims=True)
    centered = values - row_mean
    row_var = jnp.mean(centered * centered, axis=-1, keepdims=True)
    return centered * lax.rsqrt(row_var + EPSILON)


def gelu_parts(pre_act):
    cdf_part = 0.5 * (1.0 + lax.erf(pre_act * 0.7071067811865476))
    density = jnp.exp(-0.5 * pre_act * pre_act) * 0.3989422804014327
    return (pre_act * cdf_part, cdf_part + pre_act * density)


def shift(values, axis, step):
    size = SIZES[axis]
    return lax.ppermute(values, axis, [(i, (i + step) % size) for i in range(size)])


def flip(values, axes, bits=1):
    return lax.ppermute(values, axes, [(i, i ^ bits) for i in range(SIZES[axes])])


def tie(values, *others):
    return lax.optimization_barrier((values, *others))[0]


def swap(values, axis):
    return lax.all_to_all(values, axis, split_axis=0, concat_axis=0)


def spread(values, axis):
    return swap(jnp.broadcast_to(values[None], (SIZES[axis],) + values.shape), axis)


def sum_parts(parts):
    return jnp.sum(parts.astype(F32), axis=0)


def mp_scatter_x(term):
    rows, cols = term.shape
    return sum_parts(swap(term.reshape(4, rows // 4, cols), "x")).astype(BF16)


def spread_and_scatter_x(block, term):
    rows, cols = term.shape
    term = term.reshape(4, rows // 4, 4, cols // 4).transpose(0, 2, 1, 3)
    term = jnp.pad(term.reshape(4, rows, cols // 4), ((0, 0), (0, 16), (0, 0)))
    block = jnp.broadcast_to(block[None], (4,) + block.shape)
    block = swap(jnp.concatenate([block, term], axis=2), "x")
    part = sum_parts(block[:, :rows, 384:]).astype(BF16)
    part = part.reshape(4, rows // 4, cols // 4).transpose(1, 0, 2)
    return block, part.reshape(rows // 4, cols)


def mp_sum_zl(part):
    for bits in (1, 2):
        part = (part.astype(F32) + flip(part, "zl", bits).astype(F32)).astype(BF16)
    return part


def mp_gather_x(part):
    rows, cols = part.shape
    return spread(part, "x").reshape(4 * rows, cols)


def merge_stats(stats, count):
    parts = swap(jnp.broadcast_to(stats[None], (16,) + stats.shape), MP)
    total = jnp.sum(parts[:, 0], axis=0)
    mean = total / (count * 16)
    moved = parts[:, 0] / count - mean[None]
    spreads = jnp.sum(parts[:, 1], axis=0) + count * jnp.sum(moved * moved, axis=0)
    return mean, spreads / (count * 16)


def norm_kernel(place, own_ref, far_ref, late_ref, n_ref, gain_ref):
    my_zl, my_zh = place[0], place[1]
    blocks = []
    for x in range(4):
        blocks.append((own_ref, (x,), 0, x))
        blocks.append((far_ref, (x,), 2, x))
        blocks.append((late_ref, (x, 0), 1, x))
        blocks.append((late_ref, (x, 1), 3, x))
    for k, (ref, at, dz, x) in enumerate(blocks):
        gains = ref[(*at, slice(256, 272), slice(0, 384))].astype(F32)
        gain_ref[k : k + 1, :] = gains[0:1] + gains[1:2] + gains[2:3]
    width = 16 * 384

    def fold(values):
        return values[:, :128] + values[:, 128:256] + values[:, 256:]

    @pl.loop(0, 4)
    def _(t):
        rows = pl.ds(pl.multiple_of(t * 64, 64), 64)

        def read(ref, at):
            return ref[(*at, rows, slice(0, 384))].astype(F32)

        total = jnp.zeros((64, 128), F32)
        for ref, at, dz, x in blocks:
            total += fold(read(ref, at))
        mean = jnp.sum(total, axis=1, keepdims=True) / width
        total = jnp.zeros((64, 128), F32)
        for ref, at, dz, x in blocks:
            d = read(ref, at) - mean
            total += fold(d * d)
        rstd = lax.rsqrt(jnp.sum(total, axis=1, keepdims=True) / width + EPSILON)
        for k, (ref, at, dz, x) in enumerate(blocks):
            zl = my_zl ^ dz
            spot = ((zl & 1) * 4 + x) * 2 + ((zl >> 1) ^ my_zh)
            n_ref[rows, pl.ds(pl.multiple_of(spot * 384, 128), 384)] = (
                (read(ref, at) - mean) * rstd * gain_ref[k : k + 1, :]
            ).astype(BF16)


def attention_kernel(place, own_ref, other_ref, w_ref, qg_ref, f_ref):
    gain = jnp.where(place[0] == 0, qg_ref[0:1, :], qg_ref[1:2, :])
    both = jnp.dot(
        jnp.concatenate([own_ref[...], other_ref[...]], axis=0),
        w_ref[...],
        preferred_element_type=F32,
    )
    for image in range(2):
        projected = both[256 * image : 256 * image + 256]
        query = (normalize(projected[:, :128]) * gain).astype(BF16)
        key = (normalize(projected[:, 128:256]) * gain).astype(BF16)
        value = projected[:, 256:].astype(BF16)
        scores = lax.dot_general(
            query, key, (((1,), (1,)), ((), ())), preferred_element_type=F32
        ) * (HEAD ** (-0.5))
        scores = jnp.exp(scores - jnp.max(scores, axis=1, keepdims=True))
        attn = (scores / jnp.sum(scores, axis=1, keepdims=True)).astype(BF16)
        f_ref[image] = jnp.dot(attn, value, preferred_element_type=F32)


def reduce_dp(terms):
    k = terms.shape[0]
    terms = terms.reshape(k, 16, 2, 32, 256)
    terms = lax.all_to_all(terms, "c", split_axis=2, concat_axis=0)
    terms = sum_parts(terms).astype(BF16)
    terms = lax.all_to_all(terms, ("zh", "y"), split_axis=1, concat_axis=0)
    return sum_parts(terms).astype(BF16)


def shards(
    teacher_in,
    teacher_gain,
    qkv_weight,
    qk_gain,
    student_in,
    student_gain,
    up_weight,
    down_weight,
    projector,
):
    tok_rows = teacher_in.shape[0]

    first = lax.axis_index("c") == 0
    weight = qkv_weight.reshape(192, 3, 2, 128).transpose(2, 0, 1, 3).reshape(2, 192, 384)
    near = jnp.where(first, weight, weight[::-1])
    hi = lax.reduce_precision(teacher_gain, 8, 7)
    mid = lax.reduce_precision(teacher_gain - hi, 8, 7)
    low = teacher_gain - hi - mid
    gain_rows = jnp.stack([hi, mid, low] + [jnp.zeros_like(hi)] * 13).astype(BF16)
    shard = tie(jnp.concatenate([teacher_in, gain_rows], axis=0), near)
    own = jnp.broadcast_to(shard[None], (4,) + shard.shape)
    own, near = lax.optimization_barrier((own, near))
    own = swap(own, "x")
    far_block = flip(shard, "zl", 2)

    far = flip(near, "zh")
    student_normed = (normalize(student_in.astype(F32)) * student_gain).astype(BF16)
    pre_act = jnp.dot(student_normed, up_weight, preferred_element_type=F32)
    gated, slope = gelu_parts(pre_act)
    activ = gated.astype(BF16)
    mlp_term = jnp.dot(activ, down_weight, preferred_element_type=F32).astype(BF16)

    def by_core(mine, theirs):
        return jnp.where(first, jnp.stack([mine, theirs]), jnp.stack([theirs, mine]))

    given = flip(jnp.stack([near[1], far[1]]), "c")
    given, own, far_block, mlp_term = lax.optimization_barrier(
        (given, own, far_block, mlp_term)
    )
    rows = jnp.concatenate([by_core(near[0], given[0]), by_core(far[0], given[1])])
    weight = lax.all_gather(rows, "y").reshape(6144, 384)

    late = flip(jnp.stack([shard, far_block]), "zl", 1)
    far_block, part = spread_and_scatter_x(far_block, mlp_term)
    late = spread(tie(late, far_block), "x")
    late, part = lax.optimization_barrier((late, mp_sum_zl(part)))

    place_z = jnp.stack([lax.axis_index("zl"), lax.axis_index("zh")])
    place_c = lax.axis_index("c").reshape(1)
    smem = pl.BlockSpec(memory_space=pltpu.SMEM)
    vmem = pl.BlockSpec(memory_space=pltpu.VMEM)
    params = pltpu.CompilerParams(vmem_limit_bytes=40 * 1024 * 1024)
    normed = pl.pallas_call(
        norm_kernel,
        out_shape=jax.ShapeDtypeStruct((256, 6144), BF16),
        scratch_shapes=[pltpu.VMEM((16, 384), F32)],
        in_specs=[smem] + [vmem] * 3,
        out_specs=vmem,
        compiler_params=params,
        cost_estimate=pl.CostEstimate(
            flops=1000, bytes_accessed=1000, transcendentals=0
        ),
        name="teacher_norm",
    )(place_z, own, far_block, late)
    normed_other = shift(normed, "c", 1)
    mlp_sum = mp_gather_x(tie(part, normed))
    heads = pl.pallas_call(
        attention_kernel,
        out_shape=jax.ShapeDtypeStruct((2, 256, 128), F32),
        in_specs=[smem] + [vmem] * 4,
        out_specs=vmem,
        compiler_params=params,
        cost_estimate=pl.CostEstimate(
            flops=2 * 512 * 6144 * 384, bytes_accessed=11_000_000, transcendentals=131072
        ),
        name="teacher_heads",
    )(place_c, normed, normed_other, weight, qk_gain)
    crossed = shift(heads[1], "c", 1)
    features = jnp.where(
        place_c[0] == 0,
        jnp.concatenate([heads[0], crossed], axis=1),
        jnp.concatenate([crossed, heads[0]], axis=1),
    )

    block_out = (student_in.astype(F32) + mlp_sum.astype(F32)).astype(BF16)
    predicted = jnp.dot(block_out, projector, preferred_element_type=F32)

    local_sum = jnp.sum(features, axis=1)
    local_dev = features - (local_sum / 256)[:, None]
    stats = jnp.stack([local_sum, jnp.sum(local_dev * local_dev, axis=1)])
    feat_mean, feat_var = merge_stats(stats, 256)
    target = (features - feat_mean[:, None]) * lax.rsqrt(feat_var + EPSILON)[:, None]

    loss_factor = 1.0 / math.sqrt(tok_rows * 32)
    grad_pred = ((predicted - target) * loss_factor).astype(BF16)
    block_term = jnp.einsum("tf,cf->tc", grad_pred, projector, preferred_element_type=F32)
    proj_term = jnp.einsum("tc,tf->cf", block_out, grad_pred, preferred_element_type=F32)
    grad_block = mp_gather_x(mp_sum_zl(mp_scatter_x(block_term.astype(BF16))))
    down_term = jnp.einsum("tc,tf->cf", grad_block, activ, preferred_element_type=F32)
    grad_act = jnp.einsum("tc,fc->tf", grad_block, down_weight, preferred_element_type=F32)
    grad_pre = (grad_act * slope).astype(BF16)
    up_term = jnp.einsum("tc,tf->cf", student_normed, grad_pre, preferred_element_type=F32)
    terms = jnp.stack([t.astype(BF16) for t in (up_term, down_term, proj_term)])
    grad_up, grad_down, grad_projector = reduce_dp(terms)
    return grad_up, grad_down.T, grad_projector


def solution(mesh):
    fine = Mesh(mesh.devices.reshape(tuple(SIZES.values())), tuple(SIZES))
    in_specs = (
        P(DP, MP),
        P(MP),
        P(DP, None, MP),
        P(MP, None),
        P(DP, None),
        P(),
        P(None, MP),
        P(MP, None),
        P(None, MP),
    )
    out_specs = (P(DP, MP), P(MP, DP), P(DP, MP))
    return jax.shard_map(shards, mesh=fine, in_specs=in_specs, out_specs=out_specs, check_vma=False)
```

```python
import math

import jax
import jax.numpy as jnp
from jax import lax
from jax.experimental import pallas as pl
from jax.experimental.pallas import tpu as pltpu
from jax.sharding import Mesh, PartitionSpec as P

HEAD = 128
PATCH = 256
EPSILON = 1e-06
F32 = jnp.float32
BF16 = jnp.bfloat16

SIZES = {"zh": 2, "y": 8, "c": 2, "zl": 4, "x": 4}
DP = ("zh", "y", "c")
MP = ("zl", "x")


def normalize(values):
    row_mean = jnp.mean(values, axis=-1, keepdims=True)
    centered = values - row_mean
    row_var = jnp.mean(centered * centered, axis=-1, keepdims=True)
    return centered * lax.rsqrt(row_var + EPSILON)


def gelu_parts(pre_act):
    cdf_part = 0.5 * (1.0 + lax.erf(pre_act * 0.7071067811865476))
    density = jnp.exp(-0.5 * pre_act * pre_act) * 0.3989422804014327
    return (pre_act * cdf_part, cdf_part + pre_act * density)


def shift(values, axis, step):
    size = SIZES[axis]
    return lax.ppermute(values, axis, [(i, (i + step) % size) for i in range(size)])


def flip(values, axes, bits=1):
    return lax.ppermute(values, axes, [(i, i ^ bits) for i in range(SIZES[axes])])


def tie(values, *others):
    return lax.optimization_barrier((values, *others))[0]


def swap(values, axis):
    return lax.all_to_all(values, axis, split_axis=0, concat_axis=0)


def spread(values, axis):
    return swap(jnp.broadcast_to(values[None], (SIZES[axis],) + values.shape), axis)


def sum_parts(parts):
    return jnp.sum(parts.astype(F32), axis=0)


def mp_scatter_x(term):
    rows, cols = term.shape
    return sum_parts(swap(term.reshape(4, rows // 4, cols), "x")).astype(BF16)


def copies_kernel(in_ref, out_ref):
    for i in range(4):
        out_ref[i] = in_ref[...]


def four_copies(values):
    vmem = pl.BlockSpec(memory_space=pltpu.VMEM)
    return pl.pallas_call(
        copies_kernel,
        out_shape=jax.ShapeDtypeStruct((4,) + values.shape, values.dtype),
        in_specs=[vmem],
        out_specs=vmem,
        compiler_params=pltpu.CompilerParams(vmem_limit_bytes=16 * 1024 * 1024),
        cost_estimate=pl.CostEstimate(flops=0, bytes_accessed=3_000_000, transcendentals=0),
        name="four_copies",
    )(values)


def spread_and_scatter_x(block, term):
    rows, cols = term.shape
    term = term.reshape(4, rows // 4, 4, cols // 4).transpose(0, 2, 1, 3)
    term = jnp.pad(term.reshape(4, rows, cols // 4), ((0, 0), (0, 16), (0, 0)))
    block = jnp.broadcast_to(block[None], (4,) + block.shape)
    block = swap(jnp.concatenate([block, term], axis=2), "x")
    part = sum_parts(block[:, :rows, 384:]).astype(BF16)
    part = part.reshape(4, rows // 4, cols // 4).transpose(1, 0, 2)
    return block, part.reshape(rows // 4, cols)


def mp_sum_zl(part):
    for bits in (1, 2):
        part = (part.astype(F32) + flip(part, "zl", bits).astype(F32)).astype(BF16)
    return part


def mp_gather_x(part):
    rows, cols = part.shape
    return spread(part, "x").reshape(4 * rows, cols)


def merge_stats(stats, count):
    parts = swap(jnp.broadcast_to(stats[None], (16,) + stats.shape), MP)
    total = jnp.sum(parts[:, 0], axis=0)
    mean = total / (count * 16)
    moved = parts[:, 0] / count - mean[None]
    spreads = jnp.sum(parts[:, 1], axis=0) + count * jnp.sum(moved * moved, axis=0)
    return mean, spreads / (count * 16)


def norm_kernel(place, own_ref, far_ref, late_ref, n_ref, gain_ref):
    my_zl, my_zh = place[0], place[1]
    blocks = []
    for x in range(4):
        blocks.append((own_ref, (x,), 0, x))
        blocks.append((far_ref, (x,), 2, x))
        blocks.append((late_ref, (x, 0), 1, x))
        blocks.append((late_ref, (x, 1), 3, x))
    for k, (ref, at, dz, x) in enumerate(blocks):
        gains = ref[(*at, slice(256, 272), slice(0, 384))].astype(F32)
        gain_ref[k : k + 1, :] = gains[0:1] + gains[1:2] + gains[2:3]
    width = 16 * 384

    def fold(values):
        return values[:, :128] + values[:, 128:256] + values[:, 256:]

    @pl.loop(0, 4)
    def _(t):
        rows = pl.ds(pl.multiple_of(t * 64, 64), 64)

        def read(ref, at):
            return ref[(*at, rows, slice(0, 384))].astype(F32)

        total = jnp.zeros((64, 128), F32)
        for ref, at, dz, x in blocks:
            total += fold(read(ref, at))
        mean = jnp.sum(total, axis=1, keepdims=True) / width
        total = jnp.zeros((64, 128), F32)
        for ref, at, dz, x in blocks:
            d = read(ref, at) - mean
            total += fold(d * d)
        rstd = lax.rsqrt(jnp.sum(total, axis=1, keepdims=True) / width + EPSILON)
        for k, (ref, at, dz, x) in enumerate(blocks):
            zl = my_zl ^ dz
            spot = ((zl & 1) * 4 + x) * 2 + ((zl >> 1) ^ my_zh)
            n_ref[rows, pl.ds(pl.multiple_of(spot * 384, 128), 384)] = (
                (read(ref, at) - mean) * rstd * gain_ref[k : k + 1, :]
            ).astype(BF16)


def attention_kernel(place, own_ref, other_ref, w_ref, qg_ref, f_ref):
    gain = jnp.where(place[0] == 0, qg_ref[0:1, :], qg_ref[1:2, :])
    both = jnp.dot(
        jnp.concatenate([own_ref[...], other_ref[...]], axis=0),
        w_ref[...],
        preferred_element_type=F32,
    )
    for image in range(2):
        projected = both[256 * image : 256 * image + 256]
        query = (normalize(projected[:, :128]) * gain).astype(BF16)
        key = (normalize(projected[:, 128:256]) * gain).astype(BF16)
        value = projected[:, 256:].astype(BF16)
        scores = lax.dot_general(
            query, key, (((1,), (1,)), ((), ())), preferred_element_type=F32
        ) * (HEAD ** (-0.5))
        scores = jnp.exp(scores - jnp.max(scores, axis=1, keepdims=True))
        attn = (scores / jnp.sum(scores, axis=1, keepdims=True)).astype(BF16)
        f_ref[image] = jnp.dot(attn, value, preferred_element_type=F32)


def reduce_dp(terms):
    k = terms.shape[0]
    terms = terms.reshape(k, 16, 2, 32, 256)
    terms = lax.all_to_all(terms, "c", split_axis=2, concat_axis=0)
    terms = sum_parts(terms).astype(BF16)
    terms = lax.all_to_all(terms, ("zh", "y"), split_axis=1, concat_axis=0)
    return sum_parts(terms).astype(BF16)


def shards(
    teacher_in,
    teacher_gain,
    qkv_weight,
    qk_gain,
    student_in,
    student_gain,
    up_weight,
    down_weight,
    projector,
):
    tok_rows = teacher_in.shape[0]

    first = lax.axis_index("c") == 0
    weight = qkv_weight.reshape(192, 3, 2, 128).transpose(2, 0, 1, 3).reshape(2, 192, 384)
    near = jnp.where(first, weight, weight[::-1])
    far = flip(near, "zh")
    hi = lax.reduce_precision(teacher_gain, 8, 7)
    mid = lax.reduce_precision(teacher_gain - hi, 8, 7)
    low = teacher_gain - hi - mid
    gain_rows = jnp.stack([hi, mid, low] + [jnp.zeros_like(hi)] * 13).astype(BF16)
    shard = tie(jnp.concatenate([teacher_in, gain_rows], axis=0), near)
    own = spread(shard, "x")
    far_block = flip(shard, "zl", 2)

    student_normed = (normalize(student_in.astype(F32)) * student_gain).astype(BF16)
    pre_act = jnp.dot(student_normed, up_weight, preferred_element_type=F32)
    gated, slope = gelu_parts(pre_act)
    activ = gated.astype(BF16)
    mlp_term = jnp.dot(activ, down_weight, preferred_element_type=F32).astype(BF16)

    def by_core(mine, theirs):
        return jnp.where(first, jnp.stack([mine, theirs]), jnp.stack([theirs, mine]))

    given = flip(jnp.stack([near[1], far[1]]), "c")
    given, own, far_block, mlp_term = lax.optimization_barrier(
        (given, own, far_block, mlp_term)
    )
    rows = jnp.concatenate([by_core(near[0], given[0]), by_core(far[0], given[1])])
    weight = lax.all_gather(rows, "y").reshape(6144, 384)

    late = flip(jnp.stack([shard, far_block]), "zl", 1)
    far_block, part = spread_and_scatter_x(far_block, mlp_term)
    late = swap(tie(four_copies(late), far_block), "x")
    late, part = lax.optimization_barrier((late, mp_sum_zl(part)))

    place_z = jnp.stack([lax.axis_index("zl"), lax.axis_index("zh")])
    place_c = lax.axis_index("c").reshape(1)
    smem = pl.BlockSpec(memory_space=pltpu.SMEM)
    vmem = pl.BlockSpec(memory_space=pltpu.VMEM)
    params = pltpu.CompilerParams(vmem_limit_bytes=40 * 1024 * 1024)
    normed = pl.pallas_call(
        norm_kernel,
        out_shape=jax.ShapeDtypeStruct((256, 6144), BF16),
        scratch_shapes=[pltpu.VMEM((16, 384), F32)],
        in_specs=[smem] + [vmem] * 3,
        out_specs=vmem,
        compiler_params=params,
        cost_estimate=pl.CostEstimate(
            flops=1000, bytes_accessed=1000, transcendentals=0
        ),
        name="teacher_norm",
    )(place_z, own, far_block, late)
    normed_other = shift(normed, "c", 1)
    mlp_sum = mp_gather_x(tie(part, normed))
    heads = pl.pallas_call(
        attention_kernel,
        out_shape=jax.ShapeDtypeStruct((2, 256, 128), F32),
        in_specs=[smem] + [vmem] * 4,
        out_specs=vmem,
        compiler_params=params,
        cost_estimate=pl.CostEstimate(
            flops=2 * 512 * 6144 * 384, bytes_accessed=11_000_000, transcendentals=131072
        ),
        name="teacher_heads",
    )(place_c, normed, normed_other, weight, qk_gain)
    crossed = shift(heads[1], "c", 1)
    features = jnp.where(
        place_c[0] == 0,
        jnp.concatenate([heads[0], crossed], axis=1),
        jnp.concatenate([crossed, heads[0]], axis=1),
    )

    block_out = (student_in.astype(F32) + mlp_sum.astype(F32)).astype(BF16)
    predicted = jnp.dot(block_out, projector, preferred_element_type=F32)

    local_sum = jnp.sum(features, axis=1)
    local_dev = features - (local_sum / 256)[:, None]
    stats = jnp.stack([local_sum, jnp.sum(local_dev * local_dev, axis=1)])
    feat_mean, feat_var = merge_stats(stats, 256)
    target = (features - feat_mean[:, None]) * lax.rsqrt(feat_var + EPSILON)[:, None]

    loss_factor = 1.0 / math.sqrt(tok_rows * 32)
    grad_pred = ((predicted - target) * loss_factor).astype(BF16)
    block_term = jnp.einsum("tf,cf->tc", grad_pred, projector, preferred_element_type=F32)
    proj_term = jnp.einsum("tc,tf->cf", block_out, grad_pred, preferred_element_type=F32)
    grad_block = mp_gather_x(mp_sum_zl(mp_scatter_x(block_term.astype(BF16))))
    down_term = jnp.einsum("tc,tf->cf", grad_block, activ, preferred_element_type=F32)
    grad_act = jnp.einsum("tc,fc->tf", grad_block, down_weight, preferred_element_type=F32)
    grad_pre = (grad_act * slope).astype(BF16)
    up_term = jnp.einsum("tc,tf->cf", student_normed, grad_pre, preferred_element_type=F32)
    terms = jnp.stack([t.astype(BF16) for t in (up_term, down_term, proj_term)])
    grad_up, grad_down, grad_projector = reduce_dp(terms)
    return grad_up, grad_down.T, grad_projector


def solution(mesh):
    fine = Mesh(mesh.devices.reshape(tuple(SIZES.values())), tuple(SIZES))
    in_specs = (
        P(DP, MP),
        P(MP),
        P(DP, None, MP),
        P(MP, None),
        P(DP, None),
        P(),
        P(None, MP),
        P(MP, None),
        P(None, MP),
    )
    out_specs = (P(DP, MP), P(MP, DP), P(DP, MP))
    return jax.shard_map(shards, mesh=fine, in_specs=in_specs, out_specs=out_specs, check_vma=False)
```

```python
import math

import jax
import jax.numpy as jnp
from jax import lax
from jax.experimental import pallas as pl
from jax.experimental.pallas import tpu as pltpu
from jax.sharding import Mesh, PartitionSpec as P

HEAD = 128
PATCH = 256
EPSILON = 1e-06
F32 = jnp.float32
BF16 = jnp.bfloat16

SIZES = {"zh": 2, "y": 8, "c": 2, "zl": 4, "x": 4}
DP = ("zh", "y", "c")
MP = ("zl", "x")


def normalize(values):
    row_mean = jnp.mean(values, axis=-1, keepdims=True)
    centered = values - row_mean
    row_var = jnp.mean(centered * centered, axis=-1, keepdims=True)
    return centered * lax.rsqrt(row_var + EPSILON)


def gelu_parts(pre_act):
    cdf_part = 0.5 * (1.0 + lax.erf(pre_act * 0.7071067811865476))
    density = jnp.exp(-0.5 * pre_act * pre_act) * 0.3989422804014327
    return (pre_act * cdf_part, cdf_part + pre_act * density)


def shift(values, axis, step):
    size = SIZES[axis]
    return lax.ppermute(values, axis, [(i, (i + step) % size) for i in range(size)])


def flip(values, axes, bits=1):
    return lax.ppermute(values, axes, [(i, i ^ bits) for i in range(SIZES[axes])])


def tie(values, *others):
    return lax.optimization_barrier((values, *others))[0]


def swap(values, axis):
    return lax.all_to_all(values, axis, split_axis=0, concat_axis=0)


def spread(values, axis):
    return swap(jnp.broadcast_to(values[None], (SIZES[axis],) + values.shape), axis)


def sum_parts(parts):
    return jnp.sum(parts.astype(F32), axis=0)


def mp_scatter_x(term):
    rows, cols = term.shape
    return sum_parts(swap(term.reshape(4, rows // 4, cols), "x")).astype(BF16)


def copies_kernel(in_ref, out_ref):
    for i in range(4):
        out_ref[i] = in_ref[...]


def four_copies(values):
    vmem = pl.BlockSpec(memory_space=pltpu.VMEM)
    return pl.pallas_call(
        copies_kernel,
        out_shape=jax.ShapeDtypeStruct((4,) + values.shape, values.dtype),
        in_specs=[vmem],
        out_specs=vmem,
        compiler_params=pltpu.CompilerParams(vmem_limit_bytes=16 * 1024 * 1024),
        cost_estimate=pl.CostEstimate(flops=0, bytes_accessed=3_000_000, transcendentals=0),
        name="four_copies",
    )(values)


def spread_and_scatter_x(block, term):
    rows, cols = term.shape
    term = term.reshape(4, rows // 4, 4, cols // 4).transpose(0, 2, 1, 3)
    term = jnp.pad(term.reshape(4, rows, cols // 4), ((0, 0), (0, 16), (0, 0)))
    block = jnp.broadcast_to(block[None], (4,) + block.shape)
    block = swap(jnp.concatenate([block, term], axis=2), "x")
    part = sum_parts(block[:, :rows, 384:]).astype(BF16)
    part = part.reshape(4, rows // 4, cols // 4).transpose(1, 0, 2)
    return block, part.reshape(rows // 4, cols)


def mp_sum_zl(part):
    for bits in (1, 2):
        part = (part.astype(F32) + flip(part, "zl", bits).astype(F32)).astype(BF16)
    return part


def mp_gather_x(part):
    rows, cols = part.shape
    return swap(four_copies(part), "x").reshape(4 * rows, cols)


def merge_stats(stats, count):
    parts = swap(jnp.broadcast_to(stats[None], (16,) + stats.shape), MP)
    total = jnp.sum(parts[:, 0], axis=0)
    mean = total / (count * 16)
    moved = parts[:, 0] / count - mean[None]
    spreads = jnp.sum(parts[:, 1], axis=0) + count * jnp.sum(moved * moved, axis=0)
    return mean, spreads / (count * 16)


def norm_kernel(place, own_ref, far_ref, late_ref, n_ref, gain_ref):
    my_zl, my_zh = place[0], place[1]
    blocks = []
    for x in range(4):
        blocks.append((own_ref, (x,), 0, x))
        blocks.append((far_ref, (x,), 2, x))
        blocks.append((late_ref, (x, 0), 1, x))
        blocks.append((late_ref, (x, 1), 3, x))
    for k, (ref, at, dz, x) in enumerate(blocks):
        gains = ref[(*at, slice(256, 272), slice(0, 384))].astype(F32)
        gain_ref[k : k + 1, :] = gains[0:1] + gains[1:2] + gains[2:3]
    width = 16 * 384

    def fold(values):
        return values[:, :128] + values[:, 128:256] + values[:, 256:]

    @pl.loop(0, 4)
    def _(t):
        rows = pl.ds(pl.multiple_of(t * 64, 64), 64)

        def read(ref, at):
            return ref[(*at, rows, slice(0, 384))].astype(F32)

        total = jnp.zeros((64, 128), F32)
        for ref, at, dz, x in blocks:
            total += fold(read(ref, at))
        mean = jnp.sum(total, axis=1, keepdims=True) / width
        total = jnp.zeros((64, 128), F32)
        for ref, at, dz, x in blocks:
            d = read(ref, at) - mean
            total += fold(d * d)
        rstd = lax.rsqrt(jnp.sum(total, axis=1, keepdims=True) / width + EPSILON)
        for k, (ref, at, dz, x) in enumerate(blocks):
            zl = my_zl ^ dz
            spot = ((zl & 1) * 4 + x) * 2 + ((zl >> 1) ^ my_zh)
            n_ref[rows, pl.ds(pl.multiple_of(spot * 384, 128), 384)] = (
                (read(ref, at) - mean) * rstd * gain_ref[k : k + 1, :]
            ).astype(BF16)


def attention_kernel(place, own_ref, other_ref, w_ref, qg_ref, f_ref):
    gain = jnp.where(place[0] == 0, qg_ref[0:1, :], qg_ref[1:2, :])
    both = jnp.dot(
        jnp.concatenate([own_ref[...], other_ref[...]], axis=0),
        w_ref[...],
        preferred_element_type=F32,
    )
    for image in range(2):
        projected = both[256 * image : 256 * image + 256]
        query = (normalize(projected[:, :128]) * gain).astype(BF16)
        key = (normalize(projected[:, 128:256]) * gain).astype(BF16)
        value = projected[:, 256:].astype(BF16)
        scores = lax.dot_general(
            query, key, (((1,), (1,)), ((), ())), preferred_element_type=F32
        ) * (HEAD ** (-0.5))
        scores = jnp.exp(scores - jnp.max(scores, axis=1, keepdims=True))
        attn = (scores / jnp.sum(scores, axis=1, keepdims=True)).astype(BF16)
        f_ref[image] = jnp.dot(attn, value, preferred_element_type=F32)


def reduce_dp(terms):
    k = terms.shape[0]
    terms = terms.reshape(k, 16, 2, 32, 256)
    terms = lax.all_to_all(terms, "c", split_axis=2, concat_axis=0)
    terms = sum_parts(terms).astype(BF16)
    terms = lax.all_to_all(terms, ("zh", "y"), split_axis=1, concat_axis=0)
    return sum_parts(terms).astype(BF16)


def shards(
    teacher_in,
    teacher_gain,
    qkv_weight,
    qk_gain,
    student_in,
    student_gain,
    up_weight,
    down_weight,
    projector,
):
    tok_rows = teacher_in.shape[0]

    first = lax.axis_index("c") == 0
    weight = qkv_weight.reshape(192, 3, 2, 128).transpose(2, 0, 1, 3).reshape(2, 192, 384)
    near = jnp.where(first, weight, weight[::-1])
    far = flip(near, "zh")
    hi = lax.reduce_precision(teacher_gain, 8, 7)
    mid = lax.reduce_precision(teacher_gain - hi, 8, 7)
    low = teacher_gain - hi - mid
    gain_rows = jnp.stack([hi, mid, low] + [jnp.zeros_like(hi)] * 13).astype(BF16)
    shard = tie(jnp.concatenate([teacher_in, gain_rows], axis=0), near)
    own = spread(shard, "x")
    far_block = flip(shard, "zl", 2)

    student_normed = (normalize(student_in.astype(F32)) * student_gain).astype(BF16)
    pre_act = jnp.dot(student_normed, up_weight, preferred_element_type=F32)
    gated, slope = gelu_parts(pre_act)
    activ = gated.astype(BF16)
    mlp_term = jnp.dot(activ, down_weight, preferred_element_type=F32).astype(BF16)

    given = flip(jnp.stack([near[1], far[1]]), "c")
    given, own, far_block, mlp_term = lax.optimization_barrier(
        (given, own, far_block, mlp_term)
    )
    mine = jnp.stack([near[0], far[0]])
    from_first = (jnp.arange(2) == 0)[None, :, None, None]
    rows = jnp.where(from_first == first, mine[:, None], given[:, None]).reshape(4, 192, 384)
    weight = lax.all_gather(rows, "y").reshape(6144, 384)

    late = flip(jnp.stack([shard, far_block]), "zl", 1)
    far_block, part = spread_and_scatter_x(far_block, mlp_term)
    late = swap(tie(four_copies(late), far_block), "x")
    late, part = lax.optimization_barrier((late, mp_sum_zl(part)))

    place_z = jnp.stack([lax.axis_index("zl"), lax.axis_index("zh")])
    place_c = lax.axis_index("c").reshape(1)
    smem = pl.BlockSpec(memory_space=pltpu.SMEM)
    vmem = pl.BlockSpec(memory_space=pltpu.VMEM)
    params = pltpu.CompilerParams(vmem_limit_bytes=40 * 1024 * 1024)
    normed = pl.pallas_call(
        norm_kernel,
        out_shape=jax.ShapeDtypeStruct((256, 6144), BF16),
        scratch_shapes=[pltpu.VMEM((16, 384), F32)],
        in_specs=[smem] + [vmem] * 3,
        out_specs=vmem,
        compiler_params=params,
        cost_estimate=pl.CostEstimate(
            flops=1000, bytes_accessed=1000, transcendentals=0
        ),
        name="teacher_norm",
    )(place_z, own, far_block, late)
    normed_other = shift(normed, "c", 1)
    mlp_sum = mp_gather_x(tie(part, normed))
    heads = pl.pallas_call(
        attention_kernel,
        out_shape=jax.ShapeDtypeStruct((2, 256, 128), F32),
        in_specs=[smem] + [vmem] * 4,
        out_specs=vmem,
        compiler_params=params,
        cost_estimate=pl.CostEstimate(
            flops=2 * 512 * 6144 * 384, bytes_accessed=11_000_000, transcendentals=131072
        ),
        name="teacher_heads",
    )(place_c, normed, normed_other, weight, qk_gain)
    crossed = shift(heads[1], "c", 1)
    features = jnp.where(
        place_c[0] == 0,
        jnp.concatenate([heads[0], crossed], axis=1),
        jnp.concatenate([crossed, heads[0]], axis=1),
    )

    block_out = (student_in.astype(F32) + mlp_sum.astype(F32)).astype(BF16)
    predicted = jnp.dot(block_out, projector, preferred_element_type=F32)

    local_sum = jnp.sum(features, axis=1)
    local_dev = features - (local_sum / 256)[:, None]
    stats = jnp.stack([local_sum, jnp.sum(local_dev * local_dev, axis=1)])
    feat_mean, feat_var = merge_stats(stats, 256)
    target = (features - feat_mean[:, None]) * lax.rsqrt(feat_var + EPSILON)[:, None]

    loss_factor = 1.0 / math.sqrt(tok_rows * 32)
    grad_pred = ((predicted - target) * loss_factor).astype(BF16)
    block_term = jnp.einsum("tf,cf->tc", grad_pred, projector, preferred_element_type=F32)
    proj_term = jnp.einsum("tc,tf->cf", block_out, grad_pred, preferred_element_type=F32)
    grad_block = mp_gather_x(mp_sum_zl(mp_scatter_x(block_term.astype(BF16))))
    down_term = jnp.einsum("tc,tf->cf", grad_block, activ, preferred_element_type=F32)
    grad_act = jnp.einsum("tc,fc->tf", grad_block, down_weight, preferred_element_type=F32)
    grad_pre = (grad_act * slope).astype(BF16)
    up_term = jnp.einsum("tc,tf->cf", student_normed, grad_pre, preferred_element_type=F32)
    terms = jnp.stack([t.astype(BF16) for t in (up_term, down_term, proj_term)])
    grad_up, grad_down, grad_projector = reduce_dp(terms)
    return grad_up, grad_down.T, grad_projector


def solution(mesh):
    fine = Mesh(mesh.devices.reshape(tuple(SIZES.values())), tuple(SIZES))
    in_specs = (
        P(DP, MP),
        P(MP),
        P(DP, None, MP),
        P(MP, None),
        P(DP, None),
        P(),
        P(None, MP),
        P(MP, None),
        P(None, MP),
    )
    out_specs = (P(DP, MP), P(MP, DP), P(DP, MP))
    return jax.shard_map(shards, mesh=fine, in_specs=in_specs, out_specs=out_specs, check_vma=False)
```

```python
import math

import jax
import jax.numpy as jnp
from jax import lax
from jax.experimental import pallas as pl
from jax.experimental.pallas import tpu as pltpu
from jax.sharding import Mesh, PartitionSpec as P

HEAD = 128
PATCH = 256
EPSILON = 1e-06
F32 = jnp.float32
BF16 = jnp.bfloat16

SIZES = {"zh": 2, "y": 8, "c": 2, "zl": 4, "x": 4}
DP = ("zh", "y", "c")
MP = ("zl", "x")


def normalize(values):
    row_mean = jnp.mean(values, axis=-1, keepdims=True)
    centered = values - row_mean
    row_var = jnp.mean(centered * centered, axis=-1, keepdims=True)
    return centered * lax.rsqrt(row_var + EPSILON)


def gelu_parts(pre_act):
    cdf_part = 0.5 * (1.0 + lax.erf(pre_act * 0.7071067811865476))
    density = jnp.exp(-0.5 * pre_act * pre_act) * 0.3989422804014327
    return (pre_act * cdf_part, cdf_part + pre_act * density)


def shift(values, axis, step):
    size = SIZES[axis]
    return lax.ppermute(values, axis, [(i, (i + step) % size) for i in range(size)])


def flip(values, axes, bits=1):
    return lax.ppermute(values, axes, [(i, i ^ bits) for i in range(SIZES[axes])])


def tie(values, *others):
    return lax.optimization_barrier((values, *others))[0]


def swap(values, axis):
    return lax.all_to_all(values, axis, split_axis=0, concat_axis=0)


def spread(values, axis):
    return swap(jnp.broadcast_to(values[None], (SIZES[axis],) + values.shape), axis)


def sum_parts(parts):
    return jnp.sum(parts.astype(F32), axis=0)


def mp_scatter_x(term):
    rows, cols = term.shape
    return sum_parts(swap(term.reshape(4, rows // 4, cols), "x")).astype(BF16)


def copies_kernel(in_ref, out_ref):
    for i in range(4):
        out_ref[i] = in_ref[...]


def four_copies(values):
    vmem = pl.BlockSpec(memory_space=pltpu.VMEM)
    return pl.pallas_call(
        copies_kernel,
        out_shape=jax.ShapeDtypeStruct((4,) + values.shape, values.dtype),
        in_specs=[vmem],
        out_specs=vmem,
        compiler_params=pltpu.CompilerParams(vmem_limit_bytes=16 * 1024 * 1024),
        cost_estimate=pl.CostEstimate(flops=0, bytes_accessed=3_000_000, transcendentals=0),
        name="four_copies",
    )(values)


def spread_and_scatter_x(block, term):
    rows, cols = term.shape
    term = term.reshape(4, rows // 4, 4, cols // 4).transpose(0, 2, 1, 3)
    term = jnp.pad(term.reshape(4, rows, cols // 4), ((0, 0), (0, 16), (0, 0)))
    block = jnp.broadcast_to(block[None], (4,) + block.shape)
    block = swap(jnp.concatenate([block, term], axis=2), "x")
    part = sum_parts(block[:, :rows, 384:]).astype(BF16)
    part = part.reshape(4, rows // 4, cols // 4).transpose(1, 0, 2)
    return block, part.reshape(rows // 4, cols)


def mp_sum_zl(part):
    for bits in (1, 2):
        part = (part.astype(F32) + flip(part, "zl", bits).astype(F32)).astype(BF16)
    return part


def mp_gather_x(part):
    rows, cols = part.shape
    return spread(part, "x").reshape(4 * rows, cols)


def merge_stats(stats, count):
    parts = swap(jnp.broadcast_to(stats[None], (16,) + stats.shape), MP)
    total = jnp.sum(parts[:, 0], axis=0)
    mean = total / (count * 16)
    moved = parts[:, 0] / count - mean[None]
    spreads = jnp.sum(parts[:, 1], axis=0) + count * jnp.sum(moved * moved, axis=0)
    return mean, spreads / (count * 16)


def norm_kernel(place, own_ref, far_ref, late_ref, n_ref, gain_ref):
    my_zl, my_zh = place[0], place[1]
    blocks = []
    for x in range(4):
        blocks.append((own_ref, (x,), 0, x))
        blocks.append((far_ref, (x,), 2, x))
        blocks.append((late_ref, (x, 0), 1, x))
        blocks.append((late_ref, (x, 1), 3, x))
    for k, (ref, at, dz, x) in enumerate(blocks):
        gains = ref[(*at, slice(256, 272), slice(0, 384))].astype(F32)
        gain_ref[k : k + 1, :] = gains[0:1] + gains[1:2] + gains[2:3]
    width = 16 * 384

    def fold(values):
        return values[:, :128] + values[:, 128:256] + values[:, 256:]

    @pl.loop(0, 4)
    def _(t):
        rows = pl.ds(pl.multiple_of(t * 64, 64), 64)

        def read(ref, at):
            return ref[(*at, rows, slice(0, 384))].astype(F32)

        total = jnp.zeros((64, 128), F32)
        for ref, at, dz, x in blocks:
            total += fold(read(ref, at))
        mean = jnp.sum(total, axis=1, keepdims=True) / width
        total = jnp.zeros((64, 128), F32)
        for ref, at, dz, x in blocks:
            d = read(ref, at) - mean
            total += fold(d * d)
        rstd = lax.rsqrt(jnp.sum(total, axis=1, keepdims=True) / width + EPSILON)
        for k, (ref, at, dz, x) in enumerate(blocks):
            zl = my_zl ^ dz
            spot = ((zl & 1) * 4 + x) * 2 + ((zl >> 1) ^ my_zh)
            n_ref[rows, pl.ds(pl.multiple_of(spot * 384, 128), 384)] = (
                (read(ref, at) - mean) * rstd * gain_ref[k : k + 1, :]
            ).astype(BF16)


def attention_kernel(place, own_ref, other_ref, w_ref, qg_ref, f_ref):
    gain = jnp.where(place[0] == 0, qg_ref[0:1, :], qg_ref[1:2, :])
    both = jnp.dot(
        jnp.concatenate([own_ref[...], other_ref[...]], axis=0),
        w_ref[...],
        preferred_element_type=F32,
    )
    for image in range(2):
        projected = both[256 * image : 256 * image + 256]
        query = (normalize(projected[:, :128]) * gain).astype(BF16)
        key = (normalize(projected[:, 128:256]) * gain).astype(BF16)
        value = projected[:, 256:].astype(BF16)
        scores = lax.dot_general(
            query, key, (((1,), (1,)), ((), ())), preferred_element_type=F32
        ) * (HEAD ** (-0.5))
        scores = jnp.exp(scores - jnp.max(scores, axis=1, keepdims=True))
        attn = (scores / jnp.sum(scores, axis=1, keepdims=True)).astype(BF16)
        f_ref[image] = jnp.dot(attn, value, preferred_element_type=F32)


def reduce_dp(terms):
    k = terms.shape[0]
    terms = terms.reshape(k, 16, 2, 32, 256).transpose(1, 0, 2, 3, 4)
    first = lax.axis_index("c") == 0
    theirs = flip(jnp.where(first, terms[:, :, 1], terms[:, :, 0]), "c")
    mine = jnp.where(first, terms[:, :, 0], terms[:, :, 1])
    terms = (mine.astype(F32) + theirs.astype(F32)).astype(BF16)
    return sum_parts(swap(terms, ("zh", "y"))).astype(BF16)


def shards(
    teacher_in,
    teacher_gain,
    qkv_weight,
    qk_gain,
    student_in,
    student_gain,
    up_weight,
    down_weight,
    projector,
):
    tok_rows = teacher_in.shape[0]

    first = lax.axis_index("c") == 0
    weight = qkv_weight.reshape(192, 3, 2, 128).transpose(2, 0, 1, 3).reshape(2, 192, 384)
    near = jnp.where(first, weight, weight[::-1])
    far = flip(near, "zh")
    hi = lax.reduce_precision(teacher_gain, 8, 7)
    mid = lax.reduce_precision(teacher_gain - hi, 8, 7)
    low = teacher_gain - hi - mid
    gain_rows = jnp.stack([hi, mid, low] + [jnp.zeros_like(hi)] * 13).astype(BF16)
    shard = tie(jnp.concatenate([teacher_in, gain_rows], axis=0), near)
    own = spread(shard, "x")
    far_block = flip(shard, "zl", 2)

    student_normed = (normalize(student_in.astype(F32)) * student_gain).astype(BF16)
    pre_act = jnp.dot(student_normed, up_weight, preferred_element_type=F32)
    gated, slope = gelu_parts(pre_act)
    activ = gated.astype(BF16)
    mlp_term = jnp.dot(activ, down_weight, preferred_element_type=F32).astype(BF16)

    def by_core(mine, theirs):
        return jnp.where(first, jnp.stack([mine, theirs]), jnp.stack([theirs, mine]))

    given = flip(jnp.stack([near[1], far[1]]), "c")
    given, own, far_block, mlp_term = lax.optimization_barrier(
        (given, own, far_block, mlp_term)
    )
    rows = jnp.concatenate([by_core(near[0], given[0]), by_core(far[0], given[1])])
    weight = lax.all_gather(rows, "y").reshape(6144, 384)

    late = flip(jnp.stack([shard, far_block]), "zl", 1)
    far_block, part = spread_and_scatter_x(far_block, mlp_term)
    late = swap(tie(four_copies(late), far_block), "x")
    late, part = lax.optimization_barrier((late, mp_sum_zl(part)))

    place_z = jnp.stack([lax.axis_index("zl"), lax.axis_index("zh")])
    place_c = lax.axis_index("c").reshape(1)
    smem = pl.BlockSpec(memory_space=pltpu.SMEM)
    vmem = pl.BlockSpec(memory_space=pltpu.VMEM)
    params = pltpu.CompilerParams(vmem_limit_bytes=40 * 1024 * 1024)
    normed = pl.pallas_call(
        norm_kernel,
        out_shape=jax.ShapeDtypeStruct((256, 6144), BF16),
        scratch_shapes=[pltpu.VMEM((16, 384), F32)],
        in_specs=[smem] + [vmem] * 3,
        out_specs=vmem,
        compiler_params=params,
        cost_estimate=pl.CostEstimate(
            flops=1000, bytes_accessed=1000, transcendentals=0
        ),
        name="teacher_norm",
    )(place_z, own, far_block, late)
    normed_other = shift(normed, "c", 1)
    mlp_sum = mp_gather_x(tie(part, normed))
    heads = pl.pallas_call(
        attention_kernel,
        out_shape=jax.ShapeDtypeStruct((2, 256, 128), F32),
        in_specs=[smem] + [vmem] * 4,
        out_specs=vmem,
        compiler_params=params,
        cost_estimate=pl.CostEstimate(
            flops=2 * 512 * 6144 * 384, bytes_accessed=11_000_000, transcendentals=131072
        ),
        name="teacher_heads",
    )(place_c, normed, normed_other, weight, qk_gain)
    crossed = shift(heads[1], "c", 1)
    features = jnp.where(
        place_c[0] == 0,
        jnp.concatenate([heads[0], crossed], axis=1),
        jnp.concatenate([crossed, heads[0]], axis=1),
    )

    block_out = (student_in.astype(F32) + mlp_sum.astype(F32)).astype(BF16)
    predicted = jnp.dot(block_out, projector, preferred_element_type=F32)

    local_sum = jnp.sum(features, axis=1)
    local_dev = features - (local_sum / 256)[:, None]
    stats = jnp.stack([local_sum, jnp.sum(local_dev * local_dev, axis=1)])
    feat_mean, feat_var = merge_stats(stats, 256)
    target = (features - feat_mean[:, None]) * lax.rsqrt(feat_var + EPSILON)[:, None]

    loss_factor = 1.0 / math.sqrt(tok_rows * 32)
    grad_pred = ((predicted - target) * loss_factor).astype(BF16)
    block_term = jnp.einsum("tf,cf->tc", grad_pred, projector, preferred_element_type=F32)
    proj_term = jnp.einsum("tc,tf->cf", block_out, grad_pred, preferred_element_type=F32)
    grad_block = mp_gather_x(mp_sum_zl(mp_scatter_x(block_term.astype(BF16))))
    down_term = jnp.einsum("tc,tf->cf", grad_block, activ, preferred_element_type=F32)
    grad_act = jnp.einsum("tc,fc->tf", grad_block, down_weight, preferred_element_type=F32)
    grad_pre = (grad_act * slope).astype(BF16)
    up_term = jnp.einsum("tc,tf->cf", student_normed, grad_pre, preferred_element_type=F32)
    terms = jnp.stack([t.astype(BF16) for t in (up_term, down_term, proj_term)])
    grad_up, grad_down, grad_projector = reduce_dp(terms)
    return grad_up, grad_down.T, grad_projector


def solution(mesh):
    fine = Mesh(mesh.devices.reshape(tuple(SIZES.values())), tuple(SIZES))
    in_specs = (
        P(DP, MP),
        P(MP),
        P(DP, None, MP),
        P(MP, None),
        P(DP, None),
        P(),
        P(None, MP),
        P(MP, None),
        P(None, MP),
    )
    out_specs = (P(DP, MP), P(MP, DP), P(DP, MP))
    return jax.shard_map(shards, mesh=fine, in_specs=in_specs, out_specs=out_specs, check_vma=False)
```
